32 devices in a mesh: section: 4 (over y, x), depth: 8 (over z, core).
Axes of the slice: x: 2, y: 2, z: 4, core: 2. Of those that a mesh axis runs over, the one named last changes fastest.
Arguments:
- resident: bfloat16 [4, 2, 32, 16, 8, 256], P('section', None, 'depth'), may hold values from -6 to 6
- previous: bfloat16 [4, 2, 32, 16, 8, 256], P('section', None, 'depth'), may hold values from -6 to 6
- incoming: bfloat16 [3, 2, 32, 16, 8, 256], P(None, None, 'depth'), may hold values from -6 to 6
- first_weights: bfloat16 [4, 3, 3, 3, 256, 256], P('section'), may hold values from -0.078125 to 0.078125
- second_weights: bfloat16 [4, 3, 3, 3, 256, 256], P('section'), may hold values from -0.078125 to 0.078125
Outputs:
- emitted: bfloat16 [4, 2, 32, 16, 8, 256], P('section', None, 'depth')
The draws below stay inside these ranges and needn't reach their ends.
All inputs are finite; a program needn't handle non-finite values.
Results may differ from the reference program's by a relative error of at most 0.014.
Values may be sent and summed in bfloat16 or wider, within the bound.
No kernel may reach another device: no remote copies, remote signals or barrier semaphores. Data moves between devices by JAX's collectives and lax.ppermute only.
A program may use at most 64 MiB of HBM per device.

```python
import jax
import jax.numpy as jnp
from jax import lax

C = 256
H = 16
W = 8
TICKS = 4
SECTIONS = 4
NZ = 32


def level_of(stream_key, shape, shards, smallest, high):
    factor_of = 1.0
    for axis_at, blocks in shards:
        heights = jax.random.uniform(jax.random.fold_in(jax.random.fold_in(stream_key, 6), axis_at), (blocks,), jnp.float32, smallest / len(shards), high / len(shards))
        factor_of = factor_of * jnp.repeat(jnp.exp(heights), shape[axis_at] // blocks).reshape((-1,) + (1,) * (len(shape) - 1 - axis_at))
    return factor_of


def noise(rng, extent, deviation, most, cuts=(), dtype=jnp.bfloat16):
    factor_of = level_of(rng, extent, cuts, -0.22, 0.18) if cuts else 1.0
    values = jax.random.normal(rng, extent, jnp.float32) * deviation * factor_of
    return jnp.minimum(jnp.maximum(values, -most), most).astype(dtype)


def setup_inputs(seed: int = 0) -> dict:
    splits = jax.random.split(jax.random.key(seed), 6)
    resident = noise(splits[0], (SECTIONS, 2, NZ, H, W, C), 1.0, 6.0, ((0, 4), (2, 8)))
    previous = noise(splits[1], (SECTIONS, 2, NZ, H, W, C), 1.0, 6.0, ((0, 4), (2, 8)))
    incoming = noise(splits[2], (TICKS - 1, 2, NZ, H, W, C), 1.0, 6.0, ((2, 8),))
    first_weights = noise(splits[3], (SECTIONS, 3, 3, 3, C, C), (27 * C) ** -0.5, 0.078125, ((0, 4),))
    second_weights = noise(splits[4], (SECTIONS, 3, 3, 3, C, C), (27 * C) ** -0.5, 0.078125, ((0, 4),))
    return dict(resident=resident, previous=previous, incoming=incoming, first_weights=first_weights, second_weights=second_weights)


def normed(values):
    values = values.astype(jnp.float32)
    scaled = values * lax.rsqrt(lax.optimization_barrier(jnp.mean(values * values, axis=-1, keepdims=True)) + 1e-05)
    return jax.nn.silu(scaled).astype(jnp.bfloat16)

def convolve(padded, weight_cube, planes):
    rows = padded.shape[1] - 2
    columns = padded.shape[2] - 2
    chans = padded.shape[3]
    total = jnp.zeros((planes * rows * columns, weight_cube.shape[-1]), jnp.float32)
    for plane_off in range(3):
        for row_off in range(3):
            slab = jnp.concatenate([padded[plane_off:plane_off + planes, row_off:row_off + rows, col_off:col_off + columns] for col_off in range(3)], axis=-1)
            total = total + jnp.dot(slab.reshape(-1, 3 * chans), weight_cube[plane_off, row_off].reshape(3 * chans, -1), preferred_element_type=jnp.float32)
    return total.reshape(planes, rows, columns, -1)

def padded_all(values):
    return jnp.pad(values, ((1, 1), (1, 1), (1, 1), (0, 0)))

def section_step(streams, weight_one, weight_two):
    first = streams[0].astype(jnp.float32)
    second = streams[1].astype(jnp.float32)
    planes = streams.shape[1]
    first_out = (first + convolve(padded_all(normed(second)), weight_one, planes)).astype(jnp.bfloat16)
    second_out = (second + convolve(padded_all(normed(first_out)), weight_two, planes)).astype(jnp.bfloat16)
    return jnp.stack([first_out, second_out])

def reference(resident, previous, incoming, first_weights, second_weights):
    half = SECTIONS // 2
    held = resident
    source = previous
    result = resident
    for tick in range(TICKS):
        outputs = []
        for section_num in range(SECTIONS):
            streams = held[section_num]
            if section_num >= half:
                streams = (streams.astype(jnp.float32) + source[SECTIONS - 1 - section_num].astype(jnp.float32)).astype(jnp.bfloat16)
            outputs.append(section_step(streams, first_weights[section_num], second_weights[section_num]))
        result = jnp.stack(outputs)
        if tick < TICKS - 1:
            held = jnp.concatenate([incoming[tick][None], result[:-1]], axis=0)
            source = result
    return result
```

```python
import functools

import jax
import jax.numpy as jnp
from jax import lax
from jax.experimental import pallas as pl
from jax.experimental.pallas import tpu as pltpu
from jax.sharding import PartitionSpec as P

EPS = 1e-05
VMEM_LIMIT = 48 * 1024 * 1024


def act(values):
    values = values.astype(jnp.float32)
    scaled = values * lax.rsqrt(jnp.mean(values * values, axis=-1, keepdims=True) + EPS)
    return scaled / (1.0 + jnp.exp(-scaled))


def fill(even, odd, at, values, width):
    planes, voxels, chans = values.shape
    rows = voxels // width
    field = act(values).reshape(planes * rows, width, chans)
    column = lax.broadcasted_iota(jnp.int32, field.shape, 1)
    shifted = (
        jnp.where(column == 0, 0.0, pltpu.roll(field, 1, 1)),
        field,
        jnp.where(column == width - 1, 0.0, pltpu.roll(field, width - 1, 1)),
    )
    edge = jnp.zeros((planes, width, chans), jnp.float32)
    for k, part in enumerate(shifted):
        part = part.reshape(planes, voxels, chans)
        columns = pl.ds(k * chans, chans)
        even[pl.ds(at, planes), :, columns] = part.astype(jnp.bfloat16)
        odd[pl.ds(at, planes), :, columns] = jnp.concatenate([edge, part, edge], axis=1).astype(jnp.bfloat16)


def convolve(even, odd, weights, copies, planes, width):
    voxels = even.shape[1]
    total = None
    for i in range(3):
        copies[i].wait()
        taps = [odd[i : i + planes, 0:voxels], even[i : i + planes], odd[i : i + planes, 2 * width : 2 * width + voxels]]
        slab = jnp.concatenate(taps, axis=-1)
        part = jnp.dot(
            slab.reshape(planes * voxels, slab.shape[-1]), weights[i], preferred_element_type=jnp.float32
        )
        total = part if total is None else total + part
    return total.reshape(planes, voxels, -1)


def fetch(weights_hbm, weights, sems):
    copies = [pltpu.make_async_copy(weights_hbm.at[i], weights.at[i], sems.at[i]) for i in range(3)]
    for copy in copies:
        copy.start()
    return copies


def first_kernel(width, flags, q_low, q_mid, q_high, p_low, p_mid, p_high, weights_hbm, low, mid, high, even, odd, weights, sems):
    copies = fetch(weights_hbm, weights, sems)
    planes = q_mid.shape[0]
    fill(even, odd, 0, q_low[...], width)
    fill(even, odd, 2, q_mid[...], width)
    fill(even, odd, 2 + planes, q_high[...], width)
    total = convolve(even, odd, weights, copies, planes + 2, width)
    low[...] = jnp.where(flags[0] > 0, p_low[...].astype(jnp.float32) + total[:1], 0.0).astype(low.dtype)
    mid[...] = (p_mid[...].astype(jnp.float32) + total[1:-1]).astype(mid.dtype)
    high[...] = jnp.where(flags[1] > 0, p_high[...].astype(jnp.float32) + total[-1:], 0.0).astype(high.dtype)


def second_kernel(width, first_low, first_mid, first_high, q_mid, weights_hbm, out, even, odd, weights, sems):
    copies = fetch(weights_hbm, weights, sems)
    planes = q_mid.shape[0]
    fill(even, odd, 0, first_low[...], width)
    fill(even, odd, 1, first_mid[...], width)
    fill(even, odd, 1 + planes, first_high[...], width)
    total = convolve(even, odd, weights, copies, planes, width)
    out[...] = (q_mid[...].astype(jnp.float32) + total).astype(out.dtype)


def scratch(planes, voxels, chans, width):
    return [
        pltpu.VMEM((planes, voxels, 3 * chans), jnp.bfloat16),
        pltpu.VMEM((planes, voxels + 2 * width, 3 * chans), jnp.bfloat16),
        pltpu.VMEM((3, 9 * chans, chans), jnp.bfloat16),
        pltpu.SemaphoreType.DMA((3,)),
    ]


VMEM = pl.BlockSpec(memory_space=pltpu.VMEM)
SMEM = pl.BlockSpec(memory_space=pltpu.SMEM)
ANY = pl.BlockSpec(memory_space=pl.ANY)


def first_half(flags, q, q_halo, p, p_halo, weights, width):
    planes, voxels, chans = q.shape
    shape = lambda n: jax.ShapeDtypeStruct((n, voxels, chans), jnp.bfloat16)
    return pl.pallas_call(
        functools.partial(first_kernel, width),
        out_shape=(shape(1), shape(planes), shape(1)),
        in_specs=[SMEM] + [VMEM] * 6 + [ANY],
        out_specs=(VMEM, VMEM, VMEM),
        scratch_shapes=scratch(planes + 4, voxels, chans, width),
        compiler_params=pltpu.CompilerParams(vmem_limit_bytes=VMEM_LIMIT),
        cost_estimate=pl.CostEstimate(
            flops=(planes + 2) * voxels * 54 * chans * chans, bytes_accessed=8 * weights.size // 3, transcendentals=0
        ),
    )(flags, q_halo[0], q, q_halo[1], p_halo[0], p, p_halo[1], weights)


def second_half(first, q, weights, width):
    planes, voxels, chans = q.shape
    return pl.pallas_call(
        functools.partial(second_kernel, width),
        out_shape=jax.ShapeDtypeStruct(q.shape, jnp.bfloat16),
        in_specs=[VMEM] * 4 + [ANY],
        out_specs=VMEM,
        scratch_shapes=scratch(planes + 2, voxels, chans, width),
        compiler_params=pltpu.CompilerParams(vmem_limit_bytes=VMEM_LIMIT),
        cost_estimate=pl.CostEstimate(
            flops=planes * voxels * 54 * chans * chans, bytes_accessed=8 * weights.size // 3, transcendentals=0
        ),
    )(*first, q, weights)


def halo(block, width):
    count = lax.axis_size("depth")
    upward = [(i, i + 1) for i in range(count - 1)]
    downward = [(i + 1, i) for i in range(count - 1)]
    low = lax.ppermute(block[-width:], "depth", upward)
    high = lax.ppermute(block[:width], "depth", downward)
    return low, high


def local(resident, previous, incoming, first_weights, second_weights):
    section = lax.axis_index("section")
    sections = lax.axis_size("section")
    half = sections // 2
    depth = lax.axis_index("depth")
    ticks = incoming.shape[0] + 1
    _, _, planes, rows, width, chans = resident.shape
    voxels = rows * width
    flat = lambda a: a.reshape(a.shape[0], 2, planes, voxels, chans)
    resident, previous, incoming = flat(resident)[0], flat(previous)[0], flat(incoming)
    w_one = first_weights.reshape(3, 9 * chans, chans)
    w_two = second_weights.reshape(3, 9 * chans, chans)
    flags = jnp.stack([depth > 0, depth < lax.axis_size("depth") - 1]).astype(jnp.int32)

    def send(block, pairs):
        return lax.ppermute(block, "section", pairs) if pairs else block

    mirrored = send(previous, [(j, sections - 1 - j) for j in range(half)])
    across = [(j, sections - 1 - j) for j in range(1, half - 1)]
    decoder = section >= half

    def join(held, skip):
        total = (held.astype(jnp.float32) + skip.astype(jnp.float32)).astype(jnp.bfloat16)
        return jnp.where(decoder, total, held)

    out = emitted = None
    newer, older, relayed, direct = {}, {}, {}, {}
    for slot in range(ticks + 1):
        inputs = []
        for stream in range(2):
            fresh = resident[stream] if slot == 0 else incoming[min(slot, ticks - 1) - 1, stream]
            if slot == 0:
                value = fresh
            elif slot == 1:
                value = jnp.where(section == 0, fresh, join(resident[stream], mirrored[stream]))
            else:
                held = jnp.where(section == 1, older[stream], newer[stream])
                skip = jnp.where(section == sections - 1, relayed[stream], newer[stream])
                if across:
                    skip = jnp.where((section > half) & (section < sections - 1), direct[stream], skip)
                value = jnp.where(section == 0, fresh, join(held, skip))
            inputs.append(value)
        p, q = inputs
        onward = []
        if slot < ticks:
            onward = [(0, 1)] if slot < ticks - 1 else []
            if slot > 0:
                onward += [(j, j + 1) for j in range(1, sections - 1)]
        received = {}
        relays = {}
        first = first_half(flags, q, halo(q, 2), p, halo(p, 1), w_one, width)
        if onward:
            received[0] = send(first[1], onward)
        second = second_half(first, q, w_two, width)
        if onward:
            received[1] = send(second, onward)
        if 0 < slot < ticks:
            relays = {k: send(newer[k], [(1, sections - 1)]) for k in range(2)}
        if across and 0 < slot < ticks:
            direct = {0: send(first[1], across), 1: send(second, across)}
        older, newer, relayed = newer, received, relays
        out = jnp.stack([first[1], second])
        if slot == ticks - 1:
            emitted = out
    result = jnp.where(section == 0, emitted, out)
    return result.reshape(1, 2, planes, rows, width, chans)


def solution(mesh):
    in_specs = (
        P("section", None, "depth", None, None, None),
        P("section", None, "depth", None, None, None),
        P(None, None, "depth", None, None, None),
        P("section", None, None, None, None, None),
        P("section", None, None, None, None, None),
    )
    out_specs = P("section", None, "depth", None, None, None)
    return jax.shard_map(local, mesh=mesh, in_specs=in_specs, out_specs=out_specs, check_vma=False)
```

```python
import functools

import jax
import jax.numpy as jnp
from jax import lax
from jax.experimental import pallas as pl
from jax.experimental.pallas import tpu as pltpu
from jax.sharding import PartitionSpec as P

EPS = 1e-05
VMEM_LIMIT = 48 * 1024 * 1024


def act(values):
    values = values.astype(jnp.float32)
    scaled = values * lax.rsqrt(jnp.mean(values * values, axis=-1, keepdims=True) + EPS)
    return scaled * (0.5 + 0.5 * jnp.tanh(0.5 * scaled))


def fill(even, odd, at, values, width):
    planes, voxels, chans = values.shape
    rows = voxels // width
    field = act(values).reshape(planes * rows, width, chans)
    column = lax.broadcasted_iota(jnp.int32, field.shape, 1)
    shifted = (
        jnp.where(column == 0, 0.0, pltpu.roll(field, 1, 1)),
        field,
        jnp.where(column == width - 1, 0.0, pltpu.roll(field, width - 1, 1)),
    )
    edge = jnp.zeros((planes, width, chans), jnp.float32)
    for k, part in enumerate(shifted):
        part = part.reshape(planes, voxels, chans)
        columns = pl.ds(k * chans, chans)
        even[pl.ds(at, planes), :, columns] = part.astype(jnp.bfloat16)
        odd[pl.ds(at, planes), :, columns] = jnp.concatenate([edge, part, edge], axis=1).astype(jnp.bfloat16)


def convolve(even, odd, weights, copies, planes, width):
    voxels = even.shape[1]
    taps = []
    for i in range(3):
        copies[i].wait()
        for part in (odd[i : i + planes, 0:voxels], even[i : i + planes], odd[i : i + planes, 2 * width : 2 * width + voxels]):
            taps.append(part.reshape(planes * voxels, part.shape[-1]))
    slab = jnp.concatenate(taps, axis=-1)
    total = jnp.dot(slab, weights[...], preferred_element_type=jnp.float32)
    return total.reshape(planes, voxels, -1)


def fetch(weights_hbm, weights, sems):
    depth = weights.shape[0] // 3
    copies = [
        pltpu.make_async_copy(weights_hbm.at[pl.ds(i * depth, depth)], weights.at[pl.ds(i * depth, depth)], sems.at[i])
        for i in range(3)
    ]
    for copy in copies:
        copy.start()
    return copies


def first_kernel(width, flags, q_mid, q_inner, q_outer, p_mid, p_inner, p_outer, weights_hbm, low, mid, high, even, odd, weights, sems):
    copies = fetch(weights_hbm, weights, sems)
    planes = q_mid.shape[0]
    above = flags[2] > 0
    fill(even, odd, 2, q_mid[...], width)
    inner, outer = q_inner[...].astype(jnp.float32), q_outer[...].astype(jnp.float32)
    fill(even, odd, 0, jnp.where(above, outer, inner), width)
    fill(even, odd, 2 + planes, jnp.where(above, inner, outer), width)
    total = convolve(even, odd, weights, copies, planes + 2, width)
    inner, outer = p_inner[...].astype(jnp.float32), p_outer[...].astype(jnp.float32)
    low[...] = jnp.where(flags[0] > 0, jnp.where(above, outer, inner) + total[:1], 0.0).astype(low.dtype)
    mid[...] = (p_mid[...].astype(jnp.float32) + total[1:-1]).astype(mid.dtype)
    high[...] = jnp.where(flags[1] > 0, jnp.where(above, inner, outer) + total[-1:], 0.0).astype(high.dtype)


def second_kernel(width, first_low, first_mid, first_high, q_mid, weights_hbm, out, even, odd, weights, sems):
    copies = fetch(weights_hbm, weights, sems)
    planes = q_mid.shape[0]
    fill(even, odd, 0, first_low[...], width)
    fill(even, odd, 1, first_mid[...], width)
    fill(even, odd, 1 + planes, first_high[...], width)
    total = convolve(even, odd, weights, copies, planes, width)
    out[...] = (q_mid[...].astype(jnp.float32) + total).astype(out.dtype)


def scratch(planes, voxels, chans, width):
    return [
        pltpu.VMEM((planes, voxels, 3 * chans), jnp.bfloat16),
        pltpu.VMEM((planes, voxels + 2 * width, 3 * chans), jnp.bfloat16),
        pltpu.VMEM((27 * chans, chans), jnp.bfloat16),
        pltpu.SemaphoreType.DMA((3,)),
    ]


VMEM = pl.BlockSpec(memory_space=pltpu.VMEM)
SMEM = pl.BlockSpec(memory_space=pltpu.SMEM)
ANY = pl.BlockSpec(memory_space=pl.ANY)


def first_half(flags, q, q_halo, p, p_halo, weights, width):
    planes, voxels, chans = q.shape
    shape = lambda n: jax.ShapeDtypeStruct((n, voxels, chans), jnp.bfloat16)
    return pl.pallas_call(
        functools.partial(first_kernel, width),
        out_shape=(shape(1), shape(planes), shape(1)),
        in_specs=[SMEM] + [VMEM] * 6 + [ANY],
        out_specs=(VMEM, VMEM, VMEM),
        scratch_shapes=scratch(planes + 4, voxels, chans, width),
        compiler_params=pltpu.CompilerParams(vmem_limit_bytes=VMEM_LIMIT),
        cost_estimate=pl.CostEstimate(
            flops=1, bytes_accessed=1, transcendentals=0
        ),
    )(flags, q, *q_halo, p, *p_halo, weights)


def second_half(first, q, weights, width):
    planes, voxels, chans = q.shape
    return pl.pallas_call(
        functools.partial(second_kernel, width),
        out_shape=jax.ShapeDtypeStruct(q.shape, jnp.bfloat16),
        in_specs=[VMEM] * 4 + [ANY],
        out_specs=VMEM,
        scratch_shapes=scratch(planes + 2, voxels, chans, width),
        compiler_params=pltpu.CompilerParams(vmem_limit_bytes=VMEM_LIMIT),
        cost_estimate=pl.CostEstimate(
            flops=1, bytes_accessed=1, transcendentals=0
        ),
    )(*first, q, weights)


def halo(block, width, above):
    count = lax.axis_size("depth")
    planes = block.shape[0]
    top, bottom = planes - width, 0

    def swap(start, base):
        part = lax.dynamic_slice_in_dim(block, start, width, axis=0)
        pairs = [pair for i in range(base, count - 1, 2) for pair in ((i, i + 1), (i + 1, i))]
        return lax.ppermute(part, "depth", pairs)

    return swap(jnp.where(above, top, bottom), 0), swap(jnp.where(above, bottom, top), 1)


def local(resident, previous, incoming, first_weights, second_weights):
    section = lax.axis_index("section")
    sections = lax.axis_size("section")
    half = sections // 2
    depth = lax.axis_index("depth")
    ticks = incoming.shape[0] + 1
    _, _, planes, rows, width, chans = resident.shape
    voxels = rows * width
    flat = lambda a: a.reshape(a.shape[0], 2, planes, voxels, chans)
    resident, previous, incoming = flat(resident)[0], flat(previous)[0], flat(incoming)
    w_one = first_weights.reshape(27 * chans, chans)
    w_two = second_weights.reshape(27 * chans, chans)
    above = depth % 2 == 0
    flags = jnp.stack([depth > 0, depth < lax.axis_size("depth") - 1, above]).astype(jnp.int32)

    def send(block, pairs):
        return lax.ppermute(block, "section", pairs) if pairs else block

    mirrored = send(previous, [(j, sections - 1 - j) for j in range(half)])
    across = [(j, sections - 1 - j) for j in range(1, half - 1)]
    decoder = section >= half

    def join(held, skip):
        total = (held.astype(jnp.float32) + skip.astype(jnp.float32)).astype(jnp.bfloat16)
        return jnp.where(decoder, total, held)

    out = emitted = None
    newer, older, relayed, direct = {}, {}, {}, {}
    for slot in range(ticks + 1):
        inputs = []
        for stream in range(2):
            fresh = resident[stream] if slot == 0 else incoming[min(slot, ticks - 1) - 1, stream]
            if slot == 0:
                value = fresh
            elif slot == 1:
                value = jnp.where(section == 0, fresh, join(resident[stream], mirrored[stream]))
            else:
                held = jnp.where(section == 1, older[stream], newer[stream])
                skip = jnp.where(section == sections - 1, relayed[stream], newer[stream])
                if across:
                    skip = jnp.where((section > half) & (section < sections - 1), direct[stream], skip)
                value = jnp.where(section == 0, fresh, join(held, skip))
            inputs.append(value)
        p, q = inputs
        p_halo = halo(p, 1, above)
        q_halo = halo(q, 2, above)
        onward = []
        if slot < ticks:
            onward = [(0, 1)] if slot < ticks - 1 else []
            if slot > 0:
                onward += [(j, j + 1) for j in range(1, sections - 1)]
        received = {}
        relays = {}
        first = first_half(flags, q, q_halo, p, p_halo, w_one, width)
        if onward:
            received[0] = send(first[1], onward)
        second = second_half(first, q, w_two, width)
        if onward:
            received[1] = send(second, onward)
        if 0 < slot < ticks:
            relays = {k: send(newer[k], [(1, sections - 1)]) for k in range(2)}
        if across and 0 < slot < ticks:
            direct = {0: send(first[1], across), 1: send(second, across)}
        older, newer, relayed = newer, received, relays
        out = jnp.stack([first[1], second])
        if slot == ticks - 1:
            emitted = out
    result = jnp.where(section == 0, emitted, out)
    return result.reshape(1, 2, planes, rows, width, chans)


def solution(mesh):
    in_specs = (
        P("section", None, "depth", None, None, None),
        P("section", None, "depth", None, None, None),
        P(None, None, "depth", None, None, None),
        P("section", None, None, None, None, None),
        P("section", None, None, None, None, None),
    )
    out_specs = P("section", None, "depth", None, None, None)
    return jax.shard_map(local, mesh=mesh, in_specs=in_specs, out_specs=out_specs, check_vma=False)
```

```python
import functools

import jax
import jax.numpy as jnp
from jax import lax
from jax.experimental import pallas as pl
from jax.experimental.pallas import tpu as pltpu
from jax.sharding import PartitionSpec as P

EPS = 1e-05
LANES = 128
VMEM_LIMIT = 48 * 1024 * 1024


def act(values):
    values = values.astype(jnp.float32)
    scaled = values * lax.rsqrt(jnp.mean(values * values, axis=-1, keepdims=True) + EPS)
    return scaled * (0.5 + 0.5 * jnp.tanh(0.5 * scaled))


def fill(even, odd, at, values, width):
    planes, voxels, chans = values.shape
    rows = voxels // width
    field = act(values).reshape(planes * rows, width, chans)
    column = lax.broadcasted_iota(jnp.int32, field.shape, 1)
    shifted = (
        jnp.where(column == 0, 0.0, pltpu.roll(field, 1, 1)),
        field,
        jnp.where(column == width - 1, 0.0, pltpu.roll(field, width - 1, 1)),
    )
    edge = jnp.zeros((planes, width, chans), jnp.float32)
    for k, part in enumerate(shifted):
        part = part.reshape(planes, voxels, chans)
        moved = jnp.concatenate([edge, part, edge], axis=1).astype(jnp.bfloat16)
        part = part.astype(jnp.bfloat16)
        for c in range(chans // LANES):
            piece = k * (chans // LANES) + c
            columns = slice(c * LANES, (c + 1) * LANES)
            even[piece, pl.ds(at, planes)] = part[:, :, columns]
            odd[piece, pl.ds(at, planes)] = moved[:, :, columns]


def convolve(even, odd, weights, copies, planes, width):
    pieces, _, voxels, _ = even.shape
    taps = []
    for i in range(3):
        copies[i].wait()
        for j in range(3):
            for piece in range(pieces):
                source, row = (even, 0) if j == 1 else (odd, j * width)
                part = source[piece, i : i + planes, row : row + voxels]
                taps.append(part.reshape(planes * voxels, LANES))
    slab = jnp.concatenate(taps, axis=-1)
    total = jnp.dot(slab, weights[...], preferred_element_type=jnp.float32)
    return total.reshape(planes, voxels, -1)


def fetch(weights_hbm, weights, sems):
    depth = weights.shape[0] // 3
    copies = [
        pltpu.make_async_copy(weights_hbm.at[pl.ds(i * depth, depth)], weights.at[pl.ds(i * depth, depth)], sems.at[i])
        for i in range(3)
    ]
    for copy in copies:
        copy.start()
    return copies


def first_kernel(width, flags, q_mid, q_inner, q_outer, p_mid, p_inner, p_outer, weights_hbm, low, mid, high, even, odd, weights, sems):
    copies = fetch(weights_hbm, weights, sems)
    planes = q_mid.shape[0]
    above = flags[2] > 0
    fill(even, odd, 2, q_mid[...], width)
    inner, outer = q_inner[:2].astype(jnp.float32), q_outer[:2].astype(jnp.float32)
    fill(even, odd, 0, jnp.where(above, outer, inner), width)
    fill(even, odd, 2 + planes, jnp.where(above, inner, outer), width)
    total = convolve(even, odd, weights, copies, planes + 2, width)
    inner, outer = p_inner[-1:].astype(jnp.float32), p_outer[-1:].astype(jnp.float32)
    low[...] = jnp.where(flags[0] > 0, jnp.where(above, outer, inner) + total[:1], 0.0).astype(low.dtype)
    mid[...] = (p_mid[...].astype(jnp.float32) + total[1:-1]).astype(mid.dtype)
    high[...] = jnp.where(flags[1] > 0, jnp.where(above, inner, outer) + total[-1:], 0.0).astype(high.dtype)


def second_kernel(width, first_low, first_mid, first_high, q_mid, weights_hbm, out, even, odd, weights, sems):
    copies = fetch(weights_hbm, weights, sems)
    planes = q_mid.shape[0]
    fill(even, odd, 0, first_low[...], width)
    fill(even, odd, 1, first_mid[...], width)
    fill(even, odd, 1 + planes, first_high[...], width)
    total = convolve(even, odd, weights, copies, planes, width)
    out[...] = (q_mid[...].astype(jnp.float32) + total).astype(out.dtype)


def scratch(planes, voxels, chans, width):
    return [
        pltpu.VMEM((3 * chans // LANES, planes, voxels, LANES), jnp.bfloat16),
        pltpu.VMEM((3 * chans // LANES, planes, voxels + 2 * width, LANES), jnp.bfloat16),
        pltpu.VMEM((27 * chans, chans), jnp.bfloat16),
        pltpu.SemaphoreType.DMA((3,)),
    ]


VMEM = pl.BlockSpec(memory_space=pltpu.VMEM)
SMEM = pl.BlockSpec(memory_space=pltpu.SMEM)
ANY = pl.BlockSpec(memory_space=pl.ANY)


def first_half(flags, q, q_halo, p, p_halo, weights, width):
    planes, voxels, chans = q.shape
    shape = lambda n: jax.ShapeDtypeStruct((n, voxels, chans), jnp.bfloat16)
    return pl.pallas_call(
        functools.partial(first_kernel, width),
        out_shape=(shape(1), shape(planes), shape(1)),
        in_specs=[SMEM] + [VMEM] * 6 + [ANY],
        out_specs=(VMEM, VMEM, VMEM),
        scratch_shapes=scratch(planes + 4, voxels, chans, width),
        compiler_params=pltpu.CompilerParams(vmem_limit_bytes=VMEM_LIMIT),
        cost_estimate=pl.CostEstimate(
            flops=1, bytes_accessed=1, transcendentals=0
        ),
    )(flags, q, *q_halo, p, *p_halo, weights)


def second_half(first, q, weights, width):
    planes, voxels, chans = q.shape
    return pl.pallas_call(
        functools.partial(second_kernel, width),
        out_shape=jax.ShapeDtypeStruct(q.shape, jnp.bfloat16),
        in_specs=[VMEM] * 4 + [ANY],
        out_specs=VMEM,
        scratch_shapes=scratch(planes + 2, voxels, chans, width),
        compiler_params=pltpu.CompilerParams(vmem_limit_bytes=VMEM_LIMIT),
        cost_estimate=pl.CostEstimate(
            flops=1, bytes_accessed=1, transcendentals=0
        ),
    )(*first, q, weights)


def halo(blocks, widths, above):
    count = lax.axis_size("depth")

    def swap(upward, base):
        parts = [
            lax.dynamic_slice_in_dim(block, jnp.where(upward, block.shape[0] - width, 0), width, axis=0)
            for block, width in zip(blocks, widths)
        ]
        pairs = [pair for i in range(base, count - 1, 2) for pair in ((i, i + 1), (i + 1, i))]
        return lax.ppermute(jnp.concatenate(parts, axis=0), "depth", pairs)

    return swap(above, 0), swap(jnp.logical_not(above), 1)


def local(resident, previous, incoming, first_weights, second_weights):
    section = lax.axis_index("section")
    sections = lax.axis_size("section")
    half = sections // 2
    depth = lax.axis_index("depth")
    ticks = incoming.shape[0] + 1
    _, _, planes, rows, width, chans = resident.shape
    voxels = rows * width
    flat = lambda a: a.reshape(a.shape[0], 2, planes, voxels, chans)
    resident, previous, incoming = flat(resident)[0], flat(previous)[0], flat(incoming)
    w_one = first_weights.reshape(27 * chans, chans)
    w_two = second_weights.reshape(27 * chans, chans)
    above = depth % 2 == 0
    flags = jnp.stack([depth > 0, depth < lax.axis_size("depth") - 1, above]).astype(jnp.int32)

    def send(block, pairs):
        return lax.ppermute(block, "section", pairs) if pairs else block

    mirrored = send(previous, [(j, sections - 1 - j) for j in range(half)])
    across = [(j, sections - 1 - j) for j in range(1, half - 1)]
    decoder = section >= half

    def join(held, skip):
        total = (held.astype(jnp.float32) + skip.astype(jnp.float32)).astype(jnp.bfloat16)
        return jnp.where(decoder, total, held)

    out = emitted = None
    newer, older, relayed, direct = {}, {}, {}, {}

    def arrived(slot, stream):
        fresh = incoming[min(slot, ticks - 1) - 1, stream]
        if slot == 1:
            return jnp.where(section == 0, fresh, join(resident[stream], mirrored[stream]))
        held = jnp.where(section == 1, older[stream], newer[stream])
        skip = jnp.where(section == sections - 1, relayed[stream], newer[stream])
        if across:
            skip = jnp.where((section > half) & (section < sections - 1), direct[stream], skip)
        return jnp.where(section == 0, fresh, join(held, skip))

    for slot in range(ticks + 1):
        if slot < 2:
            p, q = resident if slot == 0 else (arrived(slot, 0), arrived(slot, 1))
            p_halo = q_halo = halo((q, p), (2, 1), above)
        else:
            p = arrived(slot, 0)
            p_halo = halo((p,), (1,), above)
            p, p_halo, newer[1] = lax.optimization_barrier((p, p_halo, newer[1]))
            q = arrived(slot, 1)
            q_halo = halo((q,), (2,), above)
        onward = []
        if slot < ticks:
            onward = [(0, 1)] if slot < ticks - 1 else []
            if slot > 0:
                onward += [(j, j + 1) for j in range(1, sections - 1)]
        received, relays = {}, {}
        first = first_half(flags, q, q_halo, p, p_halo, w_one, width)
        if onward:
            received[0] = send(first[1], onward)
        second = second_half(first, q, w_two, width)
        if onward:
            received[1] = send(second, onward)
        if 0 < slot < ticks:
            held_q, second = lax.optimization_barrier((newer[1], second))
            relays = {k: send(held, [(1, sections - 1)]) for k, held in enumerate((newer[0], held_q))}
        if across and 0 < slot < ticks:
            direct = {0: send(first[1], across), 1: send(second, across)}
        older, newer, relayed = newer, received, relays
        out = jnp.stack([first[1], second])
        if slot == ticks - 1:
            emitted = out
    result = jnp.where(section == 0, emitted, out)
    return result.reshape(1, 2, planes, rows, width, chans)


def solution(mesh):
    in_specs = (
        P("section", None, "depth", None, None, None),
        P("section", None, "depth", None, None, None),
        P(None, None, "depth", None, None, None),
        P("section", None, None, None, None, None),
        P("section", None, None, None, None, None),
    )
    out_specs = P("section", None, "depth", None, None, None)
    return jax.shard_map(local, mesh=mesh, in_specs=in_specs, out_specs=out_specs, check_vma=False)
```

```python
import functools

import jax
import jax.numpy as jnp
from jax import lax
from jax.experimental import pallas as pl
from jax.experimental.pallas import tpu as pltpu
from jax.sharding import PartitionSpec as P

EPS = 1e-05
VMEM_LIMIT = 24 * 1024 * 1024


def act(values):
    values = values.astype(jnp.float32)
    scaled = values * lax.rsqrt(jnp.mean(values * values, axis=-1, keepdims=True) + EPS)
    return scaled * (0.5 + 0.5 * jnp.tanh(0.5 * scaled))


def fill(even, odd, at, values, width):
    planes, _, chans = values.shape
    field = act(values)
    edge = jnp.zeros((planes, width, chans), jnp.float32)
    even[pl.ds(at, planes)] = field.astype(jnp.bfloat16)
    odd[pl.ds(at, planes)] = jnp.concatenate([edge, field, edge], axis=1).astype(jnp.bfloat16)


def convolve(even, odd, weights, planes, width):
    _, voxels, chans = even.shape
    taps = []
    for i in range(3):
        for j in range(3):
            part = even[i : i + planes] if j == 1 else odd[i : i + planes, j * width : j * width + voxels]
            taps.append(part.reshape(planes * voxels, chans))
    slab = jnp.concatenate(taps, axis=-1)
    total = None
    for k in (1, 0, 2):
        columns = jnp.concatenate([weights[(3 * n + k) * chans : (3 * n + k + 1) * chans] for n in range(9)], axis=0)
        part = jnp.dot(slab, columns, preferred_element_type=jnp.float32).reshape(-1, width, chans)
        column = lax.broadcasted_iota(jnp.int32, part.shape, 1)
        if k == 0:
            part = jnp.where(column == 0, 0.0, pltpu.roll(part, 1, 1))
        elif k == 2:
            part = jnp.where(column == width - 1, 0.0, pltpu.roll(part, width - 1, 1))
        total = part if total is None else total + part
    return total.reshape(planes, voxels, chans)


def first_kernel(width, flags, q_mid, q_inner, q_outer, p_mid, p_inner, p_outer, weights, low, mid, high, even, odd):
    planes = q_mid.shape[0]
    above = flags[2] > 0
    fill(even, odd, 2, q_mid[...], width)
    inner, outer = q_inner[:2].astype(jnp.float32), q_outer[:2].astype(jnp.float32)
    fill(even, odd, 0, jnp.where(above, outer, inner), width)
    fill(even, odd, 2 + planes, jnp.where(above, inner, outer), width)
    total = convolve(even, odd, weights, planes + 2, width)
    if p_inner.shape[0] == 2:
        inner, outer = p_inner[pl.ds(flags[2], 1)], p_outer[pl.ds(1 - flags[2], 1)]
    else:
        inner, outer = p_inner[2:], p_outer[2:]
    inner, outer = inner.astype(jnp.float32), outer.astype(jnp.float32)
    low[...] = jnp.where(flags[0] > 0, jnp.where(above, outer, inner) + total[:1], 0.0).astype(low.dtype)
    mid[...] = (p_mid[...].astype(jnp.float32) + total[1:-1]).astype(mid.dtype)
    high[...] = jnp.where(flags[1] > 0, jnp.where(above, inner, outer) + total[-1:], 0.0).astype(high.dtype)


def second_kernel(width, first_low, first_mid, first_high, q_mid, weights, out, even, odd):
    planes = q_mid.shape[0]
    fill(even, odd, 0, first_low[...], width)
    fill(even, odd, 1, first_mid[...], width)
    fill(even, odd, 1 + planes, first_high[...], width)
    total = convolve(even, odd, weights, planes, width)
    out[...] = (q_mid[...].astype(jnp.float32) + total).astype(out.dtype)


def scratch(planes, voxels, chans, width):
    return [
        pltpu.VMEM((planes, voxels, chans), jnp.bfloat16),
        pltpu.VMEM((planes, voxels + 2 * width, chans), jnp.bfloat16),
    ]


VMEM = pl.BlockSpec(memory_space=pltpu.VMEM)
SMEM = pl.BlockSpec(memory_space=pltpu.SMEM)


def first_half(flags, q, q_halo, p, p_halo, weights, width):
    planes, voxels, chans = q.shape
    shape = lambda n: jax.ShapeDtypeStruct((n, voxels, chans), jnp.bfloat16)
    return pl.pallas_call(
        functools.partial(first_kernel, width),
        out_shape=(shape(1), shape(planes), shape(1)),
        in_specs=[SMEM] + [VMEM] * 7,
        out_specs=(VMEM, VMEM, VMEM),
        scratch_shapes=scratch(planes + 4, voxels, chans, width),
        compiler_params=pltpu.CompilerParams(vmem_limit_bytes=VMEM_LIMIT),
        cost_estimate=pl.CostEstimate(
            flops=1, bytes_accessed=1, transcendentals=0
        ),
    )(flags, q, *q_halo, p, *p_halo, weights)


def second_half(first, q, weights, width):
    planes, voxels, chans = q.shape
    return pl.pallas_call(
        functools.partial(second_kernel, width),
        out_shape=jax.ShapeDtypeStruct(q.shape, jnp.bfloat16),
        in_specs=[VMEM] * 5,
        out_specs=VMEM,
        scratch_shapes=scratch(planes + 2, voxels, chans, width),
        compiler_params=pltpu.CompilerParams(vmem_limit_bytes=VMEM_LIMIT),
        cost_estimate=pl.CostEstimate(
            flops=1, bytes_accessed=1, transcendentals=0
        ),
    )(*first, q, weights)


def boundary(block, upward, width):
    return lax.dynamic_slice_in_dim(block, jnp.where(upward, block.shape[0] - width, 0), width, axis=0)


def swapped(blocks, widths, above):
    count = lax.axis_size("depth")

    def swap(upward, base):
        parts = [boundary(block, upward, width) for block, width in zip(blocks, widths)]
        pairs = [pair for i in range(base, count - 1, 2) for pair in ((i, i + 1), (i + 1, i))]
        return lax.ppermute(jnp.concatenate(parts, axis=0), "depth", pairs)

    return swap(above, 0), swap(jnp.logical_not(above), 1)


def gathered(block, above):
    count = lax.axis_size("depth")

    def gather(upward, base):
        groups = [[i, (i + 1) % count] for i in range(base, count, 2)]
        return lax.all_gather(boundary(block, upward, 1), "depth", axis_index_groups=groups, tiled=True)

    return gather(above, 0), gather(jnp.logical_not(above), 1)


def local(resident, previous, incoming, first_weights, second_weights):
    section = lax.axis_index("section")
    sections = lax.axis_size("section")
    half = sections // 2
    depth = lax.axis_index("depth")
    ticks = incoming.shape[0] + 1
    _, _, planes, rows, width, chans = resident.shape
    voxels = rows * width
    flat = lambda a: a.reshape(a.shape[0], 2, planes, voxels, chans)
    resident, previous, incoming = flat(resident)[0], flat(previous)[0], flat(incoming)
    w_one = first_weights.reshape(27 * chans, chans)
    w_two = second_weights.reshape(27 * chans, chans)
    above = depth % 2 == 0
    flags = jnp.stack([depth > 0, depth < lax.axis_size("depth") - 1, above]).astype(jnp.int32)

    def send(block, pairs):
        return lax.ppermute(block, "section", pairs) if pairs else block

    mirrored = send(previous, [(j, sections - 1 - j) for j in range(half)])
    across = [(j, sections - 1 - j) for j in range(1, half - 1)]
    decoder = section >= half

    def join(held, skip):
        total = (held.astype(jnp.float32) + skip.astype(jnp.float32)).astype(jnp.bfloat16)
        return jnp.where(decoder, total, held)

    out = emitted = None
    newer, older, relayed, direct = {}, {}, {}, {}

    def arrived(slot, stream, mirrored=None):
        fresh = incoming[min(slot, ticks - 1) - 1, stream]
        if slot == 1:
            return jnp.where(section == 0, fresh, join(resident[stream], mirrored[stream]))
        held = jnp.where(section == 1, older[stream], newer[stream])
        skip = jnp.where(section == sections - 1, relayed[stream], newer[stream])
        if across:
            skip = jnp.where((section > half) & (section < sections - 1), direct[stream], skip)
        return jnp.where(section == 0, fresh, join(held, skip))

    for slot in range(ticks + 1):
        if slot < 2:
            if slot == 1:
                mirrored, _ = lax.optimization_barrier((mirrored, first[1]))
            p, q = resident if slot == 0 else (arrived(slot, 0, mirrored), arrived(slot, 1, mirrored))
            p_halo = q_halo = swapped((q, p), (2, 1), above)
        else:
            p = arrived(slot, 0)
            p_halo = gathered(p, above)
            p, newer[1] = lax.optimization_barrier((p, newer[1]))
            q = arrived(slot, 1)
            q_halo = swapped((q,), (2,), above)
        onward = []
        if slot < ticks:
            onward = [(0, 1)] if slot < ticks - 1 else []
            if slot > 0:
                onward += [(j, j + 1) for j in range(1, sections - 1)]
        received, relays = {}, {}
        first = first_half(flags, q, q_halo, p, p_halo, w_one, width)
        if onward:
            received[0] = send(first[1], onward)
        second = second_half(first, q, w_two, width)
        if onward:
            received[1] = send(second, onward)
        if 0 < slot < ticks:
            held_q, second = lax.optimization_barrier((newer[1], second))
            relays = {k: send(held, [(1, sections - 1)]) for k, held in enumerate((newer[0], held_q))}
        if across and 0 < slot < ticks:
            direct = {0: send(first[1], across), 1: send(second, across)}
        older, newer, relayed = newer, received, relays
        out = jnp.stack([first[1], second])
        if slot == ticks - 1:
            emitted = out
    result = jnp.where(section == 0, emitted, out)
    return result.reshape(1, 2, planes, rows, width, chans)


def solution(mesh):
    in_specs = (
        P("section", None, "depth", None, None, None),
        P("section", None, "depth", None, None, None),
        P(None, None, "depth", None, None, None),
        P("section", None, None, None, None, None),
        P("section", None, None, None, None, None),
    )
    out_specs = P("section", None, "depth", None, None, None)
    return jax.shard_map(local, mesh=mesh, in_specs=in_specs, out_specs=out_specs, check_vma=False)
```

```python
import functools

import jax
import jax.numpy as jnp
from jax import lax
from jax.experimental import pallas as pl
from jax.experimental.pallas import tpu as pltpu
from jax.sharding import PartitionSpec as P

EPS = 1e-05
VMEM_LIMIT = 12 * 1024 * 1024


def act(values):
    values = values.astype(jnp.float32)
    scaled = values * lax.rsqrt(jnp.mean(values * values, axis=-1, keepdims=True) + EPS)
    return scaled * (0.5 + 0.5 * jnp.tanh(0.5 * scaled))


def fill(even, odd, at, values, width):
    planes, _, chans = values.shape
    field = act(values)
    edge = jnp.zeros((planes, width, chans), jnp.float32)
    even[pl.ds(at, planes)] = field.astype(jnp.bfloat16)
    odd[pl.ds(at, planes)] = jnp.concatenate([edge, field, edge], axis=1).astype(jnp.bfloat16)


def convolve(even, odd, weights, planes, width):
    _, voxels, chans = even.shape
    taps = []
    for i in range(3):
        for j in range(3):
            part = even[i : i + planes] if j == 1 else odd[i : i + planes, j * width : j * width + voxels]
            taps.append(part.reshape(planes * voxels, chans))
    slab = jnp.concatenate(taps, axis=-1)
    total = None
    for k in (1, 0, 2):
        columns = jnp.concatenate([weights[(3 * n + k) * chans : (3 * n + k + 1) * chans] for n in range(9)], axis=0)
        part = jnp.dot(slab, columns, preferred_element_type=jnp.float32).reshape(-1, width, chans)
        column = lax.broadcasted_iota(jnp.int32, part.shape, 1)
        if k == 0:
            part = jnp.where(column == 0, 0.0, pltpu.roll(part, 1, 1))
        elif k == 2:
            part = jnp.where(column == width - 1, 0.0, pltpu.roll(part, width - 1, 1))
        total = part if total is None else total + part
    return total.reshape(planes, voxels, chans)


def first_kernel(width, flags, p_mid, q_mid, inner_halo, outer_halo, weights, low, mid, high, even, odd):
    planes = q_mid.shape[0]
    above = flags[2] > 0
    fill(even, odd, 2, q_mid[...], width)
    inner, outer = inner_halo[:2].astype(jnp.float32), outer_halo[:2].astype(jnp.float32)
    fill(even, odd, 0, jnp.where(above, outer, inner), width)
    fill(even, odd, 2 + planes, jnp.where(above, inner, outer), width)
    total = convolve(even, odd, weights, planes + 2, width)
    inner, outer = inner_halo[2:].astype(jnp.float32), outer_halo[2:].astype(jnp.float32)
    low[...] = jnp.where(flags[0] > 0, jnp.where(above, outer, inner) + total[:1], 0.0).astype(low.dtype)
    mid[...] = (p_mid[...].astype(jnp.float32) + total[1:-1]).astype(mid.dtype)
    high[...] = jnp.where(flags[1] > 0, jnp.where(above, inner, outer) + total[-1:], 0.0).astype(high.dtype)


def second_kernel(width, first_low, first_mid, first_high, q_mid, weights, out, even, odd):
    planes = q_mid.shape[0]
    fill(even, odd, 0, first_low[...], width)
    fill(even, odd, 1, first_mid[...], width)
    fill(even, odd, 1 + planes, first_high[...], width)
    total = convolve(even, odd, weights, planes, width)
    out[...] = (q_mid[...].astype(jnp.float32) + total).astype(out.dtype)


def scratch(planes, voxels, chans, width):
    return [
        pltpu.VMEM((planes, voxels, chans), jnp.bfloat16),
        pltpu.VMEM((planes, voxels + 2 * width, chans), jnp.bfloat16),
    ]


VMEM = pl.BlockSpec(memory_space=pltpu.VMEM)
SMEM = pl.BlockSpec(memory_space=pltpu.SMEM)


def first_half(flags, p, q, halos, weights, width):
    planes, voxels, chans = q.shape
    shape = lambda n: jax.ShapeDtypeStruct((n, voxels, chans), jnp.bfloat16)
    return pl.pallas_call(
        functools.partial(first_kernel, width),
        out_shape=(shape(1), shape(planes), shape(1)),
        in_specs=[SMEM] + [VMEM] * 5,
        out_specs=(VMEM, VMEM, VMEM),
        scratch_shapes=scratch(planes + 4, voxels, chans, width),
        compiler_params=pltpu.CompilerParams(vmem_limit_bytes=VMEM_LIMIT),
        cost_estimate=pl.CostEstimate(
            flops=1, bytes_accessed=1, transcendentals=0
        ),
    )(flags, p, q, *halos, weights)


def second_half(first, q, weights, width):
    planes, voxels, chans = q.shape
    return pl.pallas_call(
        functools.partial(second_kernel, width),
        out_shape=jax.ShapeDtypeStruct(q.shape, jnp.bfloat16),
        in_specs=[VMEM] * 5,
        out_specs=VMEM,
        scratch_shapes=scratch(planes + 2, voxels, chans, width),
        compiler_params=pltpu.CompilerParams(vmem_limit_bytes=VMEM_LIMIT),
        cost_estimate=pl.CostEstimate(
            flops=1, bytes_accessed=1, transcendentals=0
        ),
    )(*first, q, weights)


def boundary(block, upward, width):
    return lax.dynamic_slice_in_dim(block, jnp.where(upward, block.shape[0] - width, 0), width, axis=0)


def swapped(p, q, above):
    count = lax.axis_size("depth")

    def swap(upward, base):
        part = jnp.concatenate([boundary(q, upward, 2), boundary(p, upward, 1)], axis=0)
        pairs = [pair for i in range(base, count - 1, 2) for pair in ((i, i + 1), (i + 1, i))]
        return lax.ppermute(part, "depth", pairs)

    return swap(above, 0), swap(jnp.logical_not(above), 1)


def local(resident, previous, incoming, first_weights, second_weights):
    section = lax.axis_index("section")
    sections = lax.axis_size("section")
    half = sections // 2
    depth = lax.axis_index("depth")
    ticks = incoming.shape[0] + 1
    _, _, planes, rows, width, chans = resident.shape
    voxels = rows * width
    flat = lambda a: a.reshape(a.shape[0], 2, planes, voxels, chans)
    resident, previous, incoming = flat(resident)[0], flat(previous)[0], flat(incoming)
    w_one = first_weights.reshape(27 * chans, chans)
    w_two = second_weights.reshape(27 * chans, chans)
    above = depth % 2 == 0
    flags = jnp.stack([depth > 0, depth < lax.axis_size("depth") - 1, above]).astype(jnp.int32)

    def send(block, pairs):
        return lax.ppermute(block, "section", pairs) if pairs else block

    across = [(j, sections - 1 - j) for j in range(1, half - 1)]
    decoder = section >= half

    def join(held, skip):
        total = (held.astype(jnp.float32) + skip.astype(jnp.float32)).astype(jnp.bfloat16)
        return jnp.where(decoder, total, held)

    newer, older, relayed, direct = {}, {}, {}, {}

    def arrived(slot, stream):
        fresh = incoming[min(slot, ticks - 1) - 1, stream]
        if slot == 1:
            return jnp.where(section == 0, fresh, join(resident[stream], mirrored[stream]))
        held = jnp.where(section == 1, older[stream], newer[stream])
        skip = jnp.where(section == sections - 1, relayed[stream], newer[stream])
        if across:
            skip = jnp.where((section > half) & (section < sections - 1), direct[stream], skip)
        return jnp.where(section == 0, fresh, join(held, skip))

    for slot in range(ticks + 1):
        if slot == 0:
            p, q = resident
            halos = swapped(p, q, above)
            inner, previous = lax.optimization_barrier((halos[0], previous))
            halos = (inner, halos[1])
            mirrored = send(previous, [(j, sections - 1 - j) for j in range(half)])
        else:
            if slot == 1:
                mirrored, _ = lax.optimization_barrier((mirrored, first[1]))
            p = arrived(slot, 0)
            if slot > 1:
                p, newer[1] = lax.optimization_barrier((p, newer[1]))
            q = arrived(slot, 1)
            halos = swapped(p, q, above)
        first = first_half(flags, p, q, halos, w_one, width)
        onward = [(j, j + 1) for j in range(1, sections - 1)]
        if slot < ticks - 1:
            onward = [(0, 1)] + onward
        received = relays = {}
        if 0 < slot < ticks:
            received = {0: send(first[1], onward)}
        second = second_half(first, q, w_two, width)
        if slot == 0:
            received = send(jnp.stack([first[1], second]), [(0, 1)])
        elif slot < ticks:
            received[1] = send(second, onward)
            held = jnp.stack([newer[0], newer[1]])
            if slot == 1:
                held, _ = lax.optimization_barrier((held, first[1]))
            relays = send(held, [(1, sections - 1)])
            if across:
                direct = {0: send(first[1], across), 1: send(second, across)}
        older, newer, relayed = newer, received, relays
    result = jnp.stack([first[1], second])
    return result.reshape(1, 2, planes, rows, width, chans)


def solution(mesh):
    in_specs = (
        P("section", None, "depth", None, None, None),
        P("section", None, "depth", None, None, None),
        P(None, None, "depth", None, None, None),
        P("section", None, None, None, None, None),
        P("section", None, None, None, None, None),
    )
    out_specs = P("section", None, "depth", None, None, None)
    return jax.shard_map(local, mesh=mesh, in_specs=in_specs, out_specs=out_specs, check_vma=False)
```

```python
import functools

import jax
import jax.numpy as jnp
from jax import lax
from jax.experimental import pallas as pl
from jax.experimental.pallas import tpu as pltpu
from jax.sharding import PartitionSpec as P

EPS = 1e-05
VMEM_LIMIT = 12 * 1024 * 1024


def act(values):
    values = values.astype(jnp.float32)
    scaled = values * lax.rsqrt(jnp.mean(values * values, axis=-1, keepdims=True) + EPS)
    return scaled * (0.5 + 0.5 * jnp.tanh(0.5 * scaled))


def fill(even, odd, at, values, width):
    planes, _, chans = values.shape
    field = act(values)
    edge = jnp.zeros((planes, width, chans), jnp.float32)
    even[pl.ds(at, planes)] = field.astype(jnp.bfloat16)
    odd[pl.ds(at, planes)] = jnp.concatenate([edge, field, edge], axis=1).astype(jnp.bfloat16)


def convolve(taps, weights, width):
    planes, voxels, chans = taps[0].shape
    slab = jnp.concatenate([part.reshape(planes * voxels, chans) for part in taps], axis=-1)
    total = None
    for k in (1, 0, 2):
        columns = jnp.concatenate([weights[(3 * n + k) * chans : (3 * n + k + 1) * chans] for n in range(9)], axis=0)
        part = jnp.dot(slab, columns, preferred_element_type=jnp.float32).reshape(-1, width, chans)
        column = lax.broadcasted_iota(jnp.int32, part.shape, 1)
        if k == 0:
            part = jnp.where(column == 0, 0.0, pltpu.roll(part, 1, 1))
        elif k == 2:
            part = jnp.where(column == width - 1, 0.0, pltpu.roll(part, width - 1, 1))
        total = part if total is None else total + part
    return total.reshape(planes, voxels, chans)


def planes_at(even, odd, start, count, width):
    voxels = even.shape[1]
    return [
        even[start : start + count] if j == 1 else odd[start : start + count, j * width : j * width + voxels]
        for j in range(3)
    ]


def inner_kernel(width, p, q, weights, even, odd, inner):
    planes = q.shape[0]
    fill(even, odd, 0, q[...], width)
    taps = [part for i in range(3) for part in planes_at(even, odd, i, planes - 2, width)]
    inner[...] = (p[1:-1].astype(jnp.float32) + convolve(taps, weights, width)).astype(inner.dtype)


def loading_kernel(width, p, q, weights_hbm, even, odd, inner, weights, sem):
    copy = pltpu.make_async_copy(weights_hbm, weights, sem)
    copy.start()
    planes = q.shape[0]
    fill(even, odd, 0, q[...], width)
    taps = [part for i in range(3) for part in planes_at(even, odd, i, planes - 2, width)]
    copy.wait()
    inner[...] = (p[1:-1].astype(jnp.float32) + convolve(taps, weights, width)).astype(inner.dtype)


def edge_kernel(
    width, flags, p, even, odd, inner, q_near, q_far, p_near, p_far, weights, low, mid, high, edge_even, edge_odd
):
    planes = p.shape[0]
    above = flags[2] > 0
    near, far = q_near[:2].astype(jnp.float32), q_far[:2].astype(jnp.float32)
    fill(edge_even, edge_odd, 0, jnp.where(above, far, near), width)
    fill(edge_even, edge_odd, 2, jnp.where(above, near, far), width)
    halo = lambda start, count: planes_at(edge_even, edge_odd, start, count, width)
    own = lambda start, count: planes_at(even, odd, start, count, width)
    sources = (
        (halo(0, 2), own(planes - 2, 2)),
        (halo(1, 1), own(0, 1), own(planes - 1, 1), halo(2, 1)),
        (own(0, 2), halo(2, 2)),
    )
    taps = [jnp.concatenate(parts, axis=0) for source in sources for parts in zip(*source)]
    total = convolve(taps, weights, width)
    near, far = p_near[-1:].astype(jnp.float32), p_far[-1:].astype(jnp.float32)
    low[...] = jnp.where(flags[0] > 0, jnp.where(above, far, near) + total[:1], 0.0).astype(low.dtype)
    mid[pl.ds(0, 1)] = (p[:1].astype(jnp.float32) + total[1:2]).astype(mid.dtype)
    mid[pl.ds(1, planes - 2)] = inner[...]
    mid[pl.ds(planes - 1, 1)] = (p[-1:].astype(jnp.float32) + total[2:3]).astype(mid.dtype)
    high[...] = jnp.where(flags[1] > 0, jnp.where(above, near, far) + total[3:], 0.0).astype(high.dtype)


def second_kernel(width, first_low, first_mid, first_high, q, weights, out, even, odd):
    planes = q.shape[0]
    fill(even, odd, 0, first_low[...], width)
    fill(even, odd, 1, first_mid[...], width)
    fill(even, odd, 1 + planes, first_high[...], width)
    taps = [part for i in range(3) for part in planes_at(even, odd, i, planes, width)]
    second = (q[...].astype(jnp.float32) + convolve(taps, weights, width)).astype(out.dtype)
    if len(out.shape) == 4:
        out[0] = first_mid[...]
        out[1] = second
    else:
        out[...] = second


def call(kernel, out_shape, scratch, arguments, width):
    specs = [pl.BlockSpec(memory_space=pltpu.VMEM) for _ in arguments]
    if kernel is edge_kernel:
        specs[0] = pl.BlockSpec(memory_space=pltpu.SMEM)
    if kernel is loading_kernel:
        specs[-1] = pl.BlockSpec(memory_space=pltpu.HBM)
    shapes = [jax.ShapeDtypeStruct(shape, jnp.bfloat16) for shape in out_shape]
    return pl.pallas_call(
        functools.partial(kernel, width),
        out_shape=shapes,
        in_specs=specs,
        out_specs=[pl.BlockSpec(memory_space=pltpu.VMEM) for _ in shapes],
        scratch_shapes=[pltpu.VMEM(shape, jnp.bfloat16) if shape else pltpu.SemaphoreType.DMA for shape in scratch],
        compiler_params=pltpu.CompilerParams(vmem_limit_bytes=VMEM_LIMIT),
        cost_estimate=pl.CostEstimate(flops=1, bytes_accessed=1, transcendentals=0),
    )(*arguments)


def stored(planes, voxels, chans, width):
    return (planes, voxels, chans), (planes, voxels + 2 * width, chans)


def inner_half(p, q, weights, width, load):
    planes, voxels, chans = q.shape
    shapes = [*stored(planes, voxels, chans, width), (planes - 2, voxels, chans)]
    if load:
        weights = pltpu.with_memory_space_constraint(weights, pltpu.HBM)
        return call(loading_kernel, shapes + [weights.shape], [()], (p, q, weights), width)
    return *call(inner_kernel, shapes, [], (p, q, weights), width), weights


def first_half(flags, p, kept, q_halos, p_halos, weights, width):
    planes, voxels, chans = p.shape
    return call(
        edge_kernel,
        [(1, voxels, chans), (planes, voxels, chans), (1, voxels, chans)],
        stored(4, voxels, chans, width),
        (flags, p, *kept, *q_halos, *p_halos, weights),
        width,
    )


def second_half(first, q, weights, width, both):
    planes, voxels, chans = q.shape
    (out,) = call(
        second_kernel,
        [(2, *q.shape) if both else q.shape],
        stored(planes + 2, voxels, chans, width),
        (*first, q, weights),
        width,
    )
    return out


def boundary(block, upward, width):
    return lax.dynamic_slice_in_dim(block, jnp.where(upward, block.shape[0] - width, 0), width, axis=0)


def swapped(blocks, widths, above):
    count = lax.axis_size("depth")

    def swap(upward, base):
        part = jnp.concatenate([boundary(block, upward, width) for block, width in zip(blocks, widths)], axis=0)
        pairs = [pair for i in range(base, count - 1, 2) for pair in ((i, i + 1), (i + 1, i))]
        return lax.ppermute(part, "depth", pairs)

    return swap(above, 0), swap(jnp.logical_not(above), 1)


def local(resident, previous, incoming, first_weights, second_weights):
    section = lax.axis_index("section")
    sections = lax.axis_size("section")
    half = sections // 2
    depth = lax.axis_index("depth")
    ticks = incoming.shape[0] + 1
    _, _, planes, rows, width, chans = resident.shape
    voxels = rows * width
    flat = lambda a: a.reshape(a.shape[0], 2, planes, voxels, chans)
    resident, previous, incoming = flat(resident)[0], flat(previous)[0], flat(incoming)
    w_one = first_weights.reshape(27 * chans, chans)
    w_two = second_weights.reshape(27 * chans, chans)
    above = depth % 2 == 0
    flags = jnp.stack([depth > 0, depth < lax.axis_size("depth") - 1, above]).astype(jnp.int32)

    def send(block, pairs):
        return lax.ppermute(block, "section", pairs) if pairs else block

    across = [(j, sections - 1 - j) for j in range(1, half - 1)]
    decoder = section >= half

    def join(held, skip):
        total = (held.astype(jnp.float32) + skip.astype(jnp.float32)).astype(jnp.bfloat16)
        return jnp.where(decoder, total, held)

    newer, older, relayed, direct = {}, {}, {}, {}

    def arrived(slot, stream):
        fresh = incoming[min(slot, ticks - 1) - 1, stream]
        if slot == 1:
            return jnp.where(section == 0, fresh, join(resident[stream], mirrored[stream]))
        held = jnp.where(section == 1, older[stream], newer[stream])
        skip = jnp.where(section == sections - 1, relayed[stream], newer[stream])
        if across:
            skip = jnp.where((section > half) & (section < sections - 1), direct[stream], skip)
        return jnp.where(section == 0, fresh, join(held, skip))

    p, q = resident
    mirrored = send(previous, [(j, sections - 1 - j) for j in range(half)])
    q_halos = p_halos = swapped((q, p), (2, 1), above)
    for slot in range(ticks + 1):
        if slot == 1:
            p, q, q_halos = following
            p_halos = q_halos
        elif slot > 1:
            p = arrived(slot, 0)
            p_halos = swapped((p,), (1,), above)
            p, p_halos, newer[1] = lax.optimization_barrier((p, p_halos, newer[1]))
            q = arrived(slot, 1)
            q_halos = swapped((q,), (2,), above)
        *kept, w_one = inner_half(p, q, w_one, width, slot == 0)
        first = first_half(flags, p, kept, q_halos, p_halos, w_one, width)
        onward = [(j, j + 1) for j in range(1, sections - 1)]
        if slot < ticks - 1:
            onward = [(0, 1)] + onward
        received, relays = {}, {}
        if slot == 0:
            mirrored, _ = lax.optimization_barrier((mirrored, first[1]))
            following = arrived(1, 0), arrived(1, 1)
            following = *following, swapped(following[::-1], (2, 1), above)
            first, joined = lax.optimization_barrier((first, following[:2]))
            following = *joined, following[2]
        elif slot < ticks:
            received[0] = send(first[1], onward)
        second = second_half(first, q, w_two, width, slot == ticks)
        if slot == 0:
            second, q_halos = lax.optimization_barrier((second, following[2]))
            following = *following[:2], q_halos
            received = send(jnp.stack([first[1], second]), [(0, 1)])
        elif slot < ticks:
            received[1] = send(second, onward)
            relay_p, relay_q = newer[0], newer[1]
            if slot == 1:
                relay_p, _ = lax.optimization_barrier((relay_p, first[1]))
            relay_q, second = lax.optimization_barrier((relay_q, second))
            relays = {0: send(relay_p, [(1, sections - 1)]), 1: send(relay_q, [(1, sections - 1)])}
            if across:
                direct = {0: send(first[1], across), 1: send(second, across)}
        older, newer, relayed = newer, received, relays
    result = second
    return result.reshape(1, 2, planes, rows, width, chans)


def solution(mesh):
    in_specs = (
        P("section", None, "depth", None, None, None),
        P("section", None, "depth", None, None, None),
        P(None, None, "depth", None, None, None),
        P("section", None, None, None, None, None),
        P("section", None, None, None, None, None),
    )
    out_specs = P("section", None, "depth", None, None, None)
    return jax.shard_map(local, mesh=mesh, in_specs=in_specs, out_specs=out_specs, check_vma=False)
```

```python
import functools

import jax
import jax.numpy as jnp
from jax import lax
from jax.experimental import pallas as pl
from jax.experimental.pallas import tpu as pltpu
from jax.sharding import PartitionSpec as P

EPS = 1e-05
VMEM_LIMIT = 12 * 1024 * 1024


def act(values):
    values = values.astype(jnp.float32)
    scaled = values * lax.rsqrt(jnp.mean(values * values, axis=-1, keepdims=True) + EPS)
    return scaled * (0.5 + 0.5 * jnp.tanh(0.5 * scaled))


def fill(even, odd, at, values, width):
    planes, _, chans = values.shape
    field = act(values)
    edge = jnp.zeros((planes, width, chans), jnp.float32)
    even[pl.ds(at, planes)] = field.astype(jnp.bfloat16)
    odd[pl.ds(at, planes)] = jnp.concatenate([edge, field, edge], axis=1).astype(jnp.bfloat16)


def convolve(taps, weights, width):
    planes, voxels, chans = taps[0].shape
    slab = jnp.concatenate([part.reshape(planes * voxels, chans) for part in taps], axis=-1)
    total = None
    for k in (1, 0, 2):
        columns = jnp.concatenate([weights[(3 * n + k) * chans : (3 * n + k + 1) * chans] for n in range(9)], axis=0)
        part = jnp.dot(slab, columns, preferred_element_type=jnp.float32).reshape(-1, width, chans)
        column = lax.broadcasted_iota(jnp.int32, part.shape, 1)
        if k == 0:
            part = jnp.where(column == 0, 0.0, pltpu.roll(part, 1, 1))
        elif k == 2:
            part = jnp.where(column == width - 1, 0.0, pltpu.roll(part, width - 1, 1))
        total = part if total is None else total + part
    return total.reshape(planes, voxels, chans)


def planes_at(even, odd, start, count, width):
    voxels = even.shape[1]
    return [
        even[start : start + count] if j == 1 else odd[start : start + count, j * width : j * width + voxels]
        for j in range(3)
    ]


def inner_kernel(width, p, q, weights, even, odd, inner):
    planes = q.shape[0]
    fill(even, odd, 0, q[...], width)
    taps = [part for i in range(3) for part in planes_at(even, odd, i, planes - 2, width)]
    inner[...] = (p[1:-1].astype(jnp.float32) + convolve(taps, weights, width)).astype(inner.dtype)


def loading_kernel(width, p, q, weights_hbm, even, odd, inner, weights, sem):
    copy = pltpu.make_async_copy(weights_hbm, weights, sem)
    copy.start()
    planes = q.shape[0]
    fill(even, odd, 0, q[...], width)
    taps = [part for i in range(3) for part in planes_at(even, odd, i, planes - 2, width)]
    copy.wait()
    inner[...] = (p[1:-1].astype(jnp.float32) + convolve(taps, weights, width)).astype(inner.dtype)


def edge_kernel(
    width, flags, p, even, odd, inner, q_near, q_far, p_near, p_far, weights, low, mid, high, edge_even, edge_odd
):
    planes = p.shape[0]
    above = flags[2] > 0
    near, far = q_near[:2].astype(jnp.float32), q_far[:2].astype(jnp.float32)
    fill(edge_even, edge_odd, 0, jnp.where(above, far, near), width)
    fill(edge_even, edge_odd, 2, jnp.where(above, near, far), width)
    halo = lambda start, count: planes_at(edge_even, edge_odd, start, count, width)
    own = lambda start, count: planes_at(even, odd, start, count, width)
    sources = (
        (halo(0, 2), own(planes - 2, 2)),
        (halo(1, 1), own(0, 1), own(planes - 1, 1), halo(2, 1)),
        (own(0, 2), halo(2, 2)),
    )
    taps = [jnp.concatenate(parts, axis=0) for source in sources for parts in zip(*source)]
    total = convolve(taps, weights, width)
    near, far = p_near[-1:].astype(jnp.float32), p_far[-1:].astype(jnp.float32)
    low[...] = jnp.where(flags[0] > 0, jnp.where(above, far, near) + total[:1], 0.0).astype(low.dtype)
    mid[pl.ds(0, 1)] = (p[:1].astype(jnp.float32) + total[1:2]).astype(mid.dtype)
    mid[pl.ds(1, planes - 2)] = inner[...]
    mid[pl.ds(planes - 1, 1)] = (p[-1:].astype(jnp.float32) + total[2:3]).astype(mid.dtype)
    high[...] = jnp.where(flags[1] > 0, jnp.where(above, near, far) + total[3:], 0.0).astype(high.dtype)


def second_kernel(width, first_low, first_mid, first_high, q, weights, out, even, odd):
    planes = q.shape[0]
    fill(even, odd, 0, first_low[...], width)
    fill(even, odd, 1, first_mid[...], width)
    fill(even, odd, 1 + planes, first_high[...], width)
    taps = [part for i in range(3) for part in planes_at(even, odd, i, planes, width)]
    second = (q[...].astype(jnp.float32) + convolve(taps, weights, width)).astype(out.dtype)
    if len(out.shape) == 4:
        out[0] = first_mid[...]
        out[1] = second
    else:
        out[...] = second


def call(kernel, out_shape, scratch, arguments, width):
    specs = [pl.BlockSpec(memory_space=pltpu.VMEM) for _ in arguments]
    if kernel is edge_kernel:
        specs[0] = pl.BlockSpec(memory_space=pltpu.SMEM)
    if kernel is loading_kernel:
        specs[-1] = pl.BlockSpec(memory_space=pltpu.HBM)
    shapes = [jax.ShapeDtypeStruct(shape, jnp.bfloat16) for shape in out_shape]
    return pl.pallas_call(
        functools.partial(kernel, width),
        out_shape=shapes,
        in_specs=specs,
        out_specs=[pl.BlockSpec(memory_space=pltpu.VMEM) for _ in shapes],
        scratch_shapes=[pltpu.VMEM(shape, jnp.bfloat16) if shape else pltpu.SemaphoreType.DMA for shape in scratch],
        compiler_params=pltpu.CompilerParams(vmem_limit_bytes=VMEM_LIMIT),
        cost_estimate=pl.CostEstimate(flops=1, bytes_accessed=1, transcendentals=0),
    )(*arguments)


def stored(planes, voxels, chans, width):
    return (planes, voxels, chans), (planes, voxels + 2 * width, chans)


def inner_half(p, q, weights, width, load):
    planes, voxels, chans = q.shape
    shapes = [*stored(planes, voxels, chans, width), (planes - 2, voxels, chans)]
    if load:
        weights = pltpu.with_memory_space_constraint(weights, pltpu.HBM)
        return call(loading_kernel, shapes + [weights.shape], [()], (p, q, weights), width)
    return *call(inner_kernel, shapes, [], (p, q, weights), width), weights


def first_half(flags, p, kept, q_halos, p_halos, weights, width):
    planes, voxels, chans = p.shape
    return call(
        edge_kernel,
        [(1, voxels, chans), (planes, voxels, chans), (1, voxels, chans)],
        stored(4, voxels, chans, width),
        (flags, p, *kept, *q_halos, *p_halos, weights),
        width,
    )


def second_half(first, q, weights, width, both):
    planes, voxels, chans = q.shape
    (out,) = call(
        second_kernel,
        [(2, *q.shape) if both else q.shape],
        stored(planes + 2, voxels, chans, width),
        (*first, q, weights),
        width,
    )
    return out


def swapped(blocks, widths, starts):
    count = lax.axis_size("depth")

    def swap(turn):
        parts = [
            lax.dynamic_slice_in_dim(block, starts[width][turn], width, axis=0) for block, width in zip(blocks, widths)
        ]
        pairs = [pair for i in range(turn, count - 1, 2) for pair in ((i, i + 1), (i + 1, i))]
        return lax.ppermute(jnp.concatenate(parts, axis=0), "depth", pairs)

    return swap(0), swap(1)


def local(resident, previous, incoming, first_weights, second_weights):
    section = lax.axis_index("section")
    sections = lax.axis_size("section")
    half = sections // 2
    depth = lax.axis_index("depth")
    ticks = incoming.shape[0] + 1
    _, _, planes, rows, width, chans = resident.shape
    voxels = rows * width
    across = [(j, sections - 1 - j) for j in range(1, half - 1)]

    above = depth % 2 == 0
    places = {
        "flags": jnp.stack([depth > 0, depth < lax.axis_size("depth") - 1, above]).astype(jnp.int32),
        "starts": {
            n: (jnp.where(above, planes - n, 0), jnp.where(above, 0, planes - n)) for n in (1, 2)
        },
        "first": section == 0,
        "second": section == 1,
        "last": section == sections - 1,
        "decoder": section >= half,
        "direct": (section > half) & (section < sections - 1) if across else (),
    }
    places, resident, previous, incoming, first_weights, second_weights = lax.optimization_barrier(
        (places, resident, previous, incoming, first_weights, second_weights)
    )
    flags, starts = places["flags"], places["starts"]

    flat = lambda a: a.reshape(a.shape[0], 2, planes, voxels, chans)
    resident, previous, incoming = flat(resident)[0], flat(previous)[0], flat(incoming)
    w_one = first_weights.reshape(27 * chans, chans)
    w_two = second_weights.reshape(27 * chans, chans)

    def send(block, pairs):
        return lax.ppermute(block, "section", pairs) if pairs else block

    def join(held, skip):
        total = (held.astype(jnp.float32) + skip.astype(jnp.float32)).astype(jnp.bfloat16)
        return jnp.where(places["decoder"], total, held)

    newer, older, relayed, direct = {}, {}, {}, {}

    def arrived(slot, stream):
        fresh = incoming[min(slot, ticks - 1) - 1, stream]
        if slot == 1:
            return jnp.where(places["first"], fresh, join(resident[stream], mirrored[stream]))
        held = jnp.where(places["second"], older[stream], newer[stream])
        skip = jnp.where(places["last"], relayed[stream], newer[stream])
        if across:
            skip = jnp.where(places["direct"], direct[stream], skip)
        return jnp.where(places["first"], fresh, join(held, skip))

    p, q = resident
    mirrored = send(previous, [(j, sections - 1 - j) for j in range(half)])
    q_halos = p_halos = swapped((q, p), (2, 1), starts)
    for slot in range(ticks + 1):
        if slot == 1:
            p, q, q_halos = following
            p_halos = q_halos
        elif slot > 1:
            p = arrived(slot, 0)
            p_halos = swapped((p,), (1,), starts)
            p, p_halos, newer[1] = lax.optimization_barrier((p, p_halos, newer[1]))
            q = arrived(slot, 1)
            q_halos = swapped((q,), (2,), starts)
        *kept, w_one = inner_half(p, q, w_one, width, slot == 0)
        first = first_half(flags, p, kept, q_halos, p_halos, w_one, width)
        onward = [(j, j + 1) for j in range(1, sections - 1)]
        if slot < ticks - 1:
            onward = [(0, 1)] + onward
        received, relays = {}, {}
        if slot == 0:
            mirrored, _ = lax.optimization_barrier((mirrored, first[1]))
            following = arrived(1, 0), arrived(1, 1)
            following = *following, swapped(following[::-1], (2, 1), starts)
            first, joined = lax.optimization_barrier((first, following[:2]))
            following = *joined, following[2]
        elif slot < ticks:
            received[0] = send(first[1], onward)
        second = second_half(first, q, w_two, width, slot == ticks)
        if slot == 0:
            second, q_halos = lax.optimization_barrier((second, following[2]))
            following = *following[:2], q_halos
            received = send(jnp.stack([first[1], second]), [(0, 1)])
        elif slot < ticks:
            received[1] = send(second, onward)
            relay_p, relay_q = newer[0], newer[1]
            if slot == 1:
                relay_p, second = lax.optimization_barrier((relay_p, second))
            relay_q, second = lax.optimization_barrier((relay_q, second))
            relays = {0: send(relay_p, [(1, sections - 1)]), 1: send(relay_q, [(1, sections - 1)])}
            if across:
                direct = {0: send(first[1], across), 1: send(second, across)}
        older, newer, relayed = newer, received, relays
    result = second
    return result.reshape(1, 2, planes, rows, width, chans)


def solution(mesh):
    in_specs = (
        P("section", None, "depth", None, None, None),
        P("section", None, "depth", None, None, None),
        P(None, None, "depth", None, None, None),
        P("section", None, None, None, None, None),
        P("section", None, None, None, None, None),
    )
    out_specs = P("section", None, "depth", None, None, None)
    return jax.shard_map(local, mesh=mesh, in_specs=in_specs, out_specs=out_specs, check_vma=False)
```

```python
import functools

import jax
import jax.numpy as jnp
from jax import lax
from jax.experimental import pallas as pl
from jax.experimental.pallas import tpu as pltpu
from jax.sharding import PartitionSpec as P

EPS = 1e-05
VMEM_LIMIT = 12 * 1024 * 1024


def act(values):
    values = values.astype(jnp.float32)
    scaled = values * lax.rsqrt(jnp.mean(values * values, axis=-1, keepdims=True) + EPS)
    return scaled * (0.5 + 0.5 * jnp.tanh(0.5 * scaled))


def fill(even, odd, at, values, width):
    planes, _, chans = values.shape
    field = act(values)
    edge = jnp.zeros((planes, width, chans), jnp.float32)
    even[pl.ds(at, planes)] = field.astype(jnp.bfloat16)
    odd[pl.ds(at, planes)] = jnp.concatenate([edge, field, edge], axis=1).astype(jnp.bfloat16)


def convolve(taps, weights, width):
    planes, voxels, chans = taps[0].shape
    slab = jnp.concatenate([part.reshape(planes * voxels, chans) for part in taps], axis=-1)
    total = None
    for k in (1, 0, 2):
        columns = jnp.concatenate([weights[(3 * n + k) * chans : (3 * n + k + 1) * chans] for n in range(9)], axis=0)
        part = jnp.dot(slab, columns, preferred_element_type=jnp.float32).reshape(-1, width, chans)
        column = lax.broadcasted_iota(jnp.int32, part.shape, 1)
        if k == 0:
            part = jnp.where(column == 0, 0.0, pltpu.roll(part, 1, 1))
        elif k == 2:
            part = jnp.where(column == width - 1, 0.0, pltpu.roll(part, width - 1, 1))
        total = part if total is None else total + part
    return total.reshape(planes, voxels, chans)


def planes_at(even, odd, start, count, width):
    voxels = even.shape[1]
    return [
        even[start : start + count] if j == 1 else odd[start : start + count, j * width : j * width + voxels]
        for j in range(3)
    ]


def inner_kernel(width, p, q, weights, even, odd, inner):
    planes = q.shape[0]
    fill(even, odd, 0, q[...], width)
    taps = [part for i in range(3) for part in planes_at(even, odd, i, planes - 2, width)]
    inner[...] = (p[1:-1].astype(jnp.float32) + convolve(taps, weights, width)).astype(inner.dtype)


def loading_kernel(width, p, q, weights_hbm, even, odd, inner, weights, sem):
    copy = pltpu.make_async_copy(weights_hbm, weights, sem)
    copy.start()
    planes = q.shape[0]
    fill(even, odd, 0, q[...], width)
    taps = [part for i in range(3) for part in planes_at(even, odd, i, planes - 2, width)]
    copy.wait()
    inner[...] = (p[1:-1].astype(jnp.float32) + convolve(taps, weights, width)).astype(inner.dtype)


def edge_kernel(
    width, flags, p, even, odd, inner, q_near, q_far, p_near, p_far, weights, low, mid, high, edge_even, edge_odd
):
    planes = p.shape[0]
    above = flags[2] > 0
    near, far = q_near[:2].astype(jnp.float32), q_far[:2].astype(jnp.float32)
    fill(edge_even, edge_odd, 0, jnp.where(above, far, near), width)
    fill(edge_even, edge_odd, 2, jnp.where(above, near, far), width)
    halo = lambda start, count: planes_at(edge_even, edge_odd, start, count, width)
    own = lambda start, count: planes_at(even, odd, start, count, width)
    sources = (
        (halo(0, 2), own(planes - 2, 2)),
        (halo(1, 1), own(0, 1), own(planes - 1, 1), halo(2, 1)),
        (own(0, 2), halo(2, 2)),
    )
    taps = [jnp.concatenate(parts, axis=0) for source in sources for parts in zip(*source)]
    total = convolve(taps, weights, width)
    near, far = p_near[-1:].astype(jnp.float32), p_far[-1:].astype(jnp.float32)
    low[...] = jnp.where(flags[0] > 0, jnp.where(above, far, near) + total[:1], 0.0).astype(low.dtype)
    mid[pl.ds(0, 1)] = (p[:1].astype(jnp.float32) + total[1:2]).astype(mid.dtype)
    mid[pl.ds(1, planes - 2)] = inner[...]
    mid[pl.ds(planes - 1, 1)] = (p[-1:].astype(jnp.float32) + total[2:3]).astype(mid.dtype)
    high[...] = jnp.where(flags[1] > 0, jnp.where(above, near, far) + total[3:], 0.0).astype(high.dtype)


def second_kernel(width, first_low, first_mid, first_high, q, weights, out, even, odd):
    planes = q.shape[0]
    fill(even, odd, 0, first_low[...], width)
    fill(even, odd, 1, first_mid[...], width)
    fill(even, odd, 1 + planes, first_high[...], width)
    taps = [part for i in range(3) for part in planes_at(even, odd, i, planes, width)]
    second = (q[...].astype(jnp.float32) + convolve(taps, weights, width)).astype(out.dtype)
    if len(out.shape) == 4:
        out[0] = first_mid[...]
        out[1] = second
    else:
        out[...] = second


def call(kernel, out_shape, scratch, arguments, width):
    specs = [pl.BlockSpec(memory_space=pltpu.VMEM) for _ in arguments]
    if kernel is edge_kernel:
        specs[0] = pl.BlockSpec(memory_space=pltpu.SMEM)
    if kernel is loading_kernel:
        specs[-1] = pl.BlockSpec(memory_space=pltpu.HBM)
    shapes = [jax.ShapeDtypeStruct(shape, jnp.bfloat16) for shape in out_shape]
    return pl.pallas_call(
        functools.partial(kernel, width),
        out_shape=shapes,
        in_specs=specs,
        out_specs=[pl.BlockSpec(memory_space=pltpu.VMEM) for _ in shapes],
        scratch_shapes=[pltpu.VMEM(shape, jnp.bfloat16) if shape else pltpu.SemaphoreType.DMA for shape in scratch],
        compiler_params=pltpu.CompilerParams(vmem_limit_bytes=VMEM_LIMIT),
        cost_estimate=pl.CostEstimate(flops=1, bytes_accessed=1, transcendentals=0),
    )(*arguments)


def stored(planes, voxels, chans, width):
    return (planes, voxels, chans), (planes, voxels + 2 * width, chans)


def inner_half(p, q, weights, width, load):
    planes, voxels, chans = q.shape
    shapes = [*stored(planes, voxels, chans, width), (planes - 2, voxels, chans)]
    if load:
        weights = pltpu.with_memory_space_constraint(weights, pltpu.HBM)
        return call(loading_kernel, shapes + [weights.shape], [()], (p, q, weights), width)
    return *call(inner_kernel, shapes, [], (p, q, weights), width), weights


def first_half(flags, p, kept, q_halos, p_halos, weights, width):
    planes, voxels, chans = p.shape
    return call(
        edge_kernel,
        [(1, voxels, chans), (planes, voxels, chans), (1, voxels, chans)],
        stored(4, voxels, chans, width),
        (flags, p, *kept, *q_halos, *p_halos, weights),
        width,
    )


def second_half(first, q, weights, width, both):
    planes, voxels, chans = q.shape
    (out,) = call(
        second_kernel,
        [(2, *q.shape) if both else q.shape],
        stored(planes + 2, voxels, chans, width),
        (*first, q, weights),
        width,
    )
    return out


def swap(turn, starts, *blocks):
    count = lax.axis_size("depth")
    parts = [lax.dynamic_slice_in_dim(block, starts[n][turn], n, axis=0) for block, n in blocks]
    pairs = [pair for i in range(turn, count - 1, 2) for pair in ((i, i + 1), (i + 1, i))]
    return lax.ppermute(jnp.concatenate(parts, axis=0), "depth", pairs)


def local(resident, previous, incoming, first_weights, second_weights):
    section = lax.axis_index("section")
    sections = lax.axis_size("section")
    half = sections // 2
    depth = lax.axis_index("depth")
    ticks = incoming.shape[0] + 1
    _, _, planes, rows, width, chans = resident.shape
    voxels = rows * width
    across = [(j, sections - 1 - j) for j in range(1, half - 1)]

    above = depth % 2 == 0
    places = {
        "flags": jnp.stack([depth > 0, depth < lax.axis_size("depth") - 1, above]).astype(jnp.int32),
        "starts": {
            n: (jnp.where(above, planes - n, 0), jnp.where(above, 0, planes - n)) for n in (1, 2)
        },
        "first": section == 0,
        "second": section == 1,
        "last": section == sections - 1,
        "decoder": section >= half,
        "direct": (section > half) & (section < sections - 1) if across else (),
    }
    places, resident, previous, incoming, first_weights, second_weights = lax.optimization_barrier(
        (places, resident, previous, incoming, first_weights, second_weights)
    )
    flags, starts = places["flags"], places["starts"]

    flat = lambda a: a.reshape(a.shape[0], 2, planes, voxels, chans)
    resident, previous, incoming = flat(resident)[0], flat(previous)[0], flat(incoming)
    w_one = first_weights.reshape(27 * chans, chans)
    w_two = second_weights.reshape(27 * chans, chans)

    def send(block, pairs):
        return lax.ppermute(block, "section", pairs) if pairs else block

    def join(held, skip):
        total = (held.astype(jnp.float32) + skip.astype(jnp.float32)).astype(jnp.bfloat16)
        return jnp.where(places["decoder"], total, held)

    newer, older, relayed, direct = {}, {}, {}, {}

    def arrived(slot, stream):
        fresh = incoming[min(slot, ticks - 1) - 1, stream]
        if slot == 1:
            return jnp.where(places["first"], fresh, join(resident[stream], mirrored[stream]))
        held = jnp.where(places["second"], older[stream], newer[stream])
        skip = jnp.where(places["last"], relayed[stream], newer[stream])
        if across:
            skip = jnp.where(places["direct"], direct[stream], skip)
        return jnp.where(places["first"], fresh, join(held, skip))

    p, q = resident
    mirrored = send(previous, [(j, sections - 1 - j) for j in range(half)])
    near, q_far = (swap(turn, starts, (q, 2), (p, 1)) for turn in range(2))
    p_far = q_far
    for slot in range(ticks + 1):
        if slot == 1:
            p, q, near, q_far = following
            p_far = q_far
        elif slot > 1:
            p = arrived(slot, 0)
            p_far = swap(1, starts, (p, 1))
            p, p_far, newer[1] = lax.optimization_barrier((p, p_far, newer[1]))
            q = arrived(slot, 1)
            near = swap(0, starts, (q, 2), (p, 1))
            q_far = swap(1, starts, (q, 2))
        *kept, w_one = inner_half(p, q, w_one, width, slot == 0)
        first = first_half(flags, p, kept, (near, q_far), (near, p_far), w_one, width)
        onward = [(j, j + 1) for j in range(1, sections - 1)] if slot > 0 else []
        if slot < ticks - 1:
            onward = [(0, 1)] + onward
        received, relays = {}, {}
        if slot < ticks:
            received[0] = send(first[1], onward)
        second = second_half(first, q, w_two, width, slot == ticks)
        if slot < ticks:
            received[1] = send(second, onward)
        if slot == 0:
            mirrored, _ = lax.optimization_barrier((mirrored, second))
            following = arrived(1, 0), arrived(1, 1)
            following += tuple(swap(turn, starts, (following[1], 2), (following[0], 1)) for turn in range(2))
        elif slot < ticks:
            relay_q, second = lax.optimization_barrier((newer[1], second))
            relays = {0: send(newer[0], [(1, sections - 1)]), 1: send(relay_q, [(1, sections - 1)])}
            if across:
                direct = {0: send(first[1], across), 1: send(second, across)}
        older, newer, relayed = newer, received, relays
    result = second
    return result.reshape(1, 2, planes, rows, width, chans)


def solution(mesh):
    in_specs = (
        P("section", None, "depth", None, None, None),
        P("section", None, "depth", None, None, None),
        P(None, None, "depth", None, None, None),
        P("section", None, None, None, None, None),
        P("section", None, None, None, None, None),
    )
    out_specs = P("section", None, "depth", None, None, None)
    return jax.shard_map(local, mesh=mesh, in_specs=in_specs, out_specs=out_specs, check_vma=False)
```

```python
import functools

import jax
import jax.numpy as jnp
from jax import lax
from jax.experimental import pallas as pl
from jax.experimental.pallas import tpu as pltpu
from jax.sharding import PartitionSpec as P

EPS = 1e-05
VMEM_LIMIT = 12 * 1024 * 1024


def act(values):
    values = values.astype(jnp.float32)
    scaled = values * lax.rsqrt(jnp.mean(values * values, axis=-1, keepdims=True) + EPS)
    return scaled * (0.5 + 0.5 * jnp.tanh(0.5 * scaled))


def fill(even, odd, at, values, width):
    planes, _, chans = values.shape
    field = act(values)
    edge = jnp.zeros((planes, width, chans), jnp.float32)
    even[pl.ds(at, planes)] = field.astype(jnp.bfloat16)
    odd[pl.ds(at, planes)] = jnp.concatenate([edge, field, edge], axis=1).astype(jnp.bfloat16)


def convolve(taps, weights, width):
    planes, voxels, chans = taps[0].shape
    slab = jnp.concatenate([part.reshape(planes * voxels, chans) for part in taps], axis=-1)
    total = None
    for k in (1, 0, 2):
        columns = jnp.concatenate([weights[(3 * n + k) * chans : (3 * n + k + 1) * chans] for n in range(9)], axis=0)
        part = jnp.dot(slab, columns, preferred_element_type=jnp.float32).reshape(-1, width, chans)
        column = lax.broadcasted_iota(jnp.int32, part.shape, 1)
        if k == 0:
            part = jnp.where(column == 0, 0.0, pltpu.roll(part, 1, 1))
        elif k == 2:
            part = jnp.where(column == width - 1, 0.0, pltpu.roll(part, width - 1, 1))
        total = part if total is None else total + part
    return total.reshape(planes, voxels, chans)


def planes_at(even, odd, start, count, width):
    voxels = even.shape[1]
    return [
        even[start : start + count] if j == 1 else odd[start : start + count, j * width : j * width + voxels]
        for j in range(3)
    ]


def inner_kernel(width, field, weights, even, odd, total):
    planes = field.shape[0]
    fill(even, odd, 0, field[...], width)
    taps = [part for i in range(3) for part in planes_at(even, odd, i, planes - 2, width)]
    total[...] = convolve(taps, weights, width)


def loading_kernel(width, field, weights_hbm, even, odd, total, weights, sem):
    copy = pltpu.make_async_copy(weights_hbm, weights, sem)
    copy.start()
    planes = field.shape[0]
    fill(even, odd, 0, field[...], width)
    taps = [part for i in range(3) for part in planes_at(even, odd, i, planes - 2, width)]
    copy.wait()
    total[...] = convolve(taps, weights, width)


def edge_kernel(width, flags, near, far, even, odd, inner, weights, *rest):
    *added, out, edge_even, edge_odd = rest
    planes = even.shape[0]
    above = flags[0] > 0
    near, far = near[...].astype(jnp.float32), far[...].astype(jnp.float32)
    fill(edge_even, edge_odd, 0, jnp.where(above, far, near), width)
    fill(edge_even, edge_odd, 1, jnp.where(above, near, far), width)
    halo = lambda plane: planes_at(edge_even, edge_odd, plane, 1, width)
    own = lambda plane: planes_at(even, odd, plane, 1, width)
    sources = ((halo(0), own(planes - 2)), (own(0), own(planes - 1)), (own(1), halo(1)))
    taps = [jnp.concatenate(pair, axis=0) for source in sources for pair in zip(*source)]
    total = convolve(taps, weights, width)
    pieces = ((0, 1, total[:1]), (1, planes - 2, inner[...]), (planes - 1, 1, total[1:]))
    for start, count, piece in pieces:
        where = pl.ds(start, count)
        if added:
            piece = added[-1][where].astype(jnp.float32) + piece
        if len(added) == 2:
            out[0, where] = added[0][where]
            out[1, where] = piece.astype(out.dtype)
        else:
            out[where] = piece.astype(out.dtype)


def call(kernel, outputs, scratch, arguments, width):
    specs = [pl.BlockSpec(memory_space=pltpu.VMEM) for _ in arguments]
    if kernel is edge_kernel:
        specs[0] = pl.BlockSpec(memory_space=pltpu.SMEM)
    if kernel is loading_kernel:
        specs[-1] = pl.BlockSpec(memory_space=pltpu.HBM)
    return pl.pallas_call(
        functools.partial(kernel, width),
        out_shape=[jax.ShapeDtypeStruct(shape, dtype) for shape, dtype in outputs],
        in_specs=specs,
        out_specs=[pl.BlockSpec(memory_space=pltpu.VMEM) for _ in outputs],
        scratch_shapes=[pltpu.VMEM(shape, jnp.bfloat16) if shape else pltpu.SemaphoreType.DMA for shape in scratch],
        compiler_params=pltpu.CompilerParams(vmem_limit_bytes=VMEM_LIMIT),
        cost_estimate=pl.CostEstimate(flops=1, bytes_accessed=1, transcendentals=0),
    )(*arguments)


def stored(planes, voxels, chans, width):
    return (planes, voxels, chans), (planes, voxels + 2 * width, chans)


def inner_planes(field, weights, width, load=False):
    planes, voxels, chans = field.shape
    outputs = [(shape, jnp.bfloat16) for shape in stored(planes, voxels, chans, width)]
    outputs.append(((planes - 2, voxels, chans), jnp.float32))
    if load:
        weights = pltpu.with_memory_space_constraint(weights, pltpu.HBM)
        outputs.append((weights.shape, jnp.bfloat16))
        return call(loading_kernel, outputs, [()], (field, weights), width)
    return *call(inner_kernel, outputs, [], (field, weights), width), weights


def all_planes(flags, near, far, kept, weights, added, width):
    shape = kept[0].shape
    _, voxels, chans = shape
    output = ((2, *shape) if len(added) == 2 else shape, jnp.bfloat16 if added else jnp.float32)
    arguments = (flags, near, far, *kept, weights, *added)
    (out,) = call(edge_kernel, [output], stored(2, voxels, chans, width), arguments, width)
    return out


def swap(turn, starts, block):
    count = lax.axis_size("depth")
    pairs = [pair for i in range(turn, count - 1, 2) for pair in ((i, i + 1), (i + 1, i))]
    return lax.ppermute(lax.dynamic_slice_in_dim(block, starts[turn], 1, axis=0), "depth", pairs)


def local(resident, previous, incoming, first_weights, second_weights):
    section = lax.axis_index("section")
    sections = lax.axis_size("section")
    half = sections // 2
    depth = lax.axis_index("depth")
    ticks = incoming.shape[0] + 1
    _, _, planes, rows, width, chans = resident.shape
    voxels = rows * width
    across = [(j, sections - 1 - j) for j in range(1, half - 1)]

    above = depth % 2 == 0
    places = {
        "flags": jnp.stack([above]).astype(jnp.int32),
        "starts": (jnp.where(above, planes - 1, 0), jnp.where(above, 0, planes - 1)),
        "first": section == 0,
        "second": section == 1,
        "last": section == sections - 1,
        "decoder": section >= half,
        "direct": (section > half) & (section < sections - 1) if across else (),
    }
    places, resident, previous, incoming, first_weights, second_weights = lax.optimization_barrier(
        (places, resident, previous, incoming, first_weights, second_weights)
    )
    flags, starts = places["flags"], places["starts"]

    flat = lambda a: a.reshape(a.shape[0], 2, planes, voxels, chans)
    resident, previous, incoming = flat(resident)[0], flat(previous)[0], flat(incoming)
    w_one = first_weights.reshape(27 * chans, chans)
    w_two = second_weights.reshape(27 * chans, chans)

    def send(block, pairs):
        return lax.ppermute(block, "section", pairs) if pairs else block

    def join(held, skip):
        total = (held.astype(jnp.float32) + skip.astype(jnp.float32)).astype(jnp.bfloat16)
        return jnp.where(places["decoder"], total, held)

    newer, older, relayed, direct = {}, {}, {}, {}

    def arrived(slot, stream):
        fresh = incoming[min(slot, ticks - 1) - 1, stream]
        if slot == 1:
            return jnp.where(places["first"], fresh, join(resident[stream], mirrored[stream]))
        held = jnp.where(places["second"], older[stream], newer[stream])
        skip = jnp.where(places["last"], relayed[stream], newer[stream])
        if across:
            skip = jnp.where(places["direct"], direct[stream], skip)
        return jnp.where(places["first"], fresh, join(held, skip))

    def swaps(block):
        return swap(0, starts, block), swap(1, starts, block)

    mirrored = send(previous, [(j, sections - 1 - j) for j in range(half)])
    p, q = resident
    halos = swaps(q)
    for slot in range(ticks + 1):
        if slot > 1:
            q = arrived(slot, 1)
            halos = swaps(q)
        *kept, w_one = inner_planes(q, w_one, width, slot == 0)
        first = all_planes(flags, *halos, kept, w_one, (p,) if slot < 2 else (), width)
        if slot > 1:
            p = arrived(slot, 0)
            first = (p.astype(jnp.float32) + first).astype(jnp.bfloat16)
        halos = swaps(first)
        *kept, _ = inner_planes(first, w_two, width)
        if slot == 0:
            mirrored, _ = lax.optimization_barrier((mirrored, first))
            following = arrived(1, 0), arrived(1, 1)
            following += (swaps(following[1]),)
        second = all_planes(flags, *halos, kept, w_two, (first, q) if slot == ticks else (q,), width)
        if slot == 0:
            p, q, halos = following
            halos, second = lax.optimization_barrier((halos, second))
        if slot < ticks:
            onward = [(j, j + 1) for j in range(1, sections - 1)] if slot > 0 else []
            if slot < ticks - 1:
                onward = [(0, 1)] + onward
            first, second = lax.optimization_barrier((first, second))
            received, relays = {1: send(second, onward), 0: send(first, onward)}, {}
            if slot > 0:
                held, _ = lax.optimization_barrier((newer, second))
                relays = {k: send(held[k], [(1, sections - 1)]) for k in (1, 0)}
                if across:
                    direct = {0: send(first, across), 1: send(second, across)}
            older, newer, relayed = newer, received, relays
    result = second
    return result.reshape(1, 2, planes, rows, width, chans)


def solution(mesh):
    in_specs = (
        P("section", None, "depth", None, None, None),
        P("section", None, "depth", None, None, None),
        P(None, None, "depth", None, None, None),
        P("section", None, None, None, None, None),
        P("section", None, None, None, None, None),
    )
    out_specs = P("section", None, "depth", None, None, None)
    return jax.shard_map(local, mesh=mesh, in_specs=in_specs, out_specs=out_specs, check_vma=False)
```

```python
import functools

import jax
import jax.numpy as jnp
from jax import lax
from jax.experimental import pallas as pl
from jax.experimental.pallas import tpu as pltpu
from jax.sharding import PartitionSpec as P

EPS = 1e-05
VMEM_LIMIT = 12 * 1024 * 1024


def act(values):
    values = values.astype(jnp.float32)
    scaled = values * lax.rsqrt(jnp.mean(values * values, axis=-1, keepdims=True) + EPS)
    return scaled * (0.5 + 0.5 * jnp.tanh(0.5 * scaled))


def fill(even, odd, at, values, width):
    planes, _, chans = values.shape
    field = act(values)
    edge = jnp.zeros((planes, width, chans), jnp.float32)
    even[pl.ds(at, planes)] = field.astype(jnp.bfloat16)
    odd[pl.ds(at, planes)] = jnp.concatenate([edge, field, edge], axis=1).astype(jnp.bfloat16)


def convolve(taps, weights, width):
    planes, voxels, chans = taps[0].shape
    slab = jnp.concatenate([part.reshape(planes * voxels, chans) for part in taps], axis=-1)
    total = None
    for k in (1, 0, 2):
        columns = jnp.concatenate([weights[(3 * n + k) * chans : (3 * n + k + 1) * chans] for n in range(9)], axis=0)
        part = jnp.dot(slab, columns, preferred_element_type=jnp.float32).reshape(-1, width, chans)
        column = lax.broadcasted_iota(jnp.int32, part.shape, 1)
        if k == 0:
            part = jnp.where(column == 0, 0.0, pltpu.roll(part, 1, 1))
        elif k == 2:
            part = jnp.where(column == width - 1, 0.0, pltpu.roll(part, width - 1, 1))
        total = part if total is None else total + part
    return total.reshape(planes, voxels, chans)


def planes_at(even, odd, start, count, width):
    voxels = even.shape[1]
    return [
        even[start : start + count] if j == 1 else odd[start : start + count, j * width : j * width + voxels]
        for j in range(3)
    ]


def inner_kernel(width, field, weights, even, odd, total):
    planes = field.shape[0]
    fill(even, odd, 0, field[...], width)
    taps = [part for i in range(3) for part in planes_at(even, odd, i, planes - 2, width)]
    total[...] = convolve(taps, weights, width)


def loading_kernel(width, field, weights_hbm, even, odd, total, weights, sem):
    copy = pltpu.make_async_copy(weights_hbm, weights, sem)
    copy.start()
    planes = field.shape[0]
    fill(even, odd, 0, field[...], width)
    taps = [part for i in range(3) for part in planes_at(even, odd, i, planes - 2, width)]
    copy.wait()
    total[...] = convolve(taps, weights, width)


def edge_kernel(width, flags, near, far, even, odd, inner, weights, *rest):
    *added, out, edge_even, edge_odd = rest
    planes = even.shape[0]
    above = flags[0] > 0
    near, far = near[...].astype(jnp.float32), far[...].astype(jnp.float32)
    fill(edge_even, edge_odd, 0, jnp.where(above, far, near), width)
    fill(edge_even, edge_odd, 1, jnp.where(above, near, far), width)
    halo = lambda plane: planes_at(edge_even, edge_odd, plane, 1, width)
    own = lambda plane: planes_at(even, odd, plane, 1, width)
    sources = ((halo(0), own(planes - 2)), (own(0), own(planes - 1)), (own(1), halo(1)))
    taps = [jnp.concatenate(pair, axis=0) for source in sources for pair in zip(*source)]
    total = convolve(taps, weights, width)
    pieces = ((0, 1, total[:1]), (1, planes - 2, inner[...]), (planes - 1, 1, total[1:]))
    for start, count, piece in pieces:
        where = pl.ds(start, count)
        if added:
            piece = added[-1][where].astype(jnp.float32) + piece
        if len(added) == 2:
            out[0, where] = added[0][where]
            out[1, where] = piece.astype(out.dtype)
        else:
            out[where] = piece.astype(out.dtype)


def call(kernel, outputs, scratch, arguments, width):
    specs = [pl.BlockSpec(memory_space=pltpu.VMEM) for _ in arguments]
    if kernel is edge_kernel:
        specs[0] = pl.BlockSpec(memory_space=pltpu.SMEM)
    if kernel is loading_kernel:
        specs[-1] = pl.BlockSpec(memory_space=pltpu.HBM)
    return pl.pallas_call(
        functools.partial(kernel, width),
        out_shape=[jax.ShapeDtypeStruct(shape, dtype) for shape, dtype in outputs],
        in_specs=specs,
        out_specs=[pl.BlockSpec(memory_space=pltpu.VMEM) for _ in outputs],
        scratch_shapes=[pltpu.VMEM(shape, jnp.bfloat16) if shape else pltpu.SemaphoreType.DMA for shape in scratch],
        compiler_params=pltpu.CompilerParams(vmem_limit_bytes=VMEM_LIMIT),
        cost_estimate=pl.CostEstimate(flops=1, bytes_accessed=1, transcendentals=0),
    )(*arguments)


def stored(planes, voxels, chans, width):
    return (planes, voxels, chans), (planes, voxels + 2 * width, chans)


def inner_planes(field, weights, width, load=False):
    planes, voxels, chans = field.shape
    outputs = [(shape, jnp.bfloat16) for shape in stored(planes, voxels, chans, width)]
    outputs.append(((planes - 2, voxels, chans), jnp.float32))
    if load:
        weights = pltpu.with_memory_space_constraint(weights, pltpu.HBM)
        outputs.append((weights.shape, jnp.bfloat16))
        return call(loading_kernel, outputs, [()], (field, weights), width)
    return *call(inner_kernel, outputs, [], (field, weights), width), weights


def all_planes(flags, near, far, kept, weights, added, width):
    shape = kept[0].shape
    _, voxels, chans = shape
    output = ((2, *shape) if len(added) == 2 else shape, jnp.bfloat16 if added else jnp.float32)
    arguments = (flags, near, far, *kept, weights, *added)
    (out,) = call(edge_kernel, [output], stored(2, voxels, chans, width), arguments, width)
    return out


def swap(turn, starts, block):
    count = lax.axis_size("depth")
    pairs = [pair for i in range(turn, count - 1, 2) for pair in ((i, i + 1), (i + 1, i))]
    return lax.ppermute(lax.dynamic_slice_in_dim(block, starts[turn], 1, axis=0), "depth", pairs)


def local(resident, previous, incoming, first_weights, second_weights):
    section = lax.axis_index("section")
    sections = lax.axis_size("section")
    half = sections // 2
    depth = lax.axis_index("depth")
    ticks = incoming.shape[0] + 1
    _, _, planes, rows, width, chans = resident.shape
    voxels = rows * width
    across = [(j, sections - 1 - j) for j in range(1, half - 1)]

    above = depth % 2 == 0
    places = {
        "flags": jnp.stack([above]).astype(jnp.int32),
        "starts": (jnp.where(above, planes - 1, 0), jnp.where(above, 0, planes - 1)),
        "first": section == 0,
        "second": section == 1,
        "last": section == sections - 1,
        "decoder": section >= half,
        "direct": (section > half) & (section < sections - 1) if across else (),
    }
    places, resident, previous, incoming, first_weights, second_weights = lax.optimization_barrier(
        (places, resident, previous, incoming, first_weights, second_weights)
    )
    flags, starts = places["flags"], places["starts"]

    flat = lambda a: a.reshape(a.shape[0], 2, planes, voxels, chans)
    resident, previous, incoming = flat(resident)[0], flat(previous)[0], flat(incoming)
    w_one = first_weights.reshape(27 * chans, chans)
    w_two = second_weights.reshape(27 * chans, chans)

    def send(block, pairs):
        return lax.ppermute(block, "section", pairs) if pairs else block

    def relay(block):
        groups = [[0, half]] + [[j, sections - j] for j in range(1, half)]
        return lax.all_gather(block, "section", axis_index_groups=groups)[0]

    def join(held, skip):
        total = (held.astype(jnp.float32) + skip.astype(jnp.float32)).astype(jnp.bfloat16)
        return jnp.where(places["decoder"], total, held)

    newer, older, relayed, direct = {}, {}, {}, {}

    def arrived(slot, stream):
        fresh = incoming[min(slot, ticks - 1) - 1, stream]
        if slot == 1:
            return jnp.where(places["first"], fresh, join(resident[stream], mirrored[stream]))
        held = jnp.where(places["second"], older[stream], newer[stream])
        skip = jnp.where(places["last"], relayed[stream], newer[stream])
        if across:
            skip = jnp.where(places["direct"], direct[stream], skip)
        return jnp.where(places["first"], fresh, join(held, skip))

    def swaps(block):
        return swap(0, starts, block), swap(1, starts, block)

    mirrored = send(previous, [(j, sections - 1 - j) for j in range(half)])
    p, q = resident
    halos = swaps(q)
    for slot in range(ticks + 1):
        if slot > 1:
            q = arrived(slot, 1)
            halos = swaps(q)
        *kept, w_one = inner_planes(q, w_one, width, slot == 0)
        first = all_planes(flags, *halos, kept, w_one, (p,) if slot < 2 else (), width)
        if slot > 1:
            p = arrived(slot, 0)
            first = (p.astype(jnp.float32) + first).astype(jnp.bfloat16)
        halos = swaps(first)
        *kept, _ = inner_planes(first, w_two, width)
        if slot == 0:
            mirrored, _ = lax.optimization_barrier((mirrored, first))
            following = arrived(1, 0), arrived(1, 1)
            following += (swaps(following[1]),)
        second = all_planes(flags, *halos, kept, w_two, (first, q) if slot == ticks else (q,), width)
        if slot == 0:
            p, q, halos = following
            halos, second = lax.optimization_barrier((halos, second))
        if slot < ticks:
            onward = [(j, j + 1) for j in range(1, sections - 1)] if slot > 0 else []
            if slot < ticks - 1:
                onward = [(0, 1)] + onward
            received, relays = {}, {k: relay(newer[k]) for k in newer}
            first, second = lax.optimization_barrier((first, second))
            received[1] = send(second, onward)
            received[0] = send(first, onward)
            if slot > 0:
                if across:
                    direct = {0: send(first, across), 1: send(second, across)}
            older, newer, relayed = newer, received, relays
    result = second
    return result.reshape(1, 2, planes, rows, width, chans)


def solution(mesh):
    in_specs = (
        P("section", None, "depth", None, None, None),
        P("section", None, "depth", None, None, None),
        P(None, None, "depth", None, None, None),
        P("section", None, None, None, None, None),
        P("section", None, None, None, None, None),
    )
    out_specs = P("section", None, "depth", None, None, None)
    return jax.shard_map(local, mesh=mesh, in_specs=in_specs, out_specs=out_specs, check_vma=False)
```

```python
import functools

import jax
import jax.numpy as jnp
from jax import lax
from jax.experimental import pallas as pl
from jax.experimental.pallas import tpu as pltpu
from jax.sharding import PartitionSpec as P

EPS = 1e-05
VMEM_LIMIT = 12 * 1024 * 1024


def act(values):
    values = values.astype(jnp.float32)
    scaled = values * lax.rsqrt(jnp.mean(values * values, axis=-1, keepdims=True) + EPS)
    return scaled * (0.5 + 0.5 * jnp.tanh(0.5 * scaled))


def fill(even, odd, at, values, width):
    planes, _, chans = values.shape
    field = act(values)
    edge = jnp.zeros((planes, width, chans), jnp.float32)
    even[pl.ds(at, planes)] = field.astype(jnp.bfloat16)
    odd[pl.ds(at, planes)] = jnp.concatenate([edge, field, edge], axis=1).astype(jnp.bfloat16)


def convolve(taps, weights, width):
    planes, voxels, chans = taps[0].shape
    slab = jnp.concatenate([part.reshape(planes * voxels, chans) for part in taps], axis=-1)
    total = None
    for k in (1, 0, 2):
        columns = jnp.concatenate([weights[(3 * n + k) * chans : (3 * n + k + 1) * chans] for n in range(9)], axis=0)
        part = jnp.dot(slab, columns, preferred_element_type=jnp.float32).reshape(-1, width, chans)
        column = lax.broadcasted_iota(jnp.int32, part.shape, 1)
        if k == 0:
            part = jnp.where(column == 0, 0.0, pltpu.roll(part, 1, 1))
        elif k == 2:
            part = jnp.where(column == width - 1, 0.0, pltpu.roll(part, width - 1, 1))
        total = part if total is None else total + part
    return total.reshape(planes, voxels, chans)


def planes_at(even, odd, start, count, width):
    voxels = even.shape[1]
    return [
        even[start : start + count] if j == 1 else odd[start : start + count, j * width : j * width + voxels]
        for j in range(3)
    ]


def inner_kernel(width, field, weights, even, odd, total):
    planes = field.shape[0]
    fill(even, odd, 0, field[...], width)
    taps = [part for i in range(3) for part in planes_at(even, odd, i, planes - 2, width)]
    total[...] = convolve(taps, weights, width)


def loading_kernel(width, field, weights_hbm, even, odd, total, weights, sem):
    copy = pltpu.make_async_copy(weights_hbm, weights, sem)
    copy.start()
    planes = field.shape[0]
    fill(even, odd, 0, field[...], width)
    taps = [part for i in range(3) for part in planes_at(even, odd, i, planes - 2, width)]
    copy.wait()
    total[...] = convolve(taps, weights, width)


def edge_kernel(width, flags, near, far, even, odd, inner, weights, *rest):
    *added, out, edge_even, edge_odd = rest
    planes = even.shape[0]
    above = flags[0] > 0
    near, far = near[...].astype(jnp.float32), far[...].astype(jnp.float32)
    fill(edge_even, edge_odd, 0, jnp.where(above, far, near), width)
    fill(edge_even, edge_odd, 1, jnp.where(above, near, far), width)
    halo = lambda plane: planes_at(edge_even, edge_odd, plane, 1, width)
    own = lambda plane: planes_at(even, odd, plane, 1, width)
    sources = ((halo(0), own(planes - 2)), (own(0), own(planes - 1)), (own(1), halo(1)))
    taps = [jnp.concatenate(pair, axis=0) for source in sources for pair in zip(*source)]
    total = convolve(taps, weights, width)
    pieces = ((0, 1, total[:1]), (1, planes - 2, inner[...]), (planes - 1, 1, total[1:]))
    for start, count, piece in pieces:
        where = pl.ds(start, count)
        if added:
            piece = added[-1][where].astype(jnp.float32) + piece
        if len(added) == 2:
            out[0, where] = added[0][where]
            out[1, where] = piece.astype(out.dtype)
        else:
            out[where] = piece.astype(out.dtype)


def call(kernel, outputs, scratch, arguments, width):
    specs = [pl.BlockSpec(memory_space=pltpu.VMEM) for _ in arguments]
    if kernel is edge_kernel:
        specs[0] = pl.BlockSpec(memory_space=pltpu.SMEM)
    if kernel is loading_kernel:
        specs[-1] = pl.BlockSpec(memory_space=pltpu.HBM)
    return pl.pallas_call(
        functools.partial(kernel, width),
        out_shape=[jax.ShapeDtypeStruct(shape, dtype) for shape, dtype in outputs],
        in_specs=specs,
        out_specs=[pl.BlockSpec(memory_space=pltpu.VMEM) for _ in outputs],
        scratch_shapes=[pltpu.VMEM(shape, jnp.bfloat16) if shape else pltpu.SemaphoreType.DMA for shape in scratch],
        compiler_params=pltpu.CompilerParams(vmem_limit_bytes=VMEM_LIMIT),
        cost_estimate=pl.CostEstimate(flops=1, bytes_accessed=1, transcendentals=0),
    )(*arguments)


def stored(planes, voxels, chans, width):
    return (planes, voxels, chans), (planes, voxels + 2 * width, chans)


def inner_planes(field, weights, width, load=False):
    planes, voxels, chans = field.shape
    outputs = [(shape, jnp.bfloat16) for shape in stored(planes, voxels, chans, width)]
    outputs.append(((planes - 2, voxels, chans), jnp.float32))
    if load:
        weights = pltpu.with_memory_space_constraint(weights, pltpu.HBM)
        outputs.append((weights.shape, jnp.bfloat16))
        return call(loading_kernel, outputs, [()], (field, weights), width)
    return *call(inner_kernel, outputs, [], (field, weights), width), weights


def all_planes(flags, near, far, kept, weights, added, width):
    shape = kept[0].shape
    _, voxels, chans = shape
    output = ((2, *shape) if len(added) == 2 else shape, jnp.bfloat16 if added else jnp.float32)
    arguments = (flags, near, far, *kept, weights, *added)
    (out,) = call(edge_kernel, [output], stored(2, voxels, chans, width), arguments, width)
    return out


def swap(turn, starts, block):
    count = lax.axis_size("depth")
    pairs = [pair for i in range(turn, count - 1, 2) for pair in ((i, i + 1), (i + 1, i))]
    return lax.ppermute(lax.dynamic_slice_in_dim(block, starts[turn], 1, axis=0), "depth", pairs)


def local(resident, previous, incoming, first_weights, second_weights):
    section = lax.axis_index("section")
    sections = lax.axis_size("section")
    half = sections // 2
    depth = lax.axis_index("depth")
    ticks = incoming.shape[0] + 1
    _, _, planes, rows, width, chans = resident.shape
    voxels = rows * width
    across = [(j, sections - 1 - j) for j in range(1, half - 1)]

    above = depth % 2 == 0
    places = {
        "flags": jnp.stack([above]).astype(jnp.int32),
        "starts": (jnp.where(above, planes - 1, 0), jnp.where(above, 0, planes - 1)),
        "first": section == 0,
        "second": section == 1,
        "before": section == sections - 2,
        "decoder": section >= half,
        "joins": (section >= half) & (section < sections - 1),
        "direct": (section > half) & (section < sections - 1) if across else (),
    }
    places, resident, previous, incoming, first_weights, second_weights = lax.optimization_barrier(
        (places, resident, previous, incoming, first_weights, second_weights)
    )
    flags, starts = places["flags"], places["starts"]

    flat = lambda a: a.reshape(a.shape[0], 2, planes, voxels, chans)
    resident, previous, incoming = flat(resident)[0], flat(previous)[0], flat(incoming)
    w_one = first_weights.reshape(27 * chans, chans)
    w_two = second_weights.reshape(27 * chans, chans)

    def send(block, pairs):
        return lax.ppermute(block, "section", pairs) if pairs else block

    def added(block, other):
        return (block.astype(jnp.float32) + other.astype(jnp.float32)).astype(jnp.bfloat16)

    newer, older, direct = {}, {}, {}

    def arrived(slot, stream):
        fresh = incoming[min(slot, ticks - 1) - 1, stream]
        if slot == 1:
            held = jnp.where(places["decoder"], added(resident[stream], mirrored[stream]), resident[stream])
        else:
            held = jnp.where(places["second"], older[stream], newer[stream])
            skip = jnp.where(places["direct"], direct[stream], newer[stream]) if across else newer[stream]
            held = jnp.where(places["joins"], added(held, skip), held)
        return jnp.where(places["first"], fresh, held)

    def swaps(block):
        return swap(0, starts, block), swap(1, starts, block)

    mirrored = send(previous, [(j, sections - 1 - j) for j in range(half)])
    p, q = resident
    halos = swaps(q)
    for slot in range(ticks + 1):
        if slot > 1:
            q = arrived(slot, 1)
            halos = swaps(q)
        *kept, w_one = inner_planes(q, w_one, width, slot == 0)
        first = all_planes(flags, *halos, kept, w_one, (p,) if slot < 2 else (), width)
        if slot > 1:
            p = arrived(slot, 0)
            first = (p.astype(jnp.float32) + first).astype(jnp.bfloat16)
        halos = swaps(first)
        *kept, _ = inner_planes(first, w_two, width)
        if slot == 0:
            mirrored, _ = lax.optimization_barrier((mirrored, first))
            following = arrived(1, 0), arrived(1, 1)
            following += (swaps(following[1]),)
        second = all_planes(flags, *halos, kept, w_two, (first, q) if slot == ticks else (q,), width)
        if slot == 0:
            p, q, halos = following
            halos, second = lax.optimization_barrier((halos, second))
        if slot == 0:
            whole = jnp.stack([first, second])
            newer = {1: send(second, [(0, 1)]), 0: send(first, [(0, 1)])}
        elif slot < ticks:
            onward = [(j, j + 1) for j in range(1, sections - 1)]
            if slot < ticks - 1:
                onward = [(0, 1)] + onward
            if slot == 1:
                newer[1], second = lax.optimization_barrier((newer[1], second))
            early, second = lax.optimization_barrier((early, second))
            sent_q = jnp.where(places["before"], added(second, early[1]), second)
            early, first, sent_q = lax.optimization_barrier((early, first, sent_q))
            sent_p = jnp.where(places["before"], added(first, early[0]), first)
            older, newer = newer, {1: send(sent_q, onward), 0: send(sent_p, onward)}
            whole = jnp.stack([sent_p, sent_q])
            if across:
                direct = {0: send(first, across), 1: send(second, across)}
        if slot < ticks - 1:
            early = send(whole, [(0, sections - 2)])
    result = second
    return result.reshape(1, 2, planes, rows, width, chans)


def solution(mesh):
    in_specs = (
        P("section", None, "depth", None, None, None),
        P("section", None, "depth", None, None, None),
        P(None, None, "depth", None, None, None),
        P("section", None, None, None, None, None),
        P("section", None, None, None, None, None),
    )
    out_specs = P("section", None, "depth", None, None, None)
    return jax.shard_map(local, mesh=mesh, in_specs=in_specs, out_specs=out_specs, check_vma=False)
```

```python
import functools

import jax
import jax.numpy as jnp
from jax import lax
from jax.experimental import pallas as pl
from jax.experimental.pallas import tpu as pltpu
from jax.sharding import PartitionSpec as P

EPS = 1e-05
VMEM_LIMIT = 12 * 1024 * 1024


def act(values):
    values = values.astype(jnp.float32)
    scaled = values * lax.rsqrt(jnp.mean(values * values, axis=-1, keepdims=True) + EPS)
    return scaled * (0.5 + 0.5 * jnp.tanh(0.5 * scaled))


def fill(even, odd, at, values, width):
    planes, _, chans = values.shape
    field = act(values)
    edge = jnp.zeros((planes, width, chans), jnp.float32)
    even[pl.ds(at, planes)] = field.astype(jnp.bfloat16)
    odd[pl.ds(at, planes)] = jnp.concatenate([edge, field, edge], axis=1).astype(jnp.bfloat16)


def convolve(taps, weights, width):
    planes, voxels, chans = taps[0].shape
    slab = jnp.concatenate([part.reshape(planes * voxels, chans) for part in taps], axis=-1)
    total = None
    for k in (1, 0, 2):
        columns = jnp.concatenate([weights[(3 * n + k) * chans : (3 * n + k + 1) * chans] for n in range(9)], axis=0)
        part = jnp.dot(slab, columns, preferred_element_type=jnp.float32).reshape(-1, width, chans)
        column = lax.broadcasted_iota(jnp.int32, part.shape, 1)
        if k == 0:
            part = jnp.where(column == 0, 0.0, pltpu.roll(part, 1, 1))
        elif k == 2:
            part = jnp.where(column == width - 1, 0.0, pltpu.roll(part, width - 1, 1))
        total = part if total is None else total + part
    return total.reshape(planes, voxels, chans)


def planes_at(even, odd, start, count, width):
    voxels = even.shape[1]
    return [
        even[start : start + count] if j == 1 else odd[start : start + count, j * width : j * width + voxels]
        for j in range(3)
    ]


def inner_kernel(width, field, weights, even, odd, total):
    planes = field.shape[0]
    fill(even, odd, 0, field[...], width)
    taps = [part for i in range(3) for part in planes_at(even, odd, i, planes - 2, width)]
    total[...] = convolve(taps, weights, width)


def loading_kernel(width, field, weights_hbm, even, odd, total, weights, sem):
    copy = pltpu.make_async_copy(weights_hbm, weights, sem)
    copy.start()
    planes = field.shape[0]
    fill(even, odd, 0, field[...], width)
    taps = [part for i in range(3) for part in planes_at(even, odd, i, planes - 2, width)]
    copy.wait()
    total[...] = convolve(taps, weights, width)


def edge_kernel(width, flags, near, far, even, odd, inner, weights, *rest):
    *added, out, edge_even, edge_odd = rest
    planes = even.shape[0]
    above = flags[0] > 0
    near, far = near[...].astype(jnp.float32), far[...].astype(jnp.float32)
    fill(edge_even, edge_odd, 0, jnp.where(above, far, near), width)
    fill(edge_even, edge_odd, 1, jnp.where(above, near, far), width)
    halo = lambda plane: planes_at(edge_even, edge_odd, plane, 1, width)
    own = lambda plane: planes_at(even, odd, plane, 1, width)
    sources = ((halo(0), own(planes - 2)), (own(0), own(planes - 1)), (own(1), halo(1)))
    taps = [jnp.concatenate(pair, axis=0) for source in sources for pair in zip(*source)]
    total = convolve(taps, weights, width)
    pieces = ((0, 1, total[:1]), (1, planes - 2, inner[...]), (planes - 1, 1, total[1:]))
    for start, count, piece in pieces:
        where = pl.ds(start, count)
        if added:
            piece = added[-1][where].astype(jnp.float32) + piece
        if len(added) == 2:
            out[0, where] = added[0][where]
            out[1, where] = piece.astype(out.dtype)
        else:
            out[where] = piece.astype(out.dtype)


def call(kernel, outputs, scratch, arguments, width):
    specs = [pl.BlockSpec(memory_space=pltpu.VMEM) for _ in arguments]
    if kernel is edge_kernel:
        specs[0] = pl.BlockSpec(memory_space=pltpu.SMEM)
    if kernel is loading_kernel:
        specs[-1] = pl.BlockSpec(memory_space=pltpu.HBM)
    return pl.pallas_call(
        functools.partial(kernel, width),
        out_shape=[jax.ShapeDtypeStruct(shape, dtype) for shape, dtype in outputs],
        in_specs=specs,
        out_specs=[pl.BlockSpec(memory_space=pltpu.VMEM) for _ in outputs],
        scratch_shapes=[pltpu.VMEM(shape, jnp.bfloat16) if shape else pltpu.SemaphoreType.DMA for shape in scratch],
        compiler_params=pltpu.CompilerParams(vmem_limit_bytes=VMEM_LIMIT),
        cost_estimate=pl.CostEstimate(flops=1, bytes_accessed=1, transcendentals=0),
    )(*arguments)


def stored(planes, voxels, chans, width):
    return (planes, voxels, chans), (planes, voxels + 2 * width, chans)


def inner_planes(field, weights, width, load=False):
    planes, voxels, chans = field.shape
    outputs = [(shape, jnp.bfloat16) for shape in stored(planes, voxels, chans, width)]
    outputs.append(((planes - 2, voxels, chans), jnp.float32))
    if load:
        weights = pltpu.with_memory_space_constraint(weights, pltpu.HBM)
        outputs.append((weights.shape, jnp.bfloat16))
        return call(loading_kernel, outputs, [()], (field, weights), width)
    return *call(inner_kernel, outputs, [], (field, weights), width), weights


def all_planes(flags, near, far, kept, weights, added, width):
    shape = kept[0].shape
    _, voxels, chans = shape
    output = ((2, *shape) if len(added) == 2 else shape, jnp.bfloat16 if added else jnp.float32)
    arguments = (flags, near, far, *kept, weights, *added)
    (out,) = call(edge_kernel, [output], stored(2, voxels, chans, width), arguments, width)
    return out


def swap(turn, starts, block):
    count = lax.axis_size("depth")
    pairs = [pair for i in range(turn, count - 1, 2) for pair in ((i, i + 1), (i + 1, i))]
    return lax.ppermute(lax.dynamic_slice_in_dim(block, starts[turn], 1, axis=0), "depth", pairs)


def local(resident, previous, incoming, first_weights, second_weights):
    section = lax.axis_index("section")
    sections = lax.axis_size("section")
    half = sections // 2
    depth = lax.axis_index("depth")
    ticks = incoming.shape[0] + 1
    _, _, planes, rows, width, chans = resident.shape
    voxels = rows * width
    across = [(j, sections - 1 - j) for j in range(1, half - 1)]

    above = depth % 2 == 0
    places = {
        "flags": jnp.stack([above]).astype(jnp.int32),
        "starts": (jnp.where(above, planes - 1, 0), jnp.where(above, 0, planes - 1)),
        "first": section == 0,
        "second": section == 1,
        "last": section == sections - 1,
        "decoder": section >= half,
        "direct": (section > half) & (section < sections - 1) if across else (),
    }
    places, resident, previous, incoming, first_weights, second_weights = lax.optimization_barrier(
        (places, resident, previous, incoming, first_weights, second_weights)
    )
    flags, starts = places["flags"], places["starts"]

    flat = lambda a: a.reshape(a.shape[0], 2, planes, voxels, chans)
    resident, previous, incoming = flat(resident)[0], flat(previous)[0], flat(incoming)
    w_one = first_weights.reshape(27 * chans, chans)
    w_two = second_weights.reshape(27 * chans, chans)

    def send(block, pairs):
        return lax.ppermute(block, "section", pairs) if pairs else block

    def join(held, skip):
        total = (held.astype(jnp.float32) + skip.astype(jnp.float32)).astype(jnp.bfloat16)
        return jnp.where(places["decoder"], total, held)

    newer, older, relayed, direct = {}, {}, {}, {}

    def arrived(slot, stream):
        fresh = incoming[min(slot, ticks - 1) - 1, stream]
        if slot == 1:
            return jnp.where(places["first"], fresh, join(resident[stream], mirrored[stream]))
        held = jnp.where(places["second"], older[stream], newer[stream])
        skip = jnp.where(places["last"], relayed[stream], newer[stream])
        if across:
            skip = jnp.where(places["direct"], direct[stream], skip)
        return jnp.where(places["first"], fresh, join(held, skip))

    def swaps(block):
        return swap(0, starts, block), swap(1, starts, block)

    mirrored = send(previous, [(j, sections - 1 - j) for j in range(half)])
    p, q = resident
    halos = swaps(q)
    for slot in range(ticks + 1):
        if slot > 1:
            if slot > 2:
                newer[1], relayed[0] = lax.optimization_barrier((newer[1], relayed[0]))
            q = arrived(slot, 1)
            halos = swaps(q)
        *kept, w_one = inner_planes(q, w_one, width, slot == 0)
        first = all_planes(flags, *halos, kept, w_one, (p,) if slot < 2 else (), width)
        if slot > 1:
            p = arrived(slot, 0)
            first = (p.astype(jnp.float32) + first).astype(jnp.bfloat16)
        halos = swaps(first)
        *kept, _ = inner_planes(first, w_two, width)
        if slot == 0:
            mirrored, _ = lax.optimization_barrier((mirrored, first))
            following = arrived(1, 0), arrived(1, 1)
            following += (swaps(following[1]),)
        second = all_planes(flags, *halos, kept, w_two, (first, q) if slot == ticks else (q,), width)
        if slot == 0:
            p, q, halos = following
            halos, second = lax.optimization_barrier((halos, second))
        if slot < ticks:
            onward = [(j, j + 1) for j in range(1, sections - 1)] if slot > 0 else []
            if slot < ticks - 1:
                onward = [(0, 1)] + onward
            relays = {}
            if slot > 0:
                held = newer
                if slot == 1:
                    held, _ = lax.optimization_barrier((held, second))
                relays = {k: send(held[k], [(1, sections - 1)]) for k in (1, 0)}
                if slot > 1:
                    relays[1], second = lax.optimization_barrier((relays[1], second))
            first, second = lax.optimization_barrier((first, second))
            received = {1: send(second, onward), 0: send(first, onward)}
            if slot > 0:
                if across:
                    direct = {0: send(first, across), 1: send(second, across)}
            older, newer, relayed = newer, received, relays
    result = second
    return result.reshape(1, 2, planes, rows, width, chans)


def solution(mesh):
    in_specs = (
        P("section", None, "depth", None, None, None),
        P("section", None, "depth", None, None, None),
        P(None, None, "depth", None, None, None),
        P("section", None, None, None, None, None),
        P("section", None, None, None, None, None),
    )
    out_specs = P("section", None, "depth", None, None, None)
    return jax.shard_map(local, mesh=mesh, in_specs=in_specs, out_specs=out_specs, check_vma=False)
```

```python
import functools

import jax
import jax.numpy as jnp
from jax import lax
from jax.experimental import pallas as pl
from jax.experimental.pallas import tpu as pltpu
from jax.sharding import PartitionSpec as P

EPS = 1e-05
VMEM_LIMIT = 12 * 1024 * 1024


def act(values):
    values = values.astype(jnp.float32)
    scaled = values * lax.rsqrt(jnp.mean(values * values, axis=-1, keepdims=True) + EPS)
    return scaled * (0.5 + 0.5 * jnp.tanh(0.5 * scaled))


def fill(even, odd, at, values, width):
    planes, _, chans = values.shape
    field = act(values)
    edge = jnp.zeros((planes, width, chans), jnp.float32)
    even[pl.ds(at, planes)] = field.astype(jnp.bfloat16)
    odd[pl.ds(at, planes)] = jnp.concatenate([edge, field, edge], axis=1).astype(jnp.bfloat16)


def shifted(part, k, width):
    planes, voxels, chans = part.shape
    part = part.reshape(-1, width, chans)
    column = lax.broadcasted_iota(jnp.int32, part.shape, 1)
    if k == 0:
        part = jnp.where(column == 0, 0.0, pltpu.roll(part, 1, 1))
    elif k == 2:
        part = jnp.where(column == width - 1, 0.0, pltpu.roll(part, width - 1, 1))
    return part.reshape(planes, voxels, chans)


def product(taps, weights, offsets, k):
    planes, voxels, chans = taps[0].shape
    slab = jnp.concatenate([part.reshape(planes * voxels, chans) for part in taps], axis=-1)
    columns = jnp.concatenate([weights[(3 * n + k) * chans : (3 * n + k + 1) * chans] for n in offsets], axis=0)
    part = jnp.dot(slab, columns, preferred_element_type=jnp.float32)
    return part.reshape(planes, voxels, chans)


def convolve(taps, weights, width):
    return sum(shifted(product(taps, weights, range(9), k), k, width) for k in (1, 0, 2))


def edges(sources, targets, weights, width):
    total = None
    for k in (1, 0, 2):
        sums = [None] * 4
        for i in range(3):
            part = product(sources[i], weights, range(3 * i, 3 * i + 3), k)
            for plane, target in enumerate(targets[i]):
                piece = part[plane : plane + 1]
                sums[target] = piece if sums[target] is None else sums[target] + piece
        part = shifted(jnp.concatenate(sums, axis=0), k, width)
        total = part if total is None else total + part
    return total


def planes_at(even, odd, start, count, width):
    voxels = even.shape[1]
    return [
        even[start : start + count] if j == 1 else odd[start : start + count, j * width : j * width + voxels]
        for j in range(3)
    ]


def own_planes(width, p, q, weights, inner, partial, even, odd, ready=None):
    planes = q.shape[0]
    fill(even, odd, 0, q[...], width)
    if ready is not None:
        ready.wait()
    taps = [part for i in range(3) for part in planes_at(even, odd, i, planes - 2, width)]
    inner[...] = (p[1:-1].astype(jnp.float32) + convolve(taps, weights, width)).astype(inner.dtype)
    own = lambda plane: planes_at(even, odd, plane, 1, width)
    pair = lambda one, other: [jnp.concatenate(both, axis=0) for both in zip(own(one), own(other))]
    sources = (pair(planes - 2, planes - 1), pair(0, planes - 1), pair(0, 1))
    partial[...] = edges(sources, ((2, 3), (1, 2), (0, 1)), weights, width)


def inner_kernel(width, p, q, weights, inner, partial, even, odd):
    own_planes(width, p, q, weights, inner, partial, even, odd)


def loading_kernel(width, p, q, weights_hbm, inner, partial, weights, even, odd, sem):
    copy = pltpu.make_async_copy(weights_hbm, weights, sem)
    copy.start()
    own_planes(width, p, q, weights, inner, partial, even, odd, copy)


def edge_kernel(width, flags, p, inner, partial, q_near, q_far, p_near, p_far, weights, low, mid, high, even, odd):
    planes = p.shape[0]
    above = flags[2] > 0
    near, far = q_near[:2].astype(jnp.float32), q_far[:2].astype(jnp.float32)
    fill(even, odd, 0, jnp.where(above, far, near), width)
    fill(even, odd, 2, jnp.where(above, near, far), width)
    sources = [planes_at(even, odd, start, 2, width) for start in range(3)]
    total = partial[...] + edges(sources, ((0, 1), (0, 3), (2, 3)), weights, width)
    near, far = p_near[-1:].astype(jnp.float32), p_far[-1:].astype(jnp.float32)
    low[...] = jnp.where(flags[0] > 0, jnp.where(above, far, near) + total[:1], 0.0).astype(low.dtype)
    mid[pl.ds(0, 1)] = (p[:1].astype(jnp.float32) + total[1:2]).astype(mid.dtype)
    mid[pl.ds(1, planes - 2)] = inner[...]
    mid[pl.ds(planes - 1, 1)] = (p[-1:].astype(jnp.float32) + total[2:3]).astype(mid.dtype)
    high[...] = jnp.where(flags[1] > 0, jnp.where(above, near, far) + total[3:], 0.0).astype(high.dtype)


def second_kernel(width, first_low, first_mid, first_high, q, weights, out, even, odd):
    planes = q.shape[0]
    fill(even, odd, 0, first_low[...], width)
    fill(even, odd, 1, first_mid[...], width)
    fill(even, odd, 1 + planes, first_high[...], width)
    taps = [part for i in range(3) for part in planes_at(even, odd, i, planes, width)]
    second = (q[...].astype(jnp.float32) + convolve(taps, weights, width)).astype(out.dtype)
    if len(out.shape) == 4:
        out[0] = first_mid[...]
        out[1] = second
    else:
        out[...] = second


def call(kernel, outputs, scratch, arguments, width):
    specs = [pl.BlockSpec(memory_space=pltpu.VMEM) for _ in arguments]
    if kernel is edge_kernel:
        specs[0] = pl.BlockSpec(memory_space=pltpu.SMEM)
    if kernel is loading_kernel:
        specs[-1] = pl.BlockSpec(memory_space=pltpu.HBM)
    return pl.pallas_call(
        functools.partial(kernel, width),
        out_shape=[jax.ShapeDtypeStruct(shape, dtype) for shape, dtype in outputs],
        in_specs=specs,
        out_specs=[pl.BlockSpec(memory_space=pltpu.VMEM) for _ in outputs],
        scratch_shapes=[pltpu.VMEM(shape, jnp.bfloat16) if shape else pltpu.SemaphoreType.DMA for shape in scratch],
        compiler_params=pltpu.CompilerParams(vmem_limit_bytes=VMEM_LIMIT),
        cost_estimate=pl.CostEstimate(flops=1, bytes_accessed=1, transcendentals=0),
    )(*arguments)


def stored(planes, voxels, chans, width):
    return (planes, voxels, chans), (planes, voxels + 2 * width, chans)


def inner_half(p, q, weights, width, load):
    planes, voxels, chans = q.shape
    outputs = [((planes - 2, voxels, chans), jnp.bfloat16), ((4, voxels, chans), jnp.float32)]
    scratch = stored(planes, voxels, chans, width)
    if load:
        weights = pltpu.with_memory_space_constraint(weights, pltpu.HBM)
        outputs.append((weights.shape, jnp.bfloat16))
        return call(loading_kernel, outputs, [*scratch, ()], (p, q, weights), width)
    return *call(inner_kernel, outputs, scratch, (p, q, weights), width), weights


def first_half(flags, p, kept, q_halos, p_halos, weights, width):
    planes, voxels, chans = p.shape
    return call(
        edge_kernel,
        [((n, voxels, chans), jnp.bfloat16) for n in (1, planes, 1)],
        stored(4, voxels, chans, width),
        (flags, p, *kept, *q_halos, *p_halos, weights),
        width,
    )


def second_half(first, q, weights, width, both):
    planes, voxels, chans = q.shape
    (out,) = call(
        second_kernel,
        [((2, *q.shape) if both else q.shape, jnp.bfloat16)],
        stored(planes + 2, voxels, chans, width),
        (*first, q, weights),
        width,
    )
    return out


def swap(turn, starts, *blocks):
    count = lax.axis_size("depth")
    parts = [lax.dynamic_slice_in_dim(block, starts[n][turn], n, axis=0) for block, n in blocks]
    pairs = [pair for i in range(turn, count - 1, 2) for pair in ((i, i + 1), (i + 1, i))]
    return lax.ppermute(jnp.concatenate(parts, axis=0), "depth", pairs)


def local(resident, previous, incoming, first_weights, second_weights):
    section = lax.axis_index("section")
    sections = lax.axis_size("section")
    half = sections // 2
    depth = lax.axis_index("depth")
    ticks = incoming.shape[0] + 1
    _, _, planes, rows, width, chans = resident.shape
    voxels = rows * width
    across = [(j, sections - 1 - j) for j in range(1, half - 1)]

    above = depth % 2 == 0
    places = {
        "flags": jnp.stack([depth > 0, depth < lax.axis_size("depth") - 1, above]).astype(jnp.int32),
        "starts": {
            n: (jnp.where(above, planes - n, 0), jnp.where(above, 0, planes - n)) for n in (1, 2)
        },
        "first": section == 0,
        "second": section == 1,
        "last": section == sections - 1,
        "decoder": section >= half,
        "direct": (section > half) & (section < sections - 1) if across else (),
    }
    places, resident, previous, incoming, first_weights, second_weights = lax.optimization_barrier(
        (places, resident, previous, incoming, first_weights, second_weights)
    )
    flags, starts = places["flags"], places["starts"]

    flat = lambda a: a.reshape(a.shape[0], 2, planes, voxels, chans)
    resident, previous, incoming = flat(resident)[0], flat(previous)[0], flat(incoming)
    w_one = first_weights.reshape(27 * chans, chans)
    w_two = second_weights.reshape(27 * chans, chans)

    def send(block, pairs):
        return lax.ppermute(block, "section", pairs) if pairs else block

    def join(held, skip):
        total = (held.astype(jnp.float32) + skip.astype(jnp.float32)).astype(jnp.bfloat16)
        return jnp.where(places["decoder"], total, held)

    newer, older, relayed, direct = {}, {}, {}, {}

    def arrived(slot, stream):
        fresh = incoming[min(slot, ticks - 1) - 1, stream]
        if slot == 1:
            return jnp.where(places["first"], fresh, join(resident[stream], mirrored[stream]))
        held = jnp.where(places["second"], older[stream], newer[stream])
        skip = jnp.where(places["last"], relayed[stream], newer[stream])
        if across:
            skip = jnp.where(places["direct"], direct[stream], skip)
        return jnp.where(places["first"], fresh, join(held, skip))

    p, q = resident
    mirrored = send(previous, [(j, sections - 1 - j) for j in range(half)])
    near, q_far = (swap(turn, starts, (q, 2), (p, 1)) for turn in range(2))
    p_far = q_far
    for slot in range(ticks + 1):
        if slot == 1:
            p, q, near, q_far = following
            p_far = q_far
        elif slot > 1:
            p = arrived(slot, 0)
            p_far = swap(1, starts, (p, 1))
            p, p_far, newer[1] = lax.optimization_barrier((p, p_far, newer[1]))
            q = arrived(slot, 1)
            near = swap(0, starts, (q, 2), (p, 1))
            q_far = swap(1, starts, (q, 2))
        *kept, w_one = inner_half(p, q, w_one, width, slot == 0)
        first = first_half(flags, p, kept, (near, q_far), (near, p_far), w_one, width)
        onward = [(j, j + 1) for j in range(1, sections - 1)] if slot > 0 else []
        if slot < ticks - 1:
            onward = [(0, 1)] + onward
        received, relays = {}, {}
        if slot < ticks:
            received[0] = send(first[1], onward)
        second = second_half(first, q, w_two, width, slot == ticks)
        if slot < ticks:
            received[1] = send(second, onward)
        if slot == 0:
            mirrored, _ = lax.optimization_barrier((mirrored, second))
            following = arrived(1, 0), arrived(1, 1)
            following += tuple(swap(turn, starts, (following[1], 2), (following[0], 1)) for turn in range(2))
        elif slot < ticks:
            relay_q, second = lax.optimization_barrier((newer[1], second))
            relays = {0: send(newer[0], [(1, sections - 1)]), 1: send(relay_q, [(1, sections - 1)])}
            if across:
                direct = {0: send(first[1], across), 1: send(second, across)}
        older, newer, relayed = newer, received, relays
    result = second
    return result.reshape(1, 2, planes, rows, width, chans)


def solution(mesh):
    in_specs = (
        P("section", None, "depth", None, None, None),
        P("section", None, "depth", None, None, None),
        P(None, None, "depth", None, None, None),
        P("section", None, None, None, None, None),
        P("section", None, None, None, None, None),
    )
    out_specs = P("section", None, "depth", None, None, None)
    return jax.shard_map(local, mesh=mesh, in_specs=in_specs, out_specs=out_specs, check_vma=False)
```

```python
import functools

import jax
import jax.numpy as jnp
from jax import lax
from jax.experimental import pallas as pl
from jax.experimental.pallas import tpu as pltpu
from jax.sharding import PartitionSpec as P

EPS = 1e-05
VMEM_LIMIT = 12 * 1024 * 1024


def act(values):
    values = values.astype(jnp.float32)
    scaled = values * lax.rsqrt(jnp.mean(values * values, axis=-1, keepdims=True) + EPS)
    return scaled * (0.5 + 0.5 * jnp.tanh(0.5 * scaled))


def fill(even, odd, at, values, width):
    planes, _, chans = values.shape
    field = act(values)
    edge = jnp.zeros((planes, width, chans), jnp.float32)
    even[pl.ds(at, planes)] = field.astype(jnp.bfloat16)
    odd[pl.ds(at, planes)] = jnp.concatenate([edge, field, edge], axis=1).astype(jnp.bfloat16)


def shifted(part, k, width):
    planes, voxels, chans = part.shape
    part = part.reshape(-1, width, chans)
    column = lax.broadcasted_iota(jnp.int32, part.shape, 1)
    if k == 0:
        part = jnp.where(column == 0, 0.0, pltpu.roll(part, 1, 1))
    elif k == 2:
        part = jnp.where(column == width - 1, 0.0, pltpu.roll(part, width - 1, 1))
    return part.reshape(planes, voxels, chans)


def product(taps, weights, offsets, k):
    planes, voxels, chans = taps[0].shape
    slab = jnp.concatenate([part.reshape(planes * voxels, chans) for part in taps], axis=-1)
    columns = jnp.concatenate([weights[(3 * n + k) * chans : (3 * n + k + 1) * chans] for n in offsets], axis=0)
    part = jnp.dot(slab, columns, preferred_element_type=jnp.float32)
    return part.reshape(planes, voxels, chans)


def convolve(taps, weights, width):
    return sum(shifted(product(taps, weights, range(9), k), k, width) for k in (1, 0, 2))


def ends(sources, weights, width):
    total = None
    for k in (1, 0, 2):
        sums = [None, None]
        for i, (taps, targets) in sources.items():
            part = product(taps, weights, range(3 * i, 3 * i + 3), k)
            for plane, target in enumerate(targets):
                piece = part[plane : plane + 1]
                sums[target] = piece if sums[target] is None else sums[target] + piece
        part = shifted(jnp.concatenate(sums, axis=0), k, width)
        total = part if total is None else total + part
    return total


def planes_at(even, odd, start, count, width):
    voxels = even.shape[1]
    return [
        even[start : start + count] if j == 1 else odd[start : start + count, j * width : j * width + voxels]
        for j in range(3)
    ]


def own_planes(width, field, weights, total, even, odd, ready=None):
    planes = field.shape[0]
    fill(even, odd, 0, field[...], width)
    if ready is not None:
        ready.wait()
    taps = [part for i in range(3) for part in planes_at(even, odd, i, planes - 2, width)]
    total[pl.ds(1, planes - 2)] = convolve(taps, weights, width)
    own = lambda plane: planes_at(even, odd, plane, 1, width)
    both = [jnp.concatenate(pair, axis=0) for pair in zip(own(0), own(planes - 1))]
    sources = {0: (own(planes - 2), (1,)), 1: (both, (0, 1)), 2: (own(1), (0,))}
    partial = ends(sources, weights, width)
    total[pl.ds(0, 1)] = partial[:1]
    total[pl.ds(planes - 1, 1)] = partial[1:]


def inner_kernel(width, field, weights, total, even, odd):
    own_planes(width, field, weights, total, even, odd)


def loading_kernel(width, field, weights_hbm, total, weights, even, odd, sem):
    copy = pltpu.make_async_copy(weights_hbm, weights, sem)
    copy.start()
    own_planes(width, field, weights, total, even, odd, copy)


def edge_kernel(width, flags, near, far, own, weights, *rest):
    *added, out, even, odd = rest
    planes = own.shape[0]
    above = flags[0] > 0
    near, far = near[...].astype(jnp.float32), far[...].astype(jnp.float32)
    fill(even, odd, 0, jnp.where(above, far, near), width)
    fill(even, odd, 1, jnp.where(above, near, far), width)
    halo = lambda plane: planes_at(even, odd, plane, 1, width)
    total = ends({0: (halo(0), (0,)), 2: (halo(1), (1,))}, weights, width)
    last = planes - 1
    pieces = (
        (0, 1, own[pl.ds(0, 1)] + total[:1]),
        (1, planes - 2, own[pl.ds(1, planes - 2)]),
        (last, 1, own[pl.ds(last, 1)] + total[1:]),
    )
    for start, count, piece in pieces:
        where = pl.ds(start, count)
        if added:
            piece = added[-1][where].astype(jnp.float32) + piece
        if len(added) == 2:
            out[0, where] = added[0][where]
            out[1, where] = piece.astype(out.dtype)
        else:
            out[where] = piece.astype(out.dtype)


def call(kernel, outputs, scratch, arguments, width):
    specs = [pl.BlockSpec(memory_space=pltpu.VMEM) for _ in arguments]
    if kernel is edge_kernel:
        specs[0] = pl.BlockSpec(memory_space=pltpu.SMEM)
    if kernel is loading_kernel:
        specs[-1] = pl.BlockSpec(memory_space=pltpu.HBM)
    return pl.pallas_call(
        functools.partial(kernel, width),
        out_shape=[jax.ShapeDtypeStruct(shape, dtype) for shape, dtype in outputs],
        in_specs=specs,
        out_specs=[pl.BlockSpec(memory_space=pltpu.VMEM) for _ in outputs],
        scratch_shapes=[pltpu.VMEM(shape, jnp.bfloat16) if shape else pltpu.SemaphoreType.DMA for shape in scratch],
        compiler_params=pltpu.CompilerParams(vmem_limit_bytes=VMEM_LIMIT),
        cost_estimate=pl.CostEstimate(flops=1, bytes_accessed=1, transcendentals=0),
    )(*arguments)


def stored(planes, voxels, chans, width):
    return (planes, voxels, chans), (planes, voxels + 2 * width, chans)


def inner_planes(field, weights, width, load=False):
    planes, voxels, chans = field.shape
    outputs = [(field.shape, jnp.float32)]
    scratch = stored(planes, voxels, chans, width)
    if load:
        weights = pltpu.with_memory_space_constraint(weights, pltpu.HBM)
        outputs.append((weights.shape, jnp.bfloat16))
        return call(loading_kernel, outputs, [*scratch, ()], (field, weights), width)
    return *call(inner_kernel, outputs, scratch, (field, weights), width), weights


def all_planes(flags, near, far, own, weights, added, width):
    _, voxels, chans = own.shape
    output = ((2, *own.shape) if len(added) == 2 else own.shape, jnp.bfloat16 if added else jnp.float32)
    arguments = (flags, near, far, own, weights, *added)
    (out,) = call(edge_kernel, [output], stored(2, voxels, chans, width), arguments, width)
    return out


def swap(turn, starts, block):
    count = lax.axis_size("depth")
    pairs = [pair for i in range(turn, count - 1, 2) for pair in ((i, i + 1), (i + 1, i))]
    return lax.ppermute(lax.dynamic_slice_in_dim(block, starts[turn], 1, axis=0), "depth", pairs)


def local(resident, previous, incoming, first_weights, second_weights):
    section = lax.axis_index("section")
    sections = lax.axis_size("section")
    half = sections // 2
    depth = lax.axis_index("depth")
    ticks = incoming.shape[0] + 1
    _, _, planes, rows, width, chans = resident.shape
    voxels = rows * width
    across = [(j, sections - 1 - j) for j in range(1, half - 1)]

    above = depth % 2 == 0
    places = {
        "flags": jnp.stack([above]).astype(jnp.int32),
        "starts": (jnp.where(above, planes - 1, 0), jnp.where(above, 0, planes - 1)),
        "first": section == 0,
        "second": section == 1,
        "last": section == sections - 1,
        "decoder": section >= half,
        "direct": (section > half) & (section < sections - 1) if across else (),
    }
    places, resident, previous, incoming, first_weights, second_weights = lax.optimization_barrier(
        (places, resident, previous, incoming, first_weights, second_weights)
    )
    flags, starts = places["flags"], places["starts"]

    flat = lambda a: a.reshape(a.shape[0], 2, planes, voxels, chans)
    resident, previous, incoming = flat(resident)[0], flat(previous)[0], flat(incoming)
    w_one = first_weights.reshape(27 * chans, chans)
    w_two = second_weights.reshape(27 * chans, chans)

    def send(block, pairs):
        return lax.ppermute(block, "section", pairs) if pairs else block

    def join(held, skip):
        total = (held.astype(jnp.float32) + skip.astype(jnp.float32)).astype(jnp.bfloat16)
        return jnp.where(places["decoder"], total, held)

    newer, older, relayed, direct = {}, {}, {}, {}

    def arrived(slot, stream):
        fresh = incoming[min(slot, ticks - 1) - 1, stream]
        if slot == 1:
            return jnp.where(places["first"], fresh, join(resident[stream], mirrored[stream]))
        held = jnp.where(places["second"], older[stream], newer[stream])
        skip = jnp.where(places["last"], relayed[stream], newer[stream])
        if across:
            skip = jnp.where(places["direct"], direct[stream], skip)
        return jnp.where(places["first"], fresh, join(held, skip))

    def swaps(block):
        return swap(0, starts, block), swap(1, starts, block)

    mirrored = send(previous, [(j, sections - 1 - j) for j in range(half)])
    p, q = resident
    halos = swaps(q)
    for slot in range(ticks + 1):
        if slot > 1:
            q = arrived(slot, 1)
            halos = swaps(q)
        own, w_one = inner_planes(q, w_one, width, slot == 0)
        first = all_planes(flags, *halos, own, w_one, (p,) if slot < 2 else (), width)
        if slot > 1:
            p = arrived(slot, 0)
            first = (p.astype(jnp.float32) + first).astype(jnp.bfloat16)
        halos = swaps(first)
        own, _ = inner_planes(first, w_two, width)
        if slot == 0:
            mirrored, _ = lax.optimization_barrier((mirrored, first))
            following = arrived(1, 0), arrived(1, 1)
            following += (swaps(following[1]),)
        second = all_planes(flags, *halos, own, w_two, (first, q) if slot == ticks else (q,), width)
        if slot == 0:
            p, q, halos = following
            halos, second = lax.optimization_barrier((halos, second))
        if slot < ticks:
            onward = [(j, j + 1) for j in range(sections - 1)] if slot > 0 else [(0, 1)]
            first, second = lax.optimization_barrier((first, second))
            received, relays = {1: send(second, onward), 0: send(first, onward)}, {}
            if slot > 0:
                held, _ = lax.optimization_barrier((newer, second))
                relays = {k: send(held[k], [(1, sections - 1)]) for k in (1, 0)}
                if across:
                    direct = {0: send(first, across), 1: send(second, across)}
            older, newer, relayed = newer, received, relays
    result = second
    return result.reshape(1, 2, planes, rows, width, chans)


def solution(mesh):
    in_specs = (
        P("section", None, "depth", None, None, None),
        P("section", None, "depth", None, None, None),
        P(None, None, "depth", None, None, None),
        P("section", None, None, None, None, None),
        P("section", None, None, None, None, None),
    )
    out_specs = P("section", None, "depth", None, None, None)
    return jax.shard_map(local, mesh=mesh, in_specs=in_specs, out_specs=out_specs, check_vma=False)
```

```python
import functools

import jax
import jax.numpy as jnp
from jax import lax
from jax.experimental import pallas as pl
from jax.experimental.pallas import tpu as pltpu
from jax.sharding import PartitionSpec as P

EPS = 1e-05
VMEM_LIMIT = 12 * 1024 * 1024


def act(values):
    values = values.astype(jnp.float32)
    scaled = values * lax.rsqrt(jnp.mean(values * values, axis=-1, keepdims=True) + EPS)
    return scaled * (0.5 + 0.5 * jnp.tanh(0.5 * scaled))


def fill(even, odd, at, values, width):
    planes, _, chans = values.shape
    field = act(values)
    edge = jnp.zeros((planes, width, chans), jnp.float32)
    even[pl.ds(at, planes)] = field.astype(jnp.bfloat16)
    odd[pl.ds(at, planes)] = jnp.concatenate([edge, field, edge], axis=1).astype(jnp.bfloat16)


def shifted(part, k, width):
    planes, voxels, chans = part.shape
    part = part.reshape(-1, width, chans)
    column = lax.broadcasted_iota(jnp.int32, part.shape, 1)
    if k == 0:
        part = jnp.where(column == 0, 0.0, pltpu.roll(part, 1, 1))
    elif k == 2:
        part = jnp.where(column == width - 1, 0.0, pltpu.roll(part, width - 1, 1))
    return part.reshape(planes, voxels, chans)


def product(taps, weights, offsets, k):
    planes, voxels, chans = taps[0].shape
    slab = jnp.concatenate([part.reshape(planes * voxels, chans) for part in taps], axis=-1)
    columns = jnp.concatenate([weights[(3 * n + k) * chans : (3 * n + k + 1) * chans] for n in offsets], axis=0)
    part = jnp.dot(slab, columns, preferred_element_type=jnp.float32)
    return part.reshape(planes, voxels, chans)


def convolve(taps, weights, width):
    return sum(shifted(product(taps, weights, range(9), k), k, width) for k in (1, 0, 2))


def ends(sources, weights, width):
    total = None
    for k in (1, 0, 2):
        sums = [None, None]
        for i, (taps, targets) in sources.items():
            part = product(taps, weights, range(3 * i, 3 * i + 3), k)
            for plane, target in enumerate(targets):
                piece = part[plane : plane + 1]
                sums[target] = piece if sums[target] is None else sums[target] + piece
        part = shifted(jnp.concatenate(sums, axis=0), k, width)
        total = part if total is None else total + part
    return total


def planes_at(even, odd, start, count, width):
    voxels = even.shape[1]
    return [
        even[start : start + count] if j == 1 else odd[start : start + count, j * width : j * width + voxels]
        for j in range(3)
    ]


def own_planes(width, field, weights, total, even, odd, ready=None):
    planes = field.shape[0]
    fill(even, odd, 0, field[...], width)
    if ready is not None:
        ready.wait()
    taps = [part for i in range(3) for part in planes_at(even, odd, i, planes - 2, width)]
    total[pl.ds(1, planes - 2)] = convolve(taps, weights, width)
    own = lambda plane: planes_at(even, odd, plane, 1, width)
    both = [jnp.concatenate(pair, axis=0) for pair in zip(own(0), own(planes - 1))]
    sources = {0: (own(planes - 2), (1,)), 1: (both, (0, 1)), 2: (own(1), (0,))}
    partial = ends(sources, weights, width)
    total[pl.ds(0, 1)] = partial[:1]
    total[pl.ds(planes - 1, 1)] = partial[1:]


def inner_kernel(width, field, weights, total, even, odd):
    own_planes(width, field, weights, total, even, odd)


def loading_kernel(width, field, weights_hbm, total, weights, even, odd, sem):
    copy = pltpu.make_async_copy(weights_hbm, weights, sem)
    copy.start()
    own_planes(width, field, weights, total, even, odd, copy)


def edge_kernel(width, flags, near, far, own, weights, *rest):
    *added, out, even, odd = rest
    planes = own.shape[0]
    above = flags[0] > 0
    near, far = near[...].astype(jnp.float32), far[...].astype(jnp.float32)
    fill(even, odd, 0, jnp.where(above, far, near), width)
    fill(even, odd, 1, jnp.where(above, near, far), width)
    halo = lambda plane: planes_at(even, odd, plane, 1, width)
    total = ends({0: (halo(0), (0,)), 2: (halo(1), (1,))}, weights, width)
    last = planes - 1
    pieces = (
        (0, 1, own[pl.ds(0, 1)] + total[:1]),
        (1, planes - 2, own[pl.ds(1, planes - 2)]),
        (last, 1, own[pl.ds(last, 1)] + total[1:]),
    )
    for start, count, piece in pieces:
        where = pl.ds(start, count)
        if added:
            piece = added[-1][where].astype(jnp.float32) + piece
        if len(added) == 2:
            out[0, where] = added[0][where]
            out[1, where] = piece.astype(out.dtype)
        else:
            out[where] = piece.astype(out.dtype)


def call(kernel, outputs, scratch, arguments, width):
    specs = [pl.BlockSpec(memory_space=pltpu.VMEM) for _ in arguments]
    if kernel is edge_kernel:
        specs[0] = pl.BlockSpec(memory_space=pltpu.SMEM)
    if kernel is loading_kernel:
        specs[-1] = pl.BlockSpec(memory_space=pltpu.HBM)
    return pl.pallas_call(
        functools.partial(kernel, width),
        out_shape=[jax.ShapeDtypeStruct(shape, dtype) for shape, dtype in outputs],
        in_specs=specs,
        out_specs=[pl.BlockSpec(memory_space=pltpu.VMEM) for _ in outputs],
        scratch_shapes=[pltpu.VMEM(shape, jnp.bfloat16) if shape else pltpu.SemaphoreType.DMA for shape in scratch],
        compiler_params=pltpu.CompilerParams(vmem_limit_bytes=VMEM_LIMIT),
        cost_estimate=pl.CostEstimate(flops=1, bytes_accessed=1, transcendentals=0),
    )(*arguments)


def stored(planes, voxels, chans, width):
    return (planes, voxels, chans), (planes, voxels + 2 * width, chans)


def inner_planes(field, weights, width, load=False):
    planes, voxels, chans = field.shape
    outputs = [(field.shape, jnp.float32)]
    scratch = stored(planes, voxels, chans, width)
    if load:
        weights = pltpu.with_memory_space_constraint(weights, pltpu.HBM)
        outputs.append((weights.shape, jnp.bfloat16))
        return call(loading_kernel, outputs, [*scratch, ()], (field, weights), width)
    return *call(inner_kernel, outputs, scratch, (field, weights), width), weights


def all_planes(flags, near, far, own, weights, added, width):
    _, voxels, chans = own.shape
    output = ((2, *own.shape) if len(added) == 2 else own.shape, jnp.bfloat16 if added else jnp.float32)
    arguments = (flags, near, far, own, weights, *added)
    (out,) = call(edge_kernel, [output], stored(2, voxels, chans, width), arguments, width)
    return out


def swap(turn, starts, block):
    count = lax.axis_size("depth")
    pairs = [pair for i in range(turn, count - 1, 2) for pair in ((i, i + 1), (i + 1, i))]
    return lax.ppermute(lax.dynamic_slice_in_dim(block, starts[turn], 1, axis=0), "depth", pairs)


def local(resident, previous, incoming, first_weights, second_weights):
    section = lax.axis_index("section")
    sections = lax.axis_size("section")
    half = sections // 2
    depth = lax.axis_index("depth")
    ticks = incoming.shape[0] + 1
    _, _, planes, rows, width, chans = resident.shape
    voxels = rows * width
    across = [(j, sections - 1 - j) for j in range(1, half - 1)]

    above = depth % 2 == 0
    places = {
        "flags": jnp.stack([above]).astype(jnp.int32),
        "starts": (jnp.where(above, planes - 1, 0), jnp.where(above, 0, planes - 1)),
        "first": section == 0,
        "second": section == 1,
        "last": section == sections - 1,
        "decoder": section >= half,
        "direct": (section > half) & (section < sections - 1) if across else (),
    }
    places, resident, previous, incoming, first_weights, second_weights = lax.optimization_barrier(
        (places, resident, previous, incoming, first_weights, second_weights)
    )
    flags, starts = places["flags"], places["starts"]

    flat = lambda a: a.reshape(a.shape[0], 2, planes, voxels, chans)
    resident, previous, incoming = flat(resident)[0], flat(previous)[0], flat(incoming)
    w_one = first_weights.reshape(27 * chans, chans)
    w_two = second_weights.reshape(27 * chans, chans)

    def send(block, pairs):
        return lax.ppermute(block, "section", pairs) if pairs else block

    def join(held, skip):
        total = (held.astype(jnp.float32) + skip.astype(jnp.float32)).astype(jnp.bfloat16)
        return jnp.where(places["decoder"], total, held)

    newer, older, relayed, direct = {}, {}, {}, {}

    def arrived(slot, stream):
        fresh = incoming[min(slot, ticks - 1) - 1, stream]
        if slot == 1:
            return jnp.where(places["first"], fresh, join(resident[stream], mirrored[stream]))
        held = jnp.where(places["second"], older[stream], newer[stream])
        skip = jnp.where(places["last"], relayed[stream], newer[stream])
        if across:
            skip = jnp.where(places["direct"], direct[stream], skip)
        return jnp.where(places["first"], fresh, join(held, skip))

    def swaps(block):
        return swap(0, starts, block), swap(1, starts, block)

    mirrored = send(previous, [(j, sections - 1 - j) for j in range(half)])
    p, q = resident
    halos = swaps(q)
    for slot in range(ticks + 1):
        if slot > 1:
            q = arrived(slot, 1)
            if slot > 2:
                q, relayed[0] = lax.optimization_barrier((q, relayed[0]))
            halos = swaps(q)
        own, w_one = inner_planes(q, w_one, width, slot == 0)
        first = all_planes(flags, *halos, own, w_one, (p,) if slot < 2 else (), width)
        if slot > 1:
            p = arrived(slot, 0)
            first = (p.astype(jnp.float32) + first).astype(jnp.bfloat16)
        halos = swaps(first)
        own, _ = inner_planes(first, w_two, width)
        if slot == 0:
            mirrored, _ = lax.optimization_barrier((mirrored, first))
            following = arrived(1, 0), arrived(1, 1)
            following += (swaps(following[1]),)
        second = all_planes(flags, *halos, own, w_two, (first, q) if slot == ticks else (q,), width)
        if slot == 0:
            p, q, halos = following
            halos, second = lax.optimization_barrier((halos, second))
        if slot < ticks:
            onward = [(j, j + 1) for j in range(sections - 1)] if slot > 0 else [(0, 1)]
            relays = {}
            if slot > 0:
                held = newer
                if slot == 1:
                    held, _ = lax.optimization_barrier((held, second))
                relays = {k: send(held[k], [(1, sections - 1)]) for k in (1, 0)}
                if slot > 1:
                    relays[1], second = lax.optimization_barrier((relays[1], second))
                if across:
                    direct = {0: send(first, across), 1: send(second, across)}
            received = {1: send(second, onward)}
            if slot > 0:
                first, received[1] = lax.optimization_barrier((first, received[1]))
            else:
                first, _ = lax.optimization_barrier((first, second))
            received[0] = send(first, onward)
            older, newer, relayed = newer, received, relays
    result = second
    return result.reshape(1, 2, planes, rows, width, chans)


def solution(mesh):
    in_specs = (
        P("section", None, "depth", None, None, None),
        P("section", None, "depth", None, None, None),
        P(None, None, "depth", None, None, None),
        P("section", None, None, None, None, None),
        P("section", None, None, None, None, None),
    )
    out_specs = P("section", None, "depth", None, None, None)
    return jax.shard_map(local, mesh=mesh, in_specs=in_specs, out_specs=out_specs, check_vma=False)
```

```python
import functools

import jax
import jax.numpy as jnp
from jax import lax
from jax.experimental import pallas as pl
from jax.experimental.pallas import tpu as pltpu
from jax.sharding import PartitionSpec as P

EPS = 1e-05
VMEM_LIMIT = 12 * 1024 * 1024


def act(values):
    values = values.astype(jnp.float32)
    scaled = values * lax.rsqrt(jnp.mean(values * values, axis=-1, keepdims=True) + EPS)
    return scaled * (0.5 + 0.5 * jnp.tanh(0.5 * scaled))


def fill(even, odd, at, values, width):
    planes, _, chans = values.shape
    field = act(values)
    edge = jnp.zeros((planes, width, chans), jnp.float32)
    even[pl.ds(at, planes)] = field.astype(jnp.bfloat16)
    odd[pl.ds(at, planes)] = jnp.concatenate([edge, field, edge], axis=1).astype(jnp.bfloat16)


def shifted(part, k, width):
    planes, voxels, chans = part.shape
    part = part.reshape(-1, width, chans)
    column = lax.broadcasted_iota(jnp.int32, part.shape, 1)
    if k == 0:
        part = jnp.where(column == 0, 0.0, pltpu.roll(part, 1, 1))
    elif k == 2:
        part = jnp.where(column == width - 1, 0.0, pltpu.roll(part, width - 1, 1))
    return part.reshape(planes, voxels, chans)


def product(taps, weights, offsets, k):
    planes, voxels, chans = taps[0].shape
    slab = jnp.concatenate([part.reshape(planes * voxels, chans) for part in taps], axis=-1)
    columns = jnp.concatenate([weights[(3 * n + k) * chans : (3 * n + k + 1) * chans] for n in offsets], axis=0)
    part = jnp.dot(slab, columns, preferred_element_type=jnp.float32)
    return part.reshape(planes, voxels, chans)


def convolve(taps, weights, width):
    return sum(shifted(product(taps, weights, range(9), k), k, width) for k in (1, 0, 2))


def edges(sources, targets, weights, width):
    total = None
    for k in (1, 0, 2):
        sums = [None] * 4
        for i in range(3):
            part = product(sources[i], weights, range(3 * i, 3 * i + 3), k)
            for plane, target in enumerate(targets[i]):
                piece = part[plane : plane + 1]
                sums[target] = piece if sums[target] is None else sums[target] + piece
        part = shifted(jnp.concatenate(sums, axis=0), k, width)
        total = part if total is None else total + part
    return total


def planes_at(even, odd, start, count, width):
    voxels = even.shape[1]
    return [
        even[start : start + count] if j == 1 else odd[start : start + count, j * width : j * width + voxels]
        for j in range(3)
    ]


def own_planes(width, inner_p, outer, weights, inner, partial, even, odd, ready=None):
    planes = outer.shape[0] - 2
    fill(even, odd, 0, outer[pl.ds(1, planes)], width)
    if ready is not None:
        ready.wait()
    taps = [part for i in range(3) for part in planes_at(even, odd, i, planes - 2, width)]
    inner[...] = (inner_p[...].astype(jnp.float32) + convolve(taps, weights, width)).astype(inner.dtype)
    own = lambda plane: planes_at(even, odd, plane, 1, width)
    pair = lambda one, other: [jnp.concatenate(both, axis=0) for both in zip(own(one), own(other))]
    sources = (pair(planes - 2, planes - 1), pair(0, planes - 1), pair(0, 1))
    partial[...] = edges(sources, ((2, 3), (1, 2), (0, 1)), weights, width)


def inner_kernel(width, inner_p, outer, weights, inner, partial, even, odd):
    own_planes(width, inner_p, outer, weights, inner, partial, even, odd)


def loading_kernel(width, inner_p, outer, weights_hbm, inner, partial, weights, even, odd, sem):
    copy = pltpu.make_async_copy(weights_hbm, weights, sem)
    copy.start()
    own_planes(width, inner_p, outer, weights, inner, partial, even, odd, copy)


def edge_kernel(width, flags, outer, inner, partial, near, far, weights, low, mid, high, even, odd):
    planes = mid.shape[0]
    above = flags[2] > 0
    near, far = near[...].astype(jnp.float32), far[...].astype(jnp.float32)
    below, beyond = jnp.where(above, far, near), jnp.where(above, near, far)
    fill(even, odd, 0, below[:2], width)
    fill(even, odd, 2, beyond[1:], width)
    sources = [planes_at(even, odd, start, 2, width) for start in range(3)]
    total = partial[...] + edges(sources, ((0, 1), (0, 3), (2, 3)), weights, width)
    low[...] = jnp.where(flags[0] > 0, below[2:] + total[:1], 0.0).astype(low.dtype)
    mid[pl.ds(0, 1)] = (outer[pl.ds(0, 1)].astype(jnp.float32) + total[1:2]).astype(mid.dtype)
    mid[pl.ds(1, planes - 2)] = inner[...]
    mid[pl.ds(planes - 1, 1)] = (outer[pl.ds(planes + 1, 1)].astype(jnp.float32) + total[2:3]).astype(mid.dtype)
    high[...] = jnp.where(flags[1] > 0, beyond[:1] + total[3:], 0.0).astype(high.dtype)


def second_kernel(width, first_low, first_mid, first_high, outer, weights, out, even, odd):
    planes = first_mid.shape[0]
    fill(even, odd, 0, first_low[...], width)
    fill(even, odd, 1, first_mid[...], width)
    fill(even, odd, 1 + planes, first_high[...], width)
    taps = [part for i in range(3) for part in planes_at(even, odd, i, planes, width)]
    second = (outer[pl.ds(1, planes)].astype(jnp.float32) + convolve(taps, weights, width)).astype(out.dtype)
    if len(out.shape) == 4:
        out[0] = first_mid[...]
        out[1] = second
    else:
        out[pl.ds(0, 1)] = first_mid[pl.ds(0, 1)]
        out[pl.ds(1, planes)] = second
        out[pl.ds(planes + 1, 1)] = first_mid[pl.ds(planes - 1, 1)]


def call(kernel, outputs, scratch, arguments, width):
    specs = [pl.BlockSpec(memory_space=pltpu.VMEM) for _ in arguments]
    if kernel is edge_kernel:
        specs[0] = pl.BlockSpec(memory_space=pltpu.SMEM)
    if kernel is loading_kernel:
        specs[-1] = pl.BlockSpec(memory_space=pltpu.HBM)
    return pl.pallas_call(
        functools.partial(kernel, width),
        out_shape=[jax.ShapeDtypeStruct(shape, dtype) for shape, dtype in outputs],
        in_specs=specs,
        out_specs=[pl.BlockSpec(memory_space=pltpu.VMEM) for _ in outputs],
        scratch_shapes=[pltpu.VMEM(shape, jnp.bfloat16) if shape else pltpu.SemaphoreType.DMA for shape in scratch],
        compiler_params=pltpu.CompilerParams(vmem_limit_bytes=VMEM_LIMIT),
        cost_estimate=pl.CostEstimate(flops=1, bytes_accessed=1, transcendentals=0),
    )(*arguments)


def stored(planes, voxels, chans, width):
    return (planes, voxels, chans), (planes, voxels + 2 * width, chans)


def inner_half(inner_p, outer, weights, width, load):
    inner, voxels, chans = inner_p.shape
    outputs = [(inner_p.shape, jnp.bfloat16), ((4, voxels, chans), jnp.float32)]
    scratch = stored(inner + 2, voxels, chans, width)
    if load:
        weights = pltpu.with_memory_space_constraint(weights, pltpu.HBM)
        outputs.append((weights.shape, jnp.bfloat16))
        return call(loading_kernel, outputs, [*scratch, ()], (inner_p, outer, weights), width)
    return *call(inner_kernel, outputs, scratch, (inner_p, outer, weights), width), weights


def first_half(flags, outer, inner, partial, halos, weights, width):
    rows, voxels, chans = outer.shape
    return call(
        edge_kernel,
        [((n, voxels, chans), jnp.bfloat16) for n in (1, rows - 2, 1)],
        stored(4, voxels, chans, width),
        (flags, outer, inner, partial, *halos, weights),
        width,
    )


def second_half(first, outer, weights, width, both):
    rows, voxels, chans = outer.shape
    (out,) = call(
        second_kernel,
        [((2, rows - 2, voxels, chans) if both else outer.shape, jnp.bfloat16)],
        stored(rows, voxels, chans, width),
        (*first, outer, weights),
        width,
    )
    return out


def swap(turn, starts, block):
    count = lax.axis_size("depth")
    pairs = [pair for i in range(turn, count - 1, 2) for pair in ((i, i + 1), (i + 1, i))]
    return lax.ppermute(lax.dynamic_slice_in_dim(block, starts[turn], 3, axis=0), "depth", pairs)


def local(resident, previous, incoming, first_weights, second_weights):
    section = lax.axis_index("section")
    sections = lax.axis_size("section")
    half = sections // 2
    depth = lax.axis_index("depth")
    ticks = incoming.shape[0] + 1
    _, _, planes, rows, width, chans = resident.shape
    voxels = rows * width
    across = [(j, sections - 1 - j) for j in range(1, half - 1)]

    above = depth % 2 == 0
    places = {
        "flags": jnp.stack([depth > 0, depth < lax.axis_size("depth") - 1, above]).astype(jnp.int32),
        "starts": (jnp.where(above, planes - 1, 0), jnp.where(above, 0, planes - 1)),
        "first": section == 0,
        "second": section == 1,
        "last": section == sections - 1,
        "decoder": section >= half,
        "direct": (section > half) & (section < sections - 1) if across else (),
    }
    places, resident, previous, incoming, first_weights, second_weights = lax.optimization_barrier(
        (places, resident, previous, incoming, first_weights, second_weights)
    )
    flags, starts = places["flags"], places["starts"]

    flat = lambda a: a.reshape(a.shape[0], 2, planes, voxels, chans)
    resident, previous, incoming = flat(resident)[0], flat(previous)[0], flat(incoming)
    w_one = first_weights.reshape(27 * chans, chans)
    w_two = second_weights.reshape(27 * chans, chans)

    def send(block, pairs):
        return lax.ppermute(block, "section", pairs) if pairs else block

    def join(held, skip):
        total = (held.astype(jnp.float32) + skip.astype(jnp.float32)).astype(jnp.bfloat16)
        return jnp.where(places["decoder"], total, held)

    def parted(streams):
        p, q = streams
        return p[1:-1], jnp.concatenate([p[:1], q, p[-1:]], axis=0)

    newer, older, direct = {}, {}, {}
    relayed = None

    def arrived(slot, part):
        fresh = parted(incoming[min(slot, ticks - 1) - 1])[part]
        held = jnp.where(places["second"], older[part], newer[part])
        passed = relayed[: planes - 2] if part == 0 else relayed[planes - 2 :]
        skip = jnp.where(places["last"], passed, newer[part])
        if across:
            skip = jnp.where(places["direct"], direct[part], skip)
        return jnp.where(places["first"], fresh, join(held, skip))

    def swaps(block):
        return swap(0, starts, block), swap(1, starts, block)

    mirrored = send(previous, [(j, sections - 1 - j) for j in range(half)])
    inner_p, outer = parted(resident)
    halos = swaps(outer)
    for slot in range(ticks + 1):
        if slot == 1:
            inner_p, outer, halos = following
        elif slot > 1:
            outer = arrived(slot, 1)
            halos = swaps(outer)
            inner_p = arrived(slot, 0)
        inner, partial, w_one = inner_half(inner_p, outer, w_one, width, slot == 0)
        onward = [(j, j + 1) for j in range(1, sections - 1)] if slot > 0 else []
        if slot < ticks - 1:
            onward = [(0, 1)] + onward
        received = {}
        if slot < ticks:
            received[0] = send(inner, onward)
            if across and slot > 0:
                direct[0] = send(inner, across)
        first = first_half(flags, outer, inner, partial, halos, w_one, width)
        sent = second_half(first, outer, w_two, width, slot == ticks)
        if slot == 0:
            mirrored, _ = lax.optimization_barrier((mirrored, sent))
            fresh = incoming[0]
            following = parted([jnp.where(places["first"], fresh[n], join(resident[n], mirrored[n])) for n in range(2)])
            following += (swaps(following[1]),)
        if slot < ticks:
            if slot > 0:
                received[0], sent = lax.optimization_barrier((received[0], sent))
            received[1] = send(sent, onward)
            if across and slot > 0:
                direct[1] = send(sent, across)
        if 0 < slot < ticks:
            held = jnp.concatenate([newer[0], newer[1]], axis=0)
            held, _ = lax.optimization_barrier((held, first[1] if slot == 1 else inner_p))
            relayed = send(held, [(1, sections - 1)])
        older, newer = newer, received
    result = sent
    return result.reshape(1, 2, planes, rows, width, chans)


def solution(mesh):
    in_specs = (
        P("section", None, "depth", None, None, None),
        P("section", None, "depth", None, None, None),
        P(None, None, "depth", None, None, None),
        P("section", None, None, None, None, None),
        P("section", None, None, None, None, None),
    )
    out_specs = P("section", None, "depth", None, None, None)
    return jax.shard_map(local, mesh=mesh, in_specs=in_specs, out_specs=out_specs, check_vma=False)
```

```python
import functools

import jax
import jax.numpy as jnp
from jax import lax
from jax.experimental import pallas as pl
from jax.experimental.pallas import tpu as pltpu
from jax.sharding import PartitionSpec as P

EPS = 1e-05
VMEM_LIMIT = 12 * 1024 * 1024


def act(values):
    values = values.astype(jnp.float32)
    scaled = values * lax.rsqrt(jnp.mean(values * values, axis=-1, keepdims=True) + EPS)
    return scaled * (0.5 + 0.5 * jnp.tanh(0.5 * scaled))


def fill(even, odd, at, values, width):
    planes, _, chans = values.shape
    field = act(values)
    edge = jnp.zeros((planes, width, chans), jnp.float32)
    even[pl.ds(at, planes)] = field.astype(jnp.bfloat16)
    odd[pl.ds(at, planes)] = jnp.concatenate([edge, field, edge], axis=1).astype(jnp.bfloat16)


def shifted(part, k, width):
    planes, voxels, chans = part.shape
    part = part.reshape(-1, width, chans)
    column = lax.broadcasted_iota(jnp.int32, part.shape, 1)
    if k == 0:
        part = jnp.where(column == 0, 0.0, pltpu.roll(part, 1, 1))
    elif k == 2:
        part = jnp.where(column == width - 1, 0.0, pltpu.roll(part, width - 1, 1))
    return part.reshape(planes, voxels, chans)


def product(taps, weights, offsets, k):
    planes, voxels, chans = taps[0].shape
    slab = jnp.concatenate([part.reshape(planes * voxels, chans) for part in taps], axis=-1)
    columns = jnp.concatenate([weights[(3 * n + k) * chans : (3 * n + k + 1) * chans] for n in offsets], axis=0)
    part = jnp.dot(slab, columns, preferred_element_type=jnp.float32)
    return part.reshape(planes, voxels, chans)


def convolve(taps, weights, width):
    return sum(shifted(product(taps, weights, range(9), k), k, width) for k in (1, 0, 2))


def edges(sources, targets, weights, width):
    total = None
    for k in (1, 0, 2):
        sums = [None] * 4
        for i in range(3):
            part = product(sources[i], weights, range(3 * i, 3 * i + 3), k)
            for plane, target in enumerate(targets[i]):
                piece = part[plane : plane + 1]
                sums[target] = piece if sums[target] is None else sums[target] + piece
        part = shifted(jnp.concatenate(sums, axis=0), k, width)
        total = part if total is None else total + part
    return total


def planes_at(even, odd, start, count, width):
    voxels = even.shape[1]
    return [
        even[start : start + count] if j == 1 else odd[start : start + count, j * width : j * width + voxels]
        for j in range(3)
    ]


def stream(ref, number):
    return ref.at[number] if len(ref.shape) == 4 else ref


def own_planes(width, p, q, weights, inner, partial, even, odd, ready=None):
    p, q = stream(p, 0), stream(q, 1)
    planes = q.shape[0]
    fill(even, odd, 0, q[...], width)
    if ready is not None:
        ready.wait()
    taps = [part for i in range(3) for part in planes_at(even, odd, i, planes - 2, width)]
    inner[...] = (p[1:-1].astype(jnp.float32) + convolve(taps, weights, width)).astype(inner.dtype)
    own = lambda plane: planes_at(even, odd, plane, 1, width)
    pair = lambda one, other: [jnp.concatenate(both, axis=0) for both in zip(own(one), own(other))]
    sources = (pair(planes - 2, planes - 1), pair(0, planes - 1), pair(0, 1))
    partial[...] = edges(sources, ((2, 3), (1, 2), (0, 1)), weights, width)


def inner_kernel(width, p, q, weights, inner, partial, even, odd):
    own_planes(width, p, q, weights, inner, partial, even, odd)


def loading_kernel(width, p, q, weights_hbm, inner, partial, weights, even, odd, sem):
    copy = pltpu.make_async_copy(weights_hbm, weights, sem)
    copy.start()
    own_planes(width, p, q, weights, inner, partial, even, odd, copy)


def edge_kernel(width, flags, p, inner, partial, near, far, weights, low, mid, high, even, odd):
    p = stream(p, 0)
    planes = p.shape[0]
    above = flags[2] > 0
    near, far = near[...].astype(jnp.float32), far[...].astype(jnp.float32)
    below, beyond = jnp.where(above, far, near), jnp.where(above, near, far)
    fill(even, odd, 0, below[:2], width)
    fill(even, odd, 2, beyond[:2], width)
    sources = [planes_at(even, odd, start, 2, width) for start in range(3)]
    total = partial[...] + edges(sources, ((0, 1), (0, 3), (2, 3)), weights, width)
    low[...] = jnp.where(flags[0] > 0, below[2:] + total[:1], 0.0).astype(low.dtype)
    mid[pl.ds(0, 1)] = (p[:1].astype(jnp.float32) + total[1:2]).astype(mid.dtype)
    mid[pl.ds(1, planes - 2)] = inner[...]
    mid[pl.ds(planes - 1, 1)] = (p[-1:].astype(jnp.float32) + total[2:3]).astype(mid.dtype)
    high[...] = jnp.where(flags[1] > 0, beyond[2:] + total[3:], 0.0).astype(high.dtype)


def second_sum(width, first_low, first_mid, first_high, q, weights, even, odd):
    q = stream(q, 1)
    planes = q.shape[0]
    fill(even, odd, 0, first_low[...], width)
    fill(even, odd, 1, first_mid[...], width)
    fill(even, odd, 1 + planes, first_high[...], width)
    taps = [part for i in range(3) for part in planes_at(even, odd, i, planes, width)]
    return q[...].astype(jnp.float32) + convolve(taps, weights, width)


def second_kernel(width, first_low, first_mid, first_high, q, weights, out, even, odd):
    out[...] = second_sum(width, first_low, first_mid, first_high, q, weights, even, odd).astype(out.dtype)


def last_kernel(width, first_low, first_mid, first_high, q, weights, out, even, odd, second, first_sem, second_sem):
    first_copy = pltpu.make_async_copy(first_mid, out.at[0], first_sem)
    first_copy.start()
    second[...] = second_sum(width, first_low, first_mid, first_high, q, weights, even, odd).astype(second.dtype)
    second_copy = pltpu.make_async_copy(second, out.at[1], second_sem)
    second_copy.start()
    first_copy.wait()
    second_copy.wait()


def call(kernel, outputs, scratch, arguments, width):
    specs = [pl.BlockSpec(memory_space=pltpu.VMEM) for _ in arguments]
    if kernel is edge_kernel:
        specs[0] = pl.BlockSpec(memory_space=pltpu.SMEM)
    if kernel is loading_kernel:
        specs[-1] = pl.BlockSpec(memory_space=pltpu.HBM)
    return pl.pallas_call(
        functools.partial(kernel, width),
        out_shape=[jax.ShapeDtypeStruct(shape, dtype) for shape, dtype in outputs],
        in_specs=specs,
        out_specs=[pl.BlockSpec(memory_space=pltpu.HBM if kernel is last_kernel else pltpu.VMEM) for _ in outputs],
        scratch_shapes=[pltpu.VMEM(shape, jnp.bfloat16) if shape else pltpu.SemaphoreType.DMA for shape in scratch],
        compiler_params=pltpu.CompilerParams(vmem_limit_bytes=VMEM_LIMIT),
        cost_estimate=pl.CostEstimate(flops=1, bytes_accessed=1, transcendentals=0),
    )(*arguments)


def stored(planes, voxels, chans, width):
    return (planes, voxels, chans), (planes, voxels + 2 * width, chans)


def inner_half(p, q, weights, width, load):
    planes, voxels, chans = q.shape[-3:]
    outputs = [((planes - 2, voxels, chans), jnp.bfloat16), ((4, voxels, chans), jnp.float32)]
    scratch = stored(planes, voxels, chans, width)
    if load:
        weights = pltpu.with_memory_space_constraint(weights, pltpu.HBM)
        outputs.append((weights.shape, jnp.bfloat16))
        return call(loading_kernel, outputs, [*scratch, ()], (p, q, weights), width)
    return *call(inner_kernel, outputs, scratch, (p, q, weights), width), weights


def first_half(flags, p, kept, halos, weights, width):
    planes, voxels, chans = p.shape[-3:]
    return call(
        edge_kernel,
        [((n, voxels, chans), jnp.bfloat16) for n in (1, planes, 1)],
        stored(4, voxels, chans, width),
        (flags, p, *kept, *halos, weights),
        width,
    )


def second_half(first, q, weights, width, last):
    shape = q.shape[-3:]
    scratch = stored(shape[0] + 2, *shape[1:], width)
    output = shape
    if last:
        scratch, output = [*scratch, shape, (), ()], (2, *shape)
    (out,) = call(last_kernel if last else second_kernel, [(output, jnp.bfloat16)], scratch, (*first, q, weights), width)
    return out


def swap(turn, starts, *blocks):
    count = lax.axis_size("depth")
    parts = []
    for block, n, *number in blocks:
        part = lax.dynamic_slice(block, (*number, starts[n][turn], 0, 0), (*[1] * len(number), n, *block.shape[-2:]))
        parts.append(part.reshape(part.shape[-3:]))
    pairs = [pair for i in range(turn, count - 1, 2) for pair in ((i, i + 1), (i + 1, i))]
    return lax.ppermute(jnp.concatenate(parts, axis=0), "depth", pairs)


def local(resident, previous, incoming, first_weights, second_weights):
    section = lax.axis_index("section")
    sections = lax.axis_size("section")
    half = sections // 2
    depth = lax.axis_index("depth")
    ticks = incoming.shape[0] + 1
    _, _, planes, rows, width, chans = resident.shape
    voxels = rows * width
    across = [(j, sections - 1 - j) for j in range(1, half - 1)]

    above = depth % 2 == 0
    places = {
        "flags": jnp.stack([depth > 0, depth < lax.axis_size("depth") - 1, above]).astype(jnp.int32),
        "starts": {
            n: (jnp.where(above, planes - n, 0), jnp.where(above, 0, planes - n)) for n in (1, 2)
        },
        "first": section == 0,
        "second": section == 1,
        "last": section == sections - 1,
        "decoder": section >= half,
        "direct": (section > half) & (section < sections - 1) if across else (),
    }
    places, resident, previous, incoming, first_weights, second_weights = lax.optimization_barrier(
        (places, resident, previous, incoming, first_weights, second_weights)
    )
    flags, starts = places["flags"], places["starts"]

    flat = lambda a: a.reshape(a.shape[0], 2, planes, voxels, chans)
    resident, previous, incoming = flat(resident)[0], flat(previous)[0], flat(incoming)
    w_one = first_weights.reshape(27 * chans, chans)
    w_two = second_weights.reshape(27 * chans, chans)

    def send(block, pairs):
        return lax.ppermute(block, "section", pairs) if pairs else block

    def join(held, skip):
        total = (held.astype(jnp.float32) + skip.astype(jnp.float32)).astype(jnp.bfloat16)
        return jnp.where(places["decoder"], total, held)

    newer, older, relayed, direct = {}, {}, {}, {}

    def arrived(slot, stream):
        fresh = incoming[min(slot, ticks - 1) - 1, stream]
        if slot == 1:
            return jnp.where(places["first"], fresh, join(resident[stream], mirrored[stream]))
        held = jnp.where(places["second"], older[stream], newer[stream])
        skip = jnp.where(places["last"], relayed[stream], newer[stream])
        if across:
            skip = jnp.where(places["direct"], direct[stream], skip)
        return jnp.where(places["first"], fresh, join(held, skip))

    p = q = resident
    mirrored = send(previous, [(j, sections - 1 - j) for j in range(half)])
    near, far = (swap(turn, starts, (resident, 2, 1), (resident, 1, 0)) for turn in range(2))
    for slot in range(ticks + 1):
        if slot == 1:
            p, q, near, far = following
        elif slot > 1:
            p = arrived(slot, 0)
            p, newer[1] = lax.optimization_barrier((p, newer[1]))
            q = arrived(slot, 1)
            near, far = (swap(turn, starts, (q, 2), (p, 1)) for turn in range(2))
        *kept, w_one = inner_half(p, q, w_one, width, slot == 0)
        first = first_half(flags, p, kept, (near, far), w_one, width)
        onward = [(j, j + 1) for j in range(1, sections - 1)] if slot > 0 else []
        if slot < ticks - 1:
            onward = [(0, 1)] + onward
        received, relays = {}, {}
        if slot < ticks:
            received[0] = send(first[1], onward)
        second = second_half(first, q, w_two, width, slot == ticks)
        if slot < ticks:
            received[1] = send(second, onward)
        if slot == 0:
            mirrored, _ = lax.optimization_barrier((mirrored, second))
            following = arrived(1, 0), arrived(1, 1)
            following += tuple(swap(turn, starts, (following[1], 2), (following[0], 1)) for turn in range(2))
        elif slot < ticks:
            relay_q, second = lax.optimization_barrier((newer[1], second))
            relays = {0: send(newer[0], [(1, sections - 1)]), 1: send(relay_q, [(1, sections - 1)])}
            if across:
                direct = {0: send(first[1], across), 1: send(second, across)}
        older, newer, relayed = newer, received, relays
    result = second
    return result.reshape(1, 2, planes, rows, width, chans)


def solution(mesh):
    in_specs = (
        P("section", None, "depth", None, None, None),
        P("section", None, "depth", None, None, None),
        P(None, None, "depth", None, None, None),
        P("section", None, None, None, None, None),
        P("section", None, None, None, None, None),
    )
    out_specs = P("section", None, "depth", None, None, None)
    return jax.shard_map(local, mesh=mesh, in_specs=in_specs, out_specs=out_specs, check_vma=False)
```

```python
import functools

import jax
import jax.numpy as jnp
from jax import lax
from jax.experimental import pallas as pl
from jax.experimental.pallas import tpu as pltpu
from jax.sharding import PartitionSpec as P

EPS = 1e-05
VMEM_LIMIT = 12 * 1024 * 1024


def act(values):
    values = values.astype(jnp.float32)
    scaled = values * lax.rsqrt(jnp.mean(values * values, axis=-1, keepdims=True) + EPS)
    return scaled * (0.5 + 0.5 * jnp.tanh(0.5 * scaled))


def fill(even, odd, at, values, width):
    planes, _, chans = values.shape
    field = act(values)
    edge = jnp.zeros((planes, width, chans), jnp.float32)
    even[pl.ds(at, planes)] = field.astype(jnp.bfloat16)
    odd[pl.ds(at, planes)] = jnp.concatenate([edge, field, edge], axis=1).astype(jnp.bfloat16)


def shifted(part, k, width):
    planes, voxels, chans = part.shape
    part = part.reshape(-1, width, chans)
    column = lax.broadcasted_iota(jnp.int32, part.shape, 1)
    if k == 0:
        part = jnp.where(column == 0, 0.0, pltpu.roll(part, 1, 1))
    elif k == 2:
        part = jnp.where(column == width - 1, 0.0, pltpu.roll(part, width - 1, 1))
    return part.reshape(planes, voxels, chans)


def product(taps, weights, offsets, k):
    planes, voxels, chans = taps[0].shape
    slab = jnp.concatenate([part.reshape(planes * voxels, chans) for part in taps], axis=-1)
    columns = jnp.concatenate([weights[(3 * n + k) * chans : (3 * n + k + 1) * chans] for n in offsets], axis=0)
    part = jnp.dot(slab, columns, preferred_element_type=jnp.float32)
    return part.reshape(planes, voxels, chans)


def convolve(taps, weights, width):
    return sum(shifted(product(taps, weights, range(9), k), k, width) for k in (1, 0, 2))


def edges(sources, targets, weights, width):
    total = None
    for k in (1, 0, 2):
        sums = [None] * 4
        for i in range(3):
            part = product(sources[i], weights, range(3 * i, 3 * i + 3), k)
            for plane, target in enumerate(targets[i]):
                piece = part[plane : plane + 1]
                sums[target] = piece if sums[target] is None else sums[target] + piece
        part = shifted(jnp.concatenate(sums, axis=0), k, width)
        total = part if total is None else total + part
    return total


def planes_at(even, odd, start, count, width):
    voxels = even.shape[1]
    return [
        even[start : start + count] if j == 1 else odd[start : start + count, j * width : j * width + voxels]
        for j in range(3)
    ]


def own_planes(width, p, q, weights, inner, partial, even, odd, ready=None):
    planes = q.shape[0]
    fill(even, odd, 0, q[...], width)
    if ready is not None:
        ready.wait()
    taps = [part for i in range(3) for part in planes_at(even, odd, i, planes - 2, width)]
    inner[...] = (p[1:-1].astype(jnp.float32) + convolve(taps, weights, width)).astype(inner.dtype)
    own = lambda plane: planes_at(even, odd, plane, 1, width)
    pair = lambda one, other: [jnp.concatenate(both, axis=0) for both in zip(own(one), own(other))]
    sources = (pair(planes - 2, planes - 1), pair(0, planes - 1), pair(0, 1))
    partial[...] = edges(sources, ((2, 3), (1, 2), (0, 1)), weights, width)


def inner_kernel(width, p, q, weights, inner, partial, even, odd):
    own_planes(width, p, q, weights, inner, partial, even, odd)


def loading_kernel(width, p, q, weights_hbm, inner, partial, weights, even, odd, sem):
    copy = pltpu.make_async_copy(weights_hbm, weights, sem)
    copy.start()
    own_planes(width, p, q, weights, inner, partial, even, odd, copy)


def edge_kernel(width, flags, p, inner, partial, near, far, weights, low, mid, high, even, odd):
    planes = p.shape[0]
    above = flags[2] > 0
    near, far = near[...].astype(jnp.float32), far[...].astype(jnp.float32)
    below, beyond = jnp.where(above, far, near), jnp.where(above, near, far)
    fill(even, odd, 0, below[:2], width)
    fill(even, odd, 2, beyond[:2], width)
    sources = [planes_at(even, odd, start, 2, width) for start in range(3)]
    total = partial[...] + edges(sources, ((0, 1), (0, 3), (2, 3)), weights, width)
    low[...] = jnp.where(flags[0] > 0, below[2:] + total[:1], 0.0).astype(low.dtype)
    mid[pl.ds(0, 1)] = (p[:1].astype(jnp.float32) + total[1:2]).astype(mid.dtype)
    mid[pl.ds(1, planes - 2)] = inner[...]
    mid[pl.ds(planes - 1, 1)] = (p[-1:].astype(jnp.float32) + total[2:3]).astype(mid.dtype)
    high[...] = jnp.where(flags[1] > 0, beyond[2:] + total[3:], 0.0).astype(high.dtype)


def second_sum(width, first_low, first_mid, first_high, q, weights, even, odd):
    planes = q.shape[0]
    fill(even, odd, 0, first_low[...], width)
    fill(even, odd, 1, first_mid[...], width)
    fill(even, odd, 1 + planes, first_high[...], width)
    taps = [part for i in range(3) for part in planes_at(even, odd, i, planes, width)]
    return q[...].astype(jnp.float32) + convolve(taps, weights, width)


def second_kernel(width, first_low, first_mid, first_high, q, weights, out, even, odd):
    out[...] = second_sum(width, first_low, first_mid, first_high, q, weights, even, odd).astype(out.dtype)


def last_kernel(width, first_low, first_mid, first_high, q, weights, out, even, odd, second, first_sem, second_sem):
    first_copy = pltpu.make_async_copy(first_mid, out.at[0], first_sem)
    first_copy.start()
    second[...] = second_sum(width, first_low, first_mid, first_high, q, weights, even, odd).astype(second.dtype)
    second_copy = pltpu.make_async_copy(second, out.at[1], second_sem)
    second_copy.start()
    first_copy.wait()
    second_copy.wait()


def call(kernel, outputs, scratch, arguments, width):
    specs = [pl.BlockSpec(memory_space=pltpu.VMEM) for _ in arguments]
    if kernel is edge_kernel:
        specs[0] = pl.BlockSpec(memory_space=pltpu.SMEM)
    if kernel is loading_kernel:
        specs[-1] = pl.BlockSpec(memory_space=pltpu.HBM)
    return pl.pallas_call(
        functools.partial(kernel, width),
        out_shape=[jax.ShapeDtypeStruct(shape, dtype) for shape, dtype in outputs],
        in_specs=specs,
        out_specs=[pl.BlockSpec(memory_space=pltpu.HBM if kernel is last_kernel else pltpu.VMEM) for _ in outputs],
        scratch_shapes=[pltpu.VMEM(shape, jnp.bfloat16) if shape else pltpu.SemaphoreType.DMA for shape in scratch],
        compiler_params=pltpu.CompilerParams(vmem_limit_bytes=VMEM_LIMIT),
        cost_estimate=pl.CostEstimate(flops=1, bytes_accessed=1, transcendentals=0),
    )(*arguments)


def stored(planes, voxels, chans, width):
    return (planes, voxels, chans), (planes, voxels + 2 * width, chans)


def inner_half(p, q, weights, width, load):
    planes, voxels, chans = q.shape
    outputs = [((planes - 2, voxels, chans), jnp.bfloat16), ((4, voxels, chans), jnp.float32)]
    scratch = stored(planes, voxels, chans, width)
    if load:
        weights = pltpu.with_memory_space_constraint(weights, pltpu.HBM)
        outputs.append((weights.shape, jnp.bfloat16))
        return call(loading_kernel, outputs, [*scratch, ()], (p, q, weights), width)
    return *call(inner_kernel, outputs, scratch, (p, q, weights), width), weights


def first_half(flags, p, kept, halos, weights, width):
    planes, voxels, chans = p.shape
    return call(
        edge_kernel,
        [((n, voxels, chans), jnp.bfloat16) for n in (1, planes, 1)],
        stored(4, voxels, chans, width),
        (flags, p, *kept, *halos, weights),
        width,
    )


def second_half(first, q, weights, width, last):
    shape = q.shape
    scratch = stored(shape[0] + 2, *shape[1:], width)
    output = shape
    if last:
        scratch, output = [*scratch, shape, (), ()], (2, *shape)
    (out,) = call(last_kernel if last else second_kernel, [(output, jnp.bfloat16)], scratch, (*first, q, weights), width)
    return out


def swap(turn, starts, *blocks):
    count = lax.axis_size("depth")
    parts = [lax.dynamic_slice_in_dim(block, starts[n][turn], n, axis=0) for block, n in blocks]
    pairs = [pair for i in range(turn, count - 1, 2) for pair in ((i, i + 1), (i + 1, i))]
    return lax.ppermute(jnp.concatenate(parts, axis=0), "depth", pairs)


def local(resident, previous, incoming, first_weights, second_weights):
    section = lax.axis_index("section")
    sections = lax.axis_size("section")
    half = sections // 2
    depth = lax.axis_index("depth")
    ticks = incoming.shape[0] + 1
    _, _, planes, rows, width, chans = resident.shape
    voxels = rows * width
    across = [(j, sections - 1 - j) for j in range(1, half - 1)]

    above = depth % 2 == 0
    places = {
        "flags": jnp.stack([depth > 0, depth < lax.axis_size("depth") - 1, above]).astype(jnp.int32),
        "starts": {
            n: (jnp.where(above, planes - n, 0), jnp.where(above, 0, planes - n)) for n in (1, 2)
        },
        "first": section == 0,
        "second": section == 1,
        "last": section == sections - 1,
        "decoder": section >= half,
        "direct": (section > half) & (section < sections - 1) if across else (),
    }
    places, resident, previous, incoming, first_weights, second_weights = lax.optimization_barrier(
        (places, resident, previous, incoming, first_weights, second_weights)
    )
    flags, starts = places["flags"], places["starts"]

    flat = lambda a: a.reshape(a.shape[0], 2, planes, voxels, chans)
    resident, previous, incoming = flat(resident)[0], flat(previous)[0], flat(incoming)
    w_one = first_weights.reshape(27 * chans, chans)
    w_two = second_weights.reshape(27 * chans, chans)

    def send(block, pairs):
        return lax.ppermute(block, "section", pairs) if pairs else block

    def join(held, skip):
        total = (held.astype(jnp.float32) + skip.astype(jnp.float32)).astype(jnp.bfloat16)
        return jnp.where(places["decoder"], total, held)

    newer, older, relayed, direct = {}, {}, {}, {}

    def arrived(slot, stream):
        fresh = incoming[min(slot, ticks - 1) - 1, stream]
        if slot == 1:
            return jnp.where(places["first"], fresh, join(resident[stream], mirrored[stream]))
        held = jnp.where(places["second"], older[stream], newer[stream])
        skip = jnp.where(places["last"], relayed[stream], newer[stream])
        if across:
            skip = jnp.where(places["direct"], direct[stream], skip)
        return jnp.where(places["first"], fresh, join(held, skip))

    p, q = resident
    mirrored = send(previous, [(j, sections - 1 - j) for j in range(half)])
    near, far = (swap(turn, starts, (q, 2), (p, 1)) for turn in range(2))
    for slot in range(ticks + 1):
        if slot == 1:
            p, q, near, far = following
        elif slot > 1:
            p = arrived(slot, 0)
            p, newer[1] = lax.optimization_barrier((p, newer[1]))
            q = arrived(slot, 1)
            near, far = (swap(turn, starts, (q, 2), (p, 1)) for turn in range(2))
        *kept, w_one = inner_half(p, q, w_one, width, slot == 0)
        onward = [(j, j + 1) for j in range(1, sections - 1)] if slot > 0 else []
        if slot < ticks - 1:
            onward = [(0, 1)] + onward
        received, relays = {}, {}
        if 0 < slot < ticks:
            early = send(kept[0], onward)
        first = first_half(flags, p, kept, (near, far), w_one, width)
        if slot == 0:
            received[0] = send(first[1], onward)
        elif slot < ticks:
            late = send(jnp.concatenate([first[1][:1], first[1][-1:]], axis=0), onward)
        second = second_half(first, q, w_two, width, slot == ticks)
        if 0 < slot < ticks:
            relays[0] = send(newer[0], [(1, sections - 1)])
            if slot == 1:
                relays[0], second = lax.optimization_barrier((relays[0], second))
            early, second = lax.optimization_barrier((early, second))
            received[0] = jnp.concatenate([late[:1], early, late[1:]], axis=0)
        if slot < ticks:
            received[1] = send(second, onward)
        if slot == 0:
            mirrored, _ = lax.optimization_barrier((mirrored, second))
            following = arrived(1, 0), arrived(1, 1)
            following += tuple(swap(turn, starts, (following[1], 2), (following[0], 1)) for turn in range(2))
        elif slot < ticks:
            relay_q, second = lax.optimization_barrier((newer[1], second))
            relays[1] = send(relay_q, [(1, sections - 1)])
            if across:
                direct = {0: send(first[1], across), 1: send(second, across)}
        older, newer, relayed = newer, received, relays
    result = second
    return result.reshape(1, 2, planes, rows, width, chans)


def solution(mesh):
    in_specs = (
        P("section", None, "depth", None, None, None),
        P("section", None, "depth", None, None, None),
        P(None, None, "depth", None, None, None),
        P("section", None, None, None, None, None),
        P("section", None, None, None, None, None),
    )
    out_specs = P("section", None, "depth", None, None, None)
    return jax.shard_map(local, mesh=mesh, in_specs=in_specs, out_specs=out_specs, check_vma=False)
```

```python
import functools

import jax
import jax.numpy as jnp
from jax import lax
from jax.experimental import pallas as pl
from jax.experimental.pallas import tpu as pltpu
from jax.sharding import PartitionSpec as P

EPS = 1e-05
VMEM_LIMIT = 12 * 1024 * 1024


def act(values):
    values = values.astype(jnp.float32)
    scaled = values * lax.rsqrt(jnp.mean(values * values, axis=-1, keepdims=True) + EPS)
    return scaled * (0.5 + 0.5 * jnp.tanh(0.5 * scaled))


def fill(even, odd, at, values, width):
    planes, _, chans = values.shape
    field = act(values)
    edge = jnp.zeros((planes, width, chans), jnp.float32)
    even[pl.ds(at, planes)] = field.astype(jnp.bfloat16)
    odd[pl.ds(at, planes)] = jnp.concatenate([edge, field, edge], axis=1).astype(jnp.bfloat16)


def shifted(part, k, width):
    planes, voxels, chans = part.shape
    part = part.reshape(-1, width, chans)
    column = lax.broadcasted_iota(jnp.int32, part.shape, 1)
    if k == 0:
        part = jnp.where(column == 0, 0.0, pltpu.roll(part, 1, 1))
    elif k == 2:
        part = jnp.where(column == width - 1, 0.0, pltpu.roll(part, width - 1, 1))
    return part.reshape(planes, voxels, chans)


def product(taps, weights, offsets, k):
    planes, voxels, chans = taps[0].shape
    slab = jnp.concatenate([part.reshape(planes * voxels, chans) for part in taps], axis=-1)
    columns = jnp.concatenate([weights[(3 * n + k) * chans : (3 * n + k + 1) * chans] for n in offsets], axis=0)
    part = jnp.dot(slab, columns, preferred_element_type=jnp.float32)
    return part.reshape(planes, voxels, chans)


def convolve(taps, weights, width):
    return sum(shifted(product(taps, weights, range(9), k), k, width) for k in (1, 0, 2))


def edges(sources, targets, weights, width):
    total = None
    for k in (1, 0, 2):
        sums = [None] * 4
        for i in range(3):
            part = product(sources[i], weights, range(3 * i, 3 * i + 3), k)
            for plane, target in enumerate(targets[i]):
                piece = part[plane : plane + 1]
                sums[target] = piece if sums[target] is None else sums[target] + piece
        part = shifted(jnp.concatenate(sums, axis=0), k, width)
        total = part if total is None else total + part
    return total


def planes_at(even, odd, start, count, width):
    voxels = even.shape[1]
    return [
        even[start : start + count] if j == 1 else odd[start : start + count, j * width : j * width + voxels]
        for j in range(3)
    ]


def own_planes(width, p, q, weights, inner, partial, even, odd, ready=None):
    planes = q.shape[0]
    fill(even, odd, 0, q[...], width)
    if ready is not None:
        ready.wait()
    taps = [part for i in range(3) for part in planes_at(even, odd, i, planes - 2, width)]
    inner[...] = (p[1:-1].astype(jnp.float32) + convolve(taps, weights, width)).astype(inner.dtype)
    own = lambda plane: planes_at(even, odd, plane, 1, width)
    pair = lambda one, other: [jnp.concatenate(both, axis=0) for both in zip(own(one), own(other))]
    sources = (pair(planes - 2, planes - 1), pair(0, planes - 1), pair(0, 1))
    partial[...] = edges(sources, ((2, 3), (1, 2), (0, 1)), weights, width)


def inner_kernel(width, p, q, weights, inner, partial, even, odd):
    own_planes(width, p, q, weights, inner, partial, even, odd)


def loading_kernel(width, p, q, weights_hbm, inner, partial, weights, even, odd, sem):
    copy = pltpu.make_async_copy(weights_hbm, weights, sem)
    copy.start()
    own_planes(width, p, q, weights, inner, partial, even, odd, copy)


def edge_kernel(width, flags, p, inner, partial, near, far, weights, low, mid, high, even, odd):
    planes = p.shape[0]
    above = flags[2] > 0
    near, far = near[...].astype(jnp.float32), far[...].astype(jnp.float32)
    below, beyond = jnp.where(above, far, near), jnp.where(above, near, far)
    fill(even, odd, 0, below[:2], width)
    fill(even, odd, 2, beyond[:2], width)
    sources = [planes_at(even, odd, start, 2, width) for start in range(3)]
    total = partial[...] + edges(sources, ((0, 1), (0, 3), (2, 3)), weights, width)
    low[...] = jnp.where(flags[0] > 0, below[2:] + total[:1], 0.0).astype(low.dtype)
    mid[pl.ds(0, 1)] = (p[:1].astype(jnp.float32) + total[1:2]).astype(mid.dtype)
    mid[pl.ds(1, planes - 2)] = inner[...]
    mid[pl.ds(planes - 1, 1)] = (p[-1:].astype(jnp.float32) + total[2:3]).astype(mid.dtype)
    high[...] = jnp.where(flags[1] > 0, beyond[2:] + total[3:], 0.0).astype(high.dtype)


def second_sum(width, first_low, first_mid, first_high, q, weights, even, odd):
    planes = q.shape[0]
    fill(even, odd, 0, first_low[...], width)
    fill(even, odd, 1, first_mid[...], width)
    fill(even, odd, 1 + planes, first_high[...], width)
    taps = [part for i in range(3) for part in planes_at(even, odd, i, planes, width)]
    return q[...].astype(jnp.float32) + convolve(taps, weights, width)


def second_kernel(width, first_low, first_mid, first_high, q, weights, out, even, odd):
    out[...] = second_sum(width, first_low, first_mid, first_high, q, weights, even, odd).astype(out.dtype)


def last_kernel(width, first_low, first_mid, first_high, q, weights, out, even, odd, second, first_sem, second_sem):
    first_copy = pltpu.make_async_copy(first_mid, out.at[0], first_sem)
    first_copy.start()
    second[...] = second_sum(width, first_low, first_mid, first_high, q, weights, even, odd).astype(second.dtype)
    second_copy = pltpu.make_async_copy(second, out.at[1], second_sem)
    second_copy.start()
    first_copy.wait()
    second_copy.wait()


def call(kernel, outputs, scratch, arguments, width):
    specs = [pl.BlockSpec(memory_space=pltpu.VMEM) for _ in arguments]
    if kernel is edge_kernel:
        specs[0] = pl.BlockSpec(memory_space=pltpu.SMEM)
    if kernel is loading_kernel:
        specs[-1] = pl.BlockSpec(memory_space=pltpu.HBM)
    return pl.pallas_call(
        functools.partial(kernel, width),
        out_shape=[jax.ShapeDtypeStruct(shape, dtype) for shape, dtype in outputs],
        in_specs=specs,
        out_specs=[pl.BlockSpec(memory_space=pltpu.HBM if kernel is last_kernel else pltpu.VMEM) for _ in outputs],
        scratch_shapes=[pltpu.VMEM(shape, jnp.bfloat16) if shape else pltpu.SemaphoreType.DMA for shape in scratch],
        compiler_params=pltpu.CompilerParams(vmem_limit_bytes=VMEM_LIMIT),
        cost_estimate=pl.CostEstimate(flops=1, bytes_accessed=1, transcendentals=0),
    )(*arguments)


def stored(planes, voxels, chans, width):
    return (planes, voxels, chans), (planes, voxels + 2 * width, chans)


def inner_half(p, q, weights, width, load):
    planes, voxels, chans = q.shape
    outputs = [((planes - 2, voxels, chans), jnp.bfloat16), ((4, voxels, chans), jnp.float32)]
    scratch = stored(planes, voxels, chans, width)
    if load:
        weights = pltpu.with_memory_space_constraint(weights, pltpu.HBM)
        outputs.append((weights.shape, jnp.bfloat16))
        return call(loading_kernel, outputs, [*scratch, ()], (p, q, weights), width)
    return *call(inner_kernel, outputs, scratch, (p, q, weights), width), weights


def first_half(flags, p, kept, halos, weights, width):
    planes, voxels, chans = p.shape
    return call(
        edge_kernel,
        [((n, voxels, chans), jnp.bfloat16) for n in (1, planes, 1)],
        stored(4, voxels, chans, width),
        (flags, p, *kept, *halos, weights),
        width,
    )


def second_half(first, q, weights, width, last):
    shape = q.shape
    scratch = stored(shape[0] + 2, *shape[1:], width)
    output = shape
    if last:
        scratch, output = [*scratch, shape, (), ()], (2, *shape)
    (out,) = call(last_kernel if last else second_kernel, [(output, jnp.bfloat16)], scratch, (*first, q, weights), width)
    return out


def swap(turn, starts, *blocks):
    count = lax.axis_size("depth")
    parts = [lax.dynamic_slice_in_dim(block, starts[n][turn], n, axis=0) for block, n in blocks]
    pairs = [pair for i in range(turn, count - 1, 2) for pair in ((i, i + 1), (i + 1, i))]
    return lax.ppermute(jnp.concatenate(parts, axis=0), "depth", pairs)


def local(resident, previous, incoming, first_weights, second_weights):
    section = lax.axis_index("section")
    sections = lax.axis_size("section")
    half = sections // 2
    depth = lax.axis_index("depth")
    ticks = incoming.shape[0] + 1
    _, _, planes, rows, width, chans = resident.shape
    voxels = rows * width
    across = [(j, sections - 1 - j) for j in range(1, half - 1)]

    above = depth % 2 == 0
    places = {
        "flags": jnp.stack([depth > 0, depth < lax.axis_size("depth") - 1, above]).astype(jnp.int32),
        "starts": {
            n: (jnp.where(above, planes - n, 0), jnp.where(above, 0, planes - n)) for n in (1, 2)
        },
        "first": section == 0,
        "second": section == 1,
        "last": section == sections - 1,
        "decoder": section >= half,
        "direct": (section > half) & (section < sections - 1) if across else (),
    }
    places, resident, previous, incoming, first_weights, second_weights = lax.optimization_barrier(
        (places, resident, previous, incoming, first_weights, second_weights)
    )
    flags, starts = places["flags"], places["starts"]

    flat = lambda a: a.reshape(a.shape[0], 2, planes, voxels, chans)
    resident, previous, incoming = flat(resident)[0], flat(previous)[0], flat(incoming)
    w_one = first_weights.reshape(27 * chans, chans)
    w_two = second_weights.reshape(27 * chans, chans)

    def send(block, pairs):
        return lax.ppermute(block, "section", pairs) if pairs else block

    def join(held, skip):
        total = (held.astype(jnp.float32) + skip.astype(jnp.float32)).astype(jnp.bfloat16)
        return jnp.where(places["decoder"], total, held)

    newer, older, relayed, direct = {}, {}, {}, {}

    def arrived(slot, stream):
        fresh = incoming[min(slot, ticks - 1) - 1, stream]
        if slot == 1:
            return jnp.where(places["first"], fresh, join(resident[stream], mirrored[stream]))
        held = jnp.where(places["second"], older[stream], newer[stream])
        skip = jnp.where(places["last"], relayed[stream], newer[stream])
        if across:
            skip = jnp.where(places["direct"], direct[stream], skip)
        return jnp.where(places["first"], fresh, join(held, skip))

    p, q = resident
    mirrored = send(previous, [(j, sections - 1 - j) for j in range(half)])
    near, far = (swap(turn, starts, (q, 2), (p, 1)) for turn in range(2))
    for slot in range(ticks + 1):
        if slot == 1:
            p, q, near, far = following
        elif slot > 1:
            p = arrived(slot, 0)
            p, newer[1] = lax.optimization_barrier((p, newer[1]))
            q = arrived(slot, 1)
            near, far = (swap(turn, starts, (q, 2), (p, 1)) for turn in range(2))
        *kept, w_one = inner_half(p, q, w_one, width, slot == 0)
        first = first_half(flags, p, kept, (near, far), w_one, width)
        onward = [(j, j + 1) for j in range(1, sections - 1)] if slot > 0 else []
        if slot < ticks - 1:
            onward = [(0, 1)] + onward
        received, relays = {}, {}
        if slot < ticks:
            received[0] = send(first[1], onward)
        second = second_half(first, q, w_two, width, slot == ticks)
        if slot < ticks:
            received[1] = send(second, onward)
        if slot == 0:
            mirrored, _ = lax.optimization_barrier((mirrored, second))
            following = arrived(1, 0), arrived(1, 1)
            following += tuple(swap(turn, starts, (following[1], 2), (following[0], 1)) for turn in range(2))
        elif slot < ticks:
            relay_q, second = lax.optimization_barrier((newer[1], second))
            relays = {0: send(newer[0], [(1, sections - 1)]), 1: send(relay_q, [(1, sections - 1)])}
            if across:
                direct = {0: send(first[1], across), 1: send(second, across)}
        older, newer, relayed = newer, received, relays
    result = second
    return result.reshape(1, 2, planes, rows, width, chans)


def solution(mesh):
    in_specs = (
        P("section", None, "depth", None, None, None),
        P("section", None, "depth", None, None, None),
        P(None, None, "depth", None, None, None),
        P("section", None, None, None, None, None),
        P("section", None, None, None, None, None),
    )
    out_specs = P("section", None, "depth", None, None, None)
    return jax.shard_map(local, mesh=mesh, in_specs=in_specs, out_specs=out_specs, check_vma=False)
```

```python
import functools

import jax
import jax.numpy as jnp
from jax import lax
from jax.experimental import pallas as pl
from jax.experimental.pallas import tpu as pltpu
from jax.sharding import PartitionSpec as P

EPS = 1e-05
VMEM_LIMIT = 12 * 1024 * 1024


def act(values):
    values = values.astype(jnp.float32)
    scaled = values * lax.rsqrt(jnp.mean(values * values, axis=-1, keepdims=True) + EPS)
    return scaled * (0.5 + 0.5 * jnp.tanh(0.5 * scaled))


def fill(even, odd, at, values, width):
    planes, _, chans = values.shape
    field = act(values)
    edge = jnp.zeros((planes, width, chans), jnp.float32)
    even[pl.ds(at, planes)] = field.astype(jnp.bfloat16)
    odd[pl.ds(at, planes)] = jnp.concatenate([edge, field, edge], axis=1).astype(jnp.bfloat16)


def shifted(part, k, width):
    planes, voxels, chans = part.shape
    part = part.reshape(-1, width, chans)
    column = lax.broadcasted_iota(jnp.int32, part.shape, 1)
    if k == 0:
        part = jnp.where(column == 0, 0.0, pltpu.roll(part, 1, 1))
    elif k == 2:
        part = jnp.where(column == width - 1, 0.0, pltpu.roll(part, width - 1, 1))
    return part.reshape(planes, voxels, chans)


def product(taps, weights, offsets, k):
    planes, voxels, chans = taps[0].shape
    slab = jnp.concatenate([part.reshape(planes * voxels, chans) for part in taps], axis=-1)
    columns = jnp.concatenate([weights[(3 * n + k) * chans : (3 * n + k + 1) * chans] for n in offsets], axis=0)
    part = jnp.dot(slab, columns, preferred_element_type=jnp.float32)
    return part.reshape(planes, voxels, chans)


def convolve(taps, weights, width):
    return sum(shifted(product(taps, weights, range(9), k), k, width) for k in (1, 0, 2))


def edges(sources, targets, weights, width):
    total = None
    for k in (1, 0, 2):
        sums = [None] * 4
        for i in range(3):
            part = product(sources[i], weights, range(3 * i, 3 * i + 3), k)
            for plane, target in enumerate(targets[i]):
                piece = part[plane : plane + 1]
                sums[target] = piece if sums[target] is None else sums[target] + piece
        part = shifted(jnp.concatenate(sums, axis=0), k, width)
        total = part if total is None else total + part
    return total


def planes_at(even, odd, start, count, width):
    voxels = even.shape[1]
    return [
        even[start : start + count] if j == 1 else odd[start : start + count, j * width : j * width + voxels]
        for j in range(3)
    ]


def own_planes(width, p, q, weights, inner, partial, even, odd, ready=None):
    planes = q.shape[0]
    fill(even, odd, 0, q[...], width)
    if ready is not None:
        ready.wait()
    taps = [part for i in range(3) for part in planes_at(even, odd, i, planes - 2, width)]
    inner[...] = (p[1:-1].astype(jnp.float32) + convolve(taps, weights, width)).astype(inner.dtype)
    own = lambda plane: planes_at(even, odd, plane, 1, width)
    pair = lambda one, other: [jnp.concatenate(both, axis=0) for both in zip(own(one), own(other))]
    sources = (pair(planes - 2, planes - 1), pair(0, planes - 1), pair(0, 1))
    partial[...] = edges(sources, ((2, 3), (1, 2), (0, 1)), weights, width)


def inner_kernel(width, p, q, weights, inner, partial, even, odd):
    own_planes(width, p, q, weights, inner, partial, even, odd)


def loading_kernel(width, p, q, weights_hbm, inner, partial, weights, even, odd, sem):
    copy = pltpu.make_async_copy(weights_hbm, weights, sem)
    copy.start()
    own_planes(width, p, q, weights, inner, partial, even, odd, copy)


def edge_kernel(width, flags, p, inner, partial, near, far, weights, low, mid, high, even, odd):
    planes = p.shape[0]
    above = flags[2] > 0
    near, far = near[...].astype(jnp.float32), far[...].astype(jnp.float32)
    below, beyond = jnp.where(above, far, near), jnp.where(above, near, far)
    fill(even, odd, 0, below[:2], width)
    fill(even, odd, 2, beyond[:2], width)
    sources = [planes_at(even, odd, start, 2, width) for start in range(3)]
    total = partial[...] + edges(sources, ((0, 1), (0, 3), (2, 3)), weights, width)
    low[...] = jnp.where(flags[0] > 0, below[2:] + total[:1], 0.0).astype(low.dtype)
    mid[pl.ds(0, 1)] = (p[:1].astype(jnp.float32) + total[1:2]).astype(mid.dtype)
    mid[pl.ds(1, planes - 2)] = inner[...]
    mid[pl.ds(planes - 1, 1)] = (p[-1:].astype(jnp.float32) + total[2:3]).astype(mid.dtype)
    high[...] = jnp.where(flags[1] > 0, beyond[2:] + total[3:], 0.0).astype(high.dtype)


def second_sum(width, first_low, first_mid, first_high, q, weights, even, odd):
    planes = q.shape[0]
    fill(even, odd, 0, first_low[...], width)
    fill(even, odd, 1, first_mid[...], width)
    fill(even, odd, 1 + planes, first_high[...], width)
    taps = [part for i in range(3) for part in planes_at(even, odd, i, planes, width)]
    return q[...].astype(jnp.float32) + convolve(taps, weights, width)


def second_kernel(width, first_low, first_mid, first_high, q, weights, out, even, odd):
    out[...] = second_sum(width, first_low, first_mid, first_high, q, weights, even, odd).astype(out.dtype)


def last_kernel(width, first_low, first_mid, first_high, q, weights, out, even, odd, second, first_sem, second_sem):
    first_copy = pltpu.make_async_copy(first_mid, out.at[0], first_sem)
    first_copy.start()
    second[...] = second_sum(width, first_low, first_mid, first_high, q, weights, even, odd).astype(second.dtype)
    second_copy = pltpu.make_async_copy(second, out.at[1], second_sem)
    second_copy.start()
    first_copy.wait()
    second_copy.wait()


def call(kernel, outputs, scratch, arguments, width):
    specs = [pl.BlockSpec(memory_space=pltpu.VMEM) for _ in arguments]
    if kernel is edge_kernel:
        specs[0] = pl.BlockSpec(memory_space=pltpu.SMEM)
    if kernel is loading_kernel:
        specs[-1] = pl.BlockSpec(memory_space=pltpu.HBM)
    return pl.pallas_call(
        functools.partial(kernel, width),
        out_shape=[jax.ShapeDtypeStruct(shape, dtype) for shape, dtype in outputs],
        in_specs=specs,
        out_specs=[pl.BlockSpec(memory_space=pltpu.HBM if kernel is last_kernel else pltpu.VMEM) for _ in outputs],
        scratch_shapes=[pltpu.VMEM(shape, jnp.bfloat16) if shape else pltpu.SemaphoreType.DMA for shape in scratch],
        compiler_params=pltpu.CompilerParams(vmem_limit_bytes=VMEM_LIMIT),
        cost_estimate=pl.CostEstimate(flops=1, bytes_accessed=1, transcendentals=0),
    )(*arguments)


def stored(planes, voxels, chans, width):
    return (planes, voxels, chans), (planes, voxels + 2 * width, chans)


def inner_half(p, q, weights, width, load):
    planes, voxels, chans = q.shape
    outputs = [((planes - 2, voxels, chans), jnp.bfloat16), ((4, voxels, chans), jnp.float32)]
    scratch = stored(planes, voxels, chans, width)
    if load:
        weights = pltpu.with_memory_space_constraint(weights, pltpu.HBM)
        outputs.append((weights.shape, jnp.bfloat16))
        return call(loading_kernel, outputs, [*scratch, ()], (p, q, weights), width)
    return *call(inner_kernel, outputs, scratch, (p, q, weights), width), weights


def first_half(flags, p, kept, halos, weights, width):
    planes, voxels, chans = p.shape
    return call(
        edge_kernel,
        [((n, voxels, chans), jnp.bfloat16) for n in (1, planes, 1)],
        stored(4, voxels, chans, width),
        (flags, p, *kept, *halos, weights),
        width,
    )


def second_half(first, q, weights, width, last):
    shape = q.shape
    scratch = stored(shape[0] + 2, *shape[1:], width)
    output = shape
    if last:
        scratch, output = [*scratch, shape, (), ()], (2, *shape)
    (out,) = call(last_kernel if last else second_kernel, [(output, jnp.bfloat16)], scratch, (*first, q, weights), width)
    return out


def swap(turn, starts, *blocks):
    count = lax.axis_size("depth")
    parts = [lax.dynamic_slice_in_dim(block, starts[n][turn], n, axis=0) for block, n in blocks]
    pairs = [pair for i in range(turn, count - 1, 2) for pair in ((i, i + 1), (i + 1, i))]
    return lax.ppermute(jnp.concatenate(parts, axis=0), "depth", pairs)


def local(resident, previous, incoming, first_weights, second_weights):
    section = lax.axis_index("section")
    sections = lax.axis_size("section")
    half = sections // 2
    depth = lax.axis_index("depth")
    ticks = incoming.shape[0] + 1
    _, _, planes, rows, width, chans = resident.shape
    voxels = rows * width
    across = [(j, sections - 1 - j) for j in range(1, half - 1)]

    above = depth % 2 == 0
    places = {
        "flags": jnp.stack([depth > 0, depth < lax.axis_size("depth") - 1, above]).astype(jnp.int32),
        "starts": {
            n: (jnp.where(above, planes - n, 0), jnp.where(above, 0, planes - n)) for n in (1, 2)
        },
        "first": section == 0,
        "second": section == 1,
        "last": section == sections - 1,
        "decoder": section >= half,
        "direct": (section > half) & (section < sections - 1) if across else (),
    }
    places, resident, previous, incoming, first_weights, second_weights = lax.optimization_barrier(
        (places, resident, previous, incoming, first_weights, second_weights)
    )
    flags, starts = places["flags"], places["starts"]

    flat = lambda a: a.reshape(a.shape[0], 2, planes, voxels, chans)
    resident, previous, incoming = flat(resident)[0], flat(previous)[0], flat(incoming)
    w_one = first_weights.reshape(27 * chans, chans)
    w_two = second_weights.reshape(27 * chans, chans)

    def send(block, pairs):
        return lax.ppermute(block, "section", pairs) if pairs else block

    def join(held, skip):
        total = (held.astype(jnp.float32) + skip.astype(jnp.float32)).astype(jnp.bfloat16)
        return jnp.where(places["decoder"], total, held)

    newer, older, relayed, direct = {}, {}, {}, {}

    def arrived(slot, stream):
        fresh = incoming[min(slot, ticks - 1) - 1, stream]
        if slot == 1:
            return jnp.where(places["first"], fresh, join(resident[stream], mirrored[stream]))
        held = jnp.where(places["second"], older[stream], newer[stream])
        skip = jnp.where(places["last"], relayed[stream], newer[stream])
        if across:
            skip = jnp.where(places["direct"], direct[stream], skip)
        return jnp.where(places["first"], fresh, join(held, skip))

    p, q = resident
    mirrored = send(previous, [(j, sections - 1 - j) for j in range(half)])
    near, far = (swap(turn, starts, (q, 2), (p, 1)) for turn in range(2))
    for slot in range(ticks + 1):
        if slot == 1:
            p, q, near, far = following
        elif slot > 1:
            p = arrived(slot, 0)
            p, newer[1] = lax.optimization_barrier((p, newer[1]))
            q = arrived(slot, 1)
            near, far = (swap(turn, starts, (q, 2), (p, 1)) for turn in range(2))
        *kept, w_one = inner_half(p, q, w_one, width, slot == 0)
        first = first_half(flags, p, kept, (near, far), w_one, width)
        onward = [(j, j + 1) for j in range(1, sections - 1)] if slot > 0 else []
        if slot < ticks - 1:
            onward = [(0, 1)] + onward
        received, relays = {}, {}
        if slot < ticks:
            received[0] = send(first[1], onward)
        second = second_half(first, q, w_two, width, slot == ticks)
        if slot < ticks:
            received[1] = send(second, onward)
        if slot == 0:
            mirrored, _ = lax.optimization_barrier((mirrored, second))
            following = arrived(1, 0), arrived(1, 1)
            following += tuple(swap(turn, starts, (following[1], 2), (following[0], 1)) for turn in range(2))
        elif slot < ticks:
            relay_p = newer[0]
            if slot == 1:
                relay_p, _ = lax.optimization_barrier((relay_p, first[1]))
            relay_q, second = lax.optimization_barrier((newer[1], second))
            relays = {0: send(relay_p, [(1, sections - 1)]), 1: send(relay_q, [(1, sections - 1)])}
            if across:
                direct = {0: send(first[1], across), 1: send(second, across)}
        older, newer, relayed = newer, received, relays
    result = second
    return result.reshape(1, 2, planes, rows, width, chans)


def solution(mesh):
    in_specs = (
        P("section", None, "depth", None, None, None),
        P("section", None, "depth", None, None, None),
        P(None, None, "depth", None, None, None),
        P("section", None, None, None, None, None),
        P("section", None, None, None, None, None),
    )
    out_specs = P("section", None, "depth", None, None, None)
    return jax.shard_map(local, mesh=mesh, in_specs=in_specs, out_specs=out_specs, check_vma=False)
```

```python
import functools

import jax
import jax.numpy as jnp
from jax import lax
from jax.experimental import pallas as pl
from jax.experimental.pallas import tpu as pltpu
from jax.sharding import PartitionSpec as P

EPS = 1e-05
VMEM_LIMIT = 12 * 1024 * 1024


def act(values):
    values = values.astype(jnp.float32)
    scaled = values * lax.rsqrt(jnp.mean(values * values, axis=-1, keepdims=True) + EPS)
    return scaled * (0.5 + 0.5 * jnp.tanh(0.5 * scaled))


def fill(even, odd, at, values, width):
    planes, _, chans = values.shape
    field = act(values)
    edge = jnp.zeros((planes, width, chans), jnp.float32)
    even[pl.ds(at, planes)] = field.astype(jnp.bfloat16)
    odd[pl.ds(at, planes)] = jnp.concatenate([edge, field, edge], axis=1).astype(jnp.bfloat16)


def shifted(part, k, width):
    planes, voxels, chans = part.shape
    part = part.reshape(-1, width, chans)
    column = lax.broadcasted_iota(jnp.int32, part.shape, 1)
    if k == 0:
        part = jnp.where(column == 0, 0.0, pltpu.roll(part, 1, 1))
    elif k == 2:
        part = jnp.where(column == width - 1, 0.0, pltpu.roll(part, width - 1, 1))
    return part.reshape(planes, voxels, chans)


def product(taps, weights, offsets, k):
    planes, voxels, chans = taps[0].shape
    slab = jnp.concatenate([part.reshape(planes * voxels, chans) for part in taps], axis=-1)
    columns = jnp.concatenate([weights[(3 * n + k) * chans : (3 * n + k + 1) * chans] for n in offsets], axis=0)
    part = jnp.dot(slab, columns, preferred_element_type=jnp.float32)
    return part.reshape(planes, voxels, chans)


def convolve(taps, weights, width):
    return sum(shifted(product(taps, weights, range(9), k), k, width) for k in (1, 0, 2))


def edges(sources, targets, weights, width):
    total = None
    for k in (1, 0, 2):
        sums = [None] * 4
        for i in range(3):
            part = product(sources[i], weights, range(3 * i, 3 * i + 3), k)
            for plane, target in enumerate(targets[i]):
                piece = part[plane : plane + 1]
                sums[target] = piece if sums[target] is None else sums[target] + piece
        part = shifted(jnp.concatenate(sums, axis=0), k, width)
        total = part if total is None else total + part
    return total


def planes_at(even, odd, start, count, width):
    voxels = even.shape[1]
    return [
        even[start : start + count] if j == 1 else odd[start : start + count, j * width : j * width + voxels]
        for j in range(3)
    ]


def own_planes(width, p, q, weights, inner, partial, even, odd, ready=None):
    planes = q.shape[0]
    fill(even, odd, 0, q[...], width)
    if ready is not None:
        ready.wait()
    taps = [part for i in range(3) for part in planes_at(even, odd, i, planes - 2, width)]
    inner[...] = (p[1:-1].astype(jnp.float32) + convolve(taps, weights, width)).astype(inner.dtype)
    own = lambda plane: planes_at(even, odd, plane, 1, width)
    pair = lambda one, other: [jnp.concatenate(both, axis=0) for both in zip(own(one), own(other))]
    sources = (pair(planes - 2, planes - 1), pair(0, planes - 1), pair(0, 1))
    partial[...] = edges(sources, ((2, 3), (1, 2), (0, 1)), weights, width)


def inner_kernel(width, p, q, weights, inner, partial, even, odd):
    own_planes(width, p, q, weights, inner, partial, even, odd)


def loading_kernel(width, p, q, weights_hbm, inner, partial, weights, even, odd, sem):
    copy = pltpu.make_async_copy(weights_hbm, weights, sem)
    copy.start()
    own_planes(width, p, q, weights, inner, partial, even, odd, copy)


def edge_kernel(width, flags, p, inner, partial, near, far, weights, low, mid, high, even, odd):
    planes = p.shape[0]
    above = flags[2] > 0
    near, far = near[...].astype(jnp.float32), far[...].astype(jnp.float32)
    below, beyond = jnp.where(above, far, near), jnp.where(above, near, far)
    fill(even, odd, 0, below[:2], width)
    fill(even, odd, 2, beyond[:2], width)
    sources = [planes_at(even, odd, start, 2, width) for start in range(3)]
    total = partial[...] + edges(sources, ((0, 1), (0, 3), (2, 3)), weights, width)
    low[...] = jnp.where(flags[0] > 0, below[2:] + total[:1], 0.0).astype(low.dtype)
    mid[pl.ds(0, 1)] = (p[:1].astype(jnp.float32) + total[1:2]).astype(mid.dtype)
    mid[pl.ds(1, planes - 2)] = inner[...]
    mid[pl.ds(planes - 1, 1)] = (p[-1:].astype(jnp.float32) + total[2:3]).astype(mid.dtype)
    high[...] = jnp.where(flags[1] > 0, beyond[2:] + total[3:], 0.0).astype(high.dtype)


def second_sum(width, first_low, first_mid, first_high, q, weights, even, odd):
    planes = q.shape[0]
    fill(even, odd, 0, first_low[...], width)
    fill(even, odd, 1, first_mid[...], width)
    fill(even, odd, 1 + planes, first_high[...], width)
    taps = [part for i in range(3) for part in planes_at(even, odd, i, planes, width)]
    return q[...].astype(jnp.float32) + convolve(taps, weights, width)


def second_kernel(width, first_low, first_mid, first_high, q, weights, out, even, odd):
    out[...] = second_sum(width, first_low, first_mid, first_high, q, weights, even, odd).astype(out.dtype)


def last_kernel(width, first_low, first_mid, first_high, q, weights, out, even, odd, second, first_sem, second_sem):
    first_copy = pltpu.make_async_copy(first_mid, out.at[0], first_sem)
    first_copy.start()
    second[...] = second_sum(width, first_low, first_mid, first_high, q, weights, even, odd).astype(second.dtype)
    second_copy = pltpu.make_async_copy(second, out.at[1], second_sem)
    second_copy.start()
    first_copy.wait()
    second_copy.wait()


def call(kernel, outputs, scratch, arguments, width):
    specs = [pl.BlockSpec(memory_space=pltpu.VMEM) for _ in arguments]
    if kernel is edge_kernel:
        specs[0] = pl.BlockSpec(memory_space=pltpu.SMEM)
    if kernel is loading_kernel:
        specs[-1] = pl.BlockSpec(memory_space=pltpu.HBM)
    return pl.pallas_call(
        functools.partial(kernel, width),
        out_shape=[jax.ShapeDtypeStruct(shape, dtype) for shape, dtype in outputs],
        in_specs=specs,
        out_specs=[pl.BlockSpec(memory_space=pltpu.HBM if kernel is last_kernel else pltpu.VMEM) for _ in outputs],
        scratch_shapes=[pltpu.VMEM(shape, jnp.bfloat16) if shape else pltpu.SemaphoreType.DMA for shape in scratch],
        compiler_params=pltpu.CompilerParams(vmem_limit_bytes=VMEM_LIMIT),
        cost_estimate=pl.CostEstimate(flops=1, bytes_accessed=1, transcendentals=0),
    )(*arguments)


def stored(planes, voxels, chans, width):
    return (planes, voxels, chans), (planes, voxels + 2 * width, chans)


def inner_half(p, q, weights, width, load):
    planes, voxels, chans = q.shape
    outputs = [((planes - 2, voxels, chans), jnp.bfloat16), ((4, voxels, chans), jnp.float32)]
    scratch = stored(planes, voxels, chans, width)
    if load:
        weights = pltpu.with_memory_space_constraint(weights, pltpu.HBM)
        outputs.append((weights.shape, jnp.bfloat16))
        return call(loading_kernel, outputs, [*scratch, ()], (p, q, weights), width)
    return *call(inner_kernel, outputs, scratch, (p, q, weights), width), weights


def first_half(flags, p, kept, halos, weights, width):
    planes, voxels, chans = p.shape
    return call(
        edge_kernel,
        [((n, voxels, chans), jnp.bfloat16) for n in (1, planes, 1)],
        stored(4, voxels, chans, width),
        (flags, p, *kept, *halos, weights),
        width,
    )


def second_half(first, q, weights, width, last):
    shape = q.shape
    scratch = stored(shape[0] + 2, *shape[1:], width)
    output = shape
    if last:
        scratch, output = [*scratch, shape, (), ()], (2, *shape)
    (out,) = call(last_kernel if last else second_kernel, [(output, jnp.bfloat16)], scratch, (*first, q, weights), width)
    return out


def swap(turn, starts, *blocks):
    count = lax.axis_size("depth")
    parts = [lax.dynamic_slice_in_dim(block, starts[n][turn], n, axis=0) for block, n in blocks]
    pairs = [pair for i in range(turn, count - 1, 2) for pair in ((i, i + 1), (i + 1, i))]
    return lax.ppermute(jnp.concatenate(parts, axis=0), "depth", pairs)


def local(resident, previous, incoming, first_weights, second_weights):
    section = lax.axis_index("section")
    sections = lax.axis_size("section")
    half = sections // 2
    depth = lax.axis_index("depth")
    ticks = incoming.shape[0] + 1
    _, _, planes, rows, width, chans = resident.shape
    voxels = rows * width
    across = [(j, sections - 1 - j) for j in range(1, half - 1)]

    above = depth % 2 == 0
    places = {
        "flags": jnp.stack([depth > 0, depth < lax.axis_size("depth") - 1, above]).astype(jnp.int32),
        "starts": {
            n: (jnp.where(above, planes - n, 0), jnp.where(above, 0, planes - n)) for n in (1, 2)
        },
        "first": section == 0,
        "second": section == 1,
        "last": section == sections - 1,
        "decoder": section >= half,
        "direct": (section > half) & (section < sections - 1) if across else (),
    }
    places, resident, previous, incoming, first_weights, second_weights = lax.optimization_barrier(
        (places, resident, previous, incoming, first_weights, second_weights)
    )
    flags, starts = places["flags"], places["starts"]

    flat = lambda a: a.reshape(a.shape[0], 2, planes, voxels, chans)
    resident, previous, incoming = flat(resident)[0], flat(previous)[0], flat(incoming)
    w_one = first_weights.reshape(27 * chans, chans)
    w_two = second_weights.reshape(27 * chans, chans)

    def send(block, pairs):
        return lax.ppermute(block, "section", pairs) if pairs else block

    def join(held, skip):
        total = (held.astype(jnp.float32) + skip.astype(jnp.float32)).astype(jnp.bfloat16)
        return jnp.where(places["decoder"], total, held)

    newer, older, relayed, direct = {}, {}, {}, {}

    def arrived(slot, stream):
        fresh = incoming[min(slot, ticks - 1) - 1, stream]
        if slot == 1:
            return jnp.where(places["first"], fresh, join(resident[stream], mirrored[stream]))
        held = jnp.where(places["second"], older[stream], newer[stream])
        skip = jnp.where(places["last"], relayed[stream], newer[stream])
        if across:
            skip = jnp.where(places["direct"], direct[stream], skip)
        return jnp.where(places["first"], fresh, join(held, skip))

    p, q = resident
    mirrored = send(previous, [(j, sections - 1 - j) for j in range(half)])
    near, far = (swap(turn, starts, (q, 2), (p, 1)) for turn in range(2))
    for slot in range(ticks + 1):
        if slot == 1:
            p, q, near, far = following
        elif slot > 1:
            p = arrived(slot, 0)
            p, newer[1] = lax.optimization_barrier((p, newer[1]))
            q = arrived(slot, 1)
            near, far = (swap(turn, starts, (q, 2), (p, 1)) for turn in range(2))
        *kept, w_one = inner_half(p, q, w_one, width, slot == 0)
        first = first_half(flags, p, kept, (near, far), w_one, width)
        onward = [(j, j + 1) for j in range(1, sections - 1)] if slot > 0 else []
        if slot < ticks - 1:
            onward = [(0, 1)] + onward
        received, relays = {}, {}
        if slot < ticks:
            received[0] = send(first[1], onward)
        second = second_half(first, q, w_two, width, slot == ticks)
        if 0 < slot < ticks:
            relay_p = send(newer[0], [(1, sections - 1)])
            if slot > 1:
                relay_p, second = lax.optimization_barrier((relay_p, second))
        if slot < ticks:
            received[1] = send(second, onward)
        if slot == 0:
            mirrored, _ = lax.optimization_barrier((mirrored, second))
            following = arrived(1, 0), arrived(1, 1)
            following += tuple(swap(turn, starts, (following[1], 2), (following[0], 1)) for turn in range(2))
        elif slot < ticks:
            relay_q, second = lax.optimization_barrier((newer[1], second))
            relays = {0: relay_p, 1: send(relay_q, [(1, sections - 1)])}
            if across:
                direct = {0: send(first[1], across), 1: send(second, across)}
        older, newer, relayed = newer, received, relays
    result = second
    return result.reshape(1, 2, planes, rows, width, chans)


def solution(mesh):
    in_specs = (
        P("section", None, "depth", None, None, None),
        P("section", None, "depth", None, None, None),
        P(None, None, "depth", None, None, None),
        P("section", None, None, None, None, None),
        P("section", None, None, None, None, None),
    )
    out_specs = P("section", None, "depth", None, None, None)
    return jax.shard_map(local, mesh=mesh, in_specs=in_specs, out_specs=out_specs, check_vma=False)
```

```python
import functools

import jax
import jax.numpy as jnp
from jax import lax
from jax.experimental import pallas as pl
from jax.experimental.pallas import tpu as pltpu
from jax.sharding import PartitionSpec as P

EPS = 1e-05
VMEM_LIMIT = 12 * 1024 * 1024


def act(values):
    values = values.astype(jnp.float32)
    scaled = values * lax.rsqrt(jnp.mean(values * values, axis=-1, keepdims=True) + EPS)
    return scaled * (0.5 + 0.5 * jnp.tanh(0.5 * scaled))


def fill(even, odd, at, values, width):
    planes, _, chans = values.shape
    field = act(values)
    edge = jnp.zeros((planes, width, chans), jnp.float32)
    even[pl.ds(at, planes)] = field.astype(jnp.bfloat16)
    odd[pl.ds(at, planes)] = jnp.concatenate([edge, field, edge], axis=1).astype(jnp.bfloat16)


def shifted(part, k, width):
    planes, voxels, chans = part.shape
    part = part.reshape(-1, width, chans)
    column = lax.broadcasted_iota(jnp.int32, part.shape, 1)
    if k == 0:
        part = jnp.where(column == 0, 0.0, pltpu.roll(part, 1, 1))
    elif k == 2:
        part = jnp.where(column == width - 1, 0.0, pltpu.roll(part, width - 1, 1))
    return part.reshape(planes, voxels, chans)


def product(taps, weights, offsets, k):
    planes, voxels, chans = taps[0].shape
    slab = jnp.concatenate([part.reshape(planes * voxels, chans) for part in taps], axis=-1)
    columns = jnp.concatenate([weights[(3 * n + k) * chans : (3 * n + k + 1) * chans] for n in offsets], axis=0)
    part = jnp.dot(slab, columns, preferred_element_type=jnp.float32)
    return part.reshape(planes, voxels, chans)


def convolve(taps, weights, width):
    return sum(shifted(product(taps, weights, range(9), k), k, width) for k in (1, 0, 2))


def edges(sources, targets, weights, width):
    total = None
    for k in (1, 0, 2):
        sums = [None] * 4
        for i in range(3):
            part = product(sources[i], weights, range(3 * i, 3 * i + 3), k)
            for plane, target in enumerate(targets[i]):
                piece = part[plane : plane + 1]
                sums[target] = piece if sums[target] is None else sums[target] + piece
        part = shifted(jnp.concatenate(sums, axis=0), k, width)
        total = part if total is None else total + part
    return total


def planes_at(even, odd, start, count, width):
    voxels = even.shape[1]
    return [
        even[start : start + count] if j == 1 else odd[start : start + count, j * width : j * width + voxels]
        for j in range(3)
    ]


def own_planes(width, p, q, weights, inner, partial, even, odd, ready=None):
    planes = q.shape[0]
    fill(even, odd, 0, q[...], width)
    if ready is not None:
        ready.wait()
    taps = [part for i in range(3) for part in planes_at(even, odd, i, planes - 2, width)]
    inner[...] = (p[1:-1].astype(jnp.float32) + convolve(taps, weights, width)).astype(inner.dtype)
    own = lambda plane: planes_at(even, odd, plane, 1, width)
    pair = lambda one, other: [jnp.concatenate(both, axis=0) for both in zip(own(one), own(other))]
    sources = (pair(planes - 2, planes - 1), pair(0, planes - 1), pair(0, 1))
    partial[...] = edges(sources, ((2, 3), (1, 2), (0, 1)), weights, width)


def inner_kernel(width, p, q, weights, inner, partial, even, odd):
    own_planes(width, p, q, weights, inner, partial, even, odd)


def loading_kernel(width, p, q, weights_hbm, inner, partial, weights, even, odd, sem):
    copy = pltpu.make_async_copy(weights_hbm, weights, sem)
    copy.start()
    own_planes(width, p, q, weights, inner, partial, even, odd, copy)


def edge_kernel(width, flags, p, inner, partial, near, far, weights, low, mid, high, even, odd):
    planes = p.shape[0]
    above = flags[2] > 0
    near, far = near[...].astype(jnp.float32), far[...].astype(jnp.float32)
    below, beyond = jnp.where(above, far, near), jnp.where(above, near, far)
    fill(even, odd, 0, below[:2], width)
    fill(even, odd, 2, beyond[:2], width)
    sources = [planes_at(even, odd, start, 2, width) for start in range(3)]
    total = partial[...] + edges(sources, ((0, 1), (0, 3), (2, 3)), weights, width)
    low[...] = jnp.where(flags[0] > 0, below[2:] + total[:1], 0.0).astype(low.dtype)
    mid[pl.ds(0, 1)] = (p[:1].astype(jnp.float32) + total[1:2]).astype(mid.dtype)
    mid[pl.ds(1, planes - 2)] = inner[...]
    mid[pl.ds(planes - 1, 1)] = (p[-1:].astype(jnp.float32) + total[2:3]).astype(mid.dtype)
    high[...] = jnp.where(flags[1] > 0, beyond[2:] + total[3:], 0.0).astype(high.dtype)


def second_sum(width, first_low, first_mid, first_high, q, weights, even, odd):
    planes = q.shape[0]
    fill(even, odd, 0, first_low[...], width)
    fill(even, odd, 1, first_mid[...], width)
    fill(even, odd, 1 + planes, first_high[...], width)
    taps = [part for i in range(3) for part in planes_at(even, odd, i, planes, width)]
    return q[...].astype(jnp.float32) + convolve(taps, weights, width)


def second_kernel(width, first_low, first_mid, first_high, q, weights, out, even, odd):
    out[...] = second_sum(width, first_low, first_mid, first_high, q, weights, even, odd).astype(out.dtype)


def last_kernel(width, first_low, first_mid, first_high, q, weights, out, even, odd, second, first_sem, low_sem, high_sem):
    first_copy = pltpu.make_async_copy(first_mid, out.at[0], first_sem)
    first_copy.start()
    planes = q.shape[0]
    fill(even, odd, 0, first_low[...], width)
    fill(even, odd, 1, first_mid[...], width)
    fill(even, odd, 1 + planes, first_high[...], width)
    half = planes // 2
    copies = [first_copy]
    for start, count, sem in ((0, half, low_sem), (half, planes - half, high_sem)):
        taps = [part for i in range(3) for part in planes_at(even, odd, start + i, count, width)]
        part = pl.ds(start, count)
        second[part] = (q[part].astype(jnp.float32) + convolve(taps, weights, width)).astype(second.dtype)
        copy = pltpu.make_async_copy(second.at[part], out.at[1, part], sem)
        copy.start()
        copies.append(copy)
    for copy in copies:
        copy.wait()


def call(kernel, outputs, scratch, arguments, width):
    specs = [pl.BlockSpec(memory_space=pltpu.VMEM) for _ in arguments]
    if kernel is edge_kernel:
        specs[0] = pl.BlockSpec(memory_space=pltpu.SMEM)
    if kernel is loading_kernel:
        specs[-1] = pl.BlockSpec(memory_space=pltpu.HBM)
    return pl.pallas_call(
        functools.partial(kernel, width),
        out_shape=[jax.ShapeDtypeStruct(shape, dtype) for shape, dtype in outputs],
        in_specs=specs,
        out_specs=[pl.BlockSpec(memory_space=pltpu.HBM if kernel is last_kernel else pltpu.VMEM) for _ in outputs],
        scratch_shapes=[pltpu.VMEM(shape, jnp.bfloat16) if shape else pltpu.SemaphoreType.DMA for shape in scratch],
        compiler_params=pltpu.CompilerParams(vmem_limit_bytes=VMEM_LIMIT),
        cost_estimate=pl.CostEstimate(flops=1, bytes_accessed=1, transcendentals=0),
    )(*arguments)


def stored(planes, voxels, chans, width):
    return (planes, voxels, chans), (planes, voxels + 2 * width, chans)


def inner_half(p, q, weights, width, load):
    planes, voxels, chans = q.shape
    outputs = [((planes - 2, voxels, chans), jnp.bfloat16), ((4, voxels, chans), jnp.float32)]
    scratch = stored(planes, voxels, chans, width)
    if load:
        weights = pltpu.with_memory_space_constraint(weights, pltpu.HBM)
        outputs.append((weights.shape, jnp.bfloat16))
        return call(loading_kernel, outputs, [*scratch, ()], (p, q, weights), width)
    return *call(inner_kernel, outputs, scratch, (p, q, weights), width), weights


def first_half(flags, p, kept, halos, weights, width):
    planes, voxels, chans = p.shape
    return call(
        edge_kernel,
        [((n, voxels, chans), jnp.bfloat16) for n in (1, planes, 1)],
        stored(4, voxels, chans, width),
        (flags, p, *kept, *halos, weights),
        width,
    )


def second_half(first, q, weights, width, last):
    shape = q.shape
    scratch = stored(shape[0] + 2, *shape[1:], width)
    output = shape
    if last:
        scratch, output = [*scratch, shape, (), (), ()], (2, *shape)
    (out,) = call(last_kernel if last else second_kernel, [(output, jnp.bfloat16)], scratch, (*first, q, weights), width)
    return out


def swap(turn, starts, *blocks):
    count = lax.axis_size("depth")
    parts = [lax.dynamic_slice_in_dim(block, starts[n][turn], n, axis=0) for block, n in blocks]
    pairs = [pair for i in range(turn, count - 1, 2) for pair in ((i, i + 1), (i + 1, i))]
    return lax.ppermute(jnp.concatenate(parts, axis=0), "depth", pairs)


def local(resident, previous, incoming, first_weights, second_weights):
    section = lax.axis_index("section")
    sections = lax.axis_size("section")
    half = sections // 2
    depth = lax.axis_index("depth")
    ticks = incoming.shape[0] + 1
    _, _, planes, rows, width, chans = resident.shape
    voxels = rows * width
    across = [(j, sections - 1 - j) for j in range(1, half - 1)]

    above = depth % 2 == 0
    places = {
        "flags": jnp.stack([depth > 0, depth < lax.axis_size("depth") - 1, above]).astype(jnp.int32),
        "starts": {
            n: (jnp.where(above, planes - n, 0), jnp.where(above, 0, planes - n)) for n in (1, 2)
        },
        "first": section == 0,
        "second": section == 1,
        "last": section == sections - 1,
        "decoder": section >= half,
        "direct": (section > half) & (section < sections - 1) if across else (),
    }
    places, resident, previous, incoming, first_weights, second_weights = lax.optimization_barrier(
        (places, resident, previous, incoming, first_weights, second_weights)
    )
    flags, starts = places["flags"], places["starts"]

    flat = lambda a: a.reshape(a.shape[0], 2, planes, voxels, chans)
    resident, previous, incoming = flat(resident)[0], flat(previous)[0], flat(incoming)
    w_one = first_weights.reshape(27 * chans, chans)
    w_two = second_weights.reshape(27 * chans, chans)

    def send(block, pairs):
        return lax.ppermute(block, "section", pairs) if pairs else block

    def join(held, skip):
        total = (held.astype(jnp.float32) + skip.astype(jnp.float32)).astype(jnp.bfloat16)
        return jnp.where(places["decoder"], total, held)

    newer, older, relayed, direct = {}, {}, {}, {}

    def arrived(slot, stream):
        fresh = incoming[min(slot, ticks - 1) - 1, stream]
        if slot == 1:
            return jnp.where(places["first"], fresh, join(resident[stream], mirrored[stream]))
        held = jnp.where(places["second"], older[stream], newer[stream])
        skip = jnp.where(places["last"], relayed[stream], newer[stream])
        if across:
            skip = jnp.where(places["direct"], direct[stream], skip)
        return jnp.where(places["first"], fresh, join(held, skip))

    p, q = resident
    mirrored = send(previous, [(j, sections - 1 - j) for j in range(half)])
    near, far = (swap(turn, starts, (q, 2), (p, 1)) for turn in range(2))
    for slot in range(ticks + 1):
        if slot == 1:
            p, q, near, far = following
        elif slot > 1:
            p = arrived(slot, 0)
            p, newer[1] = lax.optimization_barrier((p, newer[1]))
            q = arrived(slot, 1)
            near, far = (swap(turn, starts, (q, 2), (p, 1)) for turn in range(2))
        *kept, w_one = inner_half(p, q, w_one, width, slot == 0)
        first = first_half(flags, p, kept, (near, far), w_one, width)
        onward = [(j, j + 1) for j in range(1, sections - 1)] if slot > 0 else []
        if slot < ticks - 1:
            onward = [(0, 1)] + onward
        received, relays = {}, {}
        if slot < ticks:
            received[0] = send(first[1], onward)
        second = second_half(first, q, w_two, width, slot == ticks)
        if slot < ticks:
            received[1] = send(second, onward)
        if slot == 0:
            mirrored, _ = lax.optimization_barrier((mirrored, second))
            following = arrived(1, 0), arrived(1, 1)
            following += tuple(swap(turn, starts, (following[1], 2), (following[0], 1)) for turn in range(2))
        elif slot < ticks:
            relay_q, second = lax.optimization_barrier((newer[1], second))
            relays = {0: send(newer[0], [(1, sections - 1)]), 1: send(relay_q, [(1, sections - 1)])}
            if across:
                direct = {0: send(first[1], across), 1: send(second, across)}
        older, newer, relayed = newer, received, relays
    result = second
    return result.reshape(1, 2, planes, rows, width, chans)


def solution(mesh):
    in_specs = (
        P("section", None, "depth", None, None, None),
        P("section", None, "depth", None, None, None),
        P(None, None, "depth", None, None, None),
        P("section", None, None, None, None, None),
        P("section", None, None, None, None, None),
    )
    out_specs = P("section", None, "depth", None, None, None)
    return jax.shard_map(local, mesh=mesh, in_specs=in_specs, out_specs=out_specs, check_vma=False)
```

```python
import functools

import jax
import jax.numpy as jnp
from jax import lax
from jax.experimental import pallas as pl
from jax.experimental.pallas import tpu as pltpu
from jax.sharding import PartitionSpec as P

EPS = 1e-05
VMEM_LIMIT = 12 * 1024 * 1024


def act(values):
    values = values.astype(jnp.float32)
    scaled = values * lax.rsqrt(jnp.mean(values * values, axis=-1, keepdims=True) + EPS)
    return scaled * (0.5 + 0.5 * jnp.tanh(0.5 * scaled))


def fill(even, odd, at, values, width):
    planes, _, chans = values.shape
    field = act(values)
    edge = jnp.zeros((planes, width, chans), jnp.float32)
    even[pl.ds(at, planes)] = field.astype(jnp.bfloat16)
    odd[pl.ds(at, planes)] = jnp.concatenate([edge, field, edge], axis=1).astype(jnp.bfloat16)


def shifted(part, k, width):
    planes, voxels, chans = part.shape
    part = part.reshape(-1, width, chans)
    column = lax.broadcasted_iota(jnp.int32, part.shape, 1)
    if k == 0:
        part = jnp.where(column == 0, 0.0, pltpu.roll(part, 1, 1))
    elif k == 2:
        part = jnp.where(column == width - 1, 0.0, pltpu.roll(part, width - 1, 1))
    return part.reshape(planes, voxels, chans)


def product(taps, weights, offsets, k):
    planes, voxels, chans = taps[0].shape
    slab = jnp.concatenate([part.reshape(planes * voxels, chans) for part in taps], axis=-1)
    columns = jnp.concatenate([weights[(3 * n + k) * chans : (3 * n + k + 1) * chans] for n in offsets], axis=0)
    part = jnp.dot(slab, columns, preferred_element_type=jnp.float32)
    return part.reshape(planes, voxels, chans)


def convolve(taps, weights, width):
    return sum(shifted(product(taps, weights, range(9), k), k, width) for k in (1, 0, 2))


def edges(sources, targets, weights, width):
    total = None
    for k in (1, 0, 2):
        sums = [None] * 4
        for i in range(3):
            part = product(sources[i], weights, range(3 * i, 3 * i + 3), k)
            for plane, target in enumerate(targets[i]):
                piece = part[plane : plane + 1]
                sums[target] = piece if sums[target] is None else sums[target] + piece
        part = shifted(jnp.concatenate(sums, axis=0), k, width)
        total = part if total is None else total + part
    return total


def planes_at(even, odd, start, count, width):
    voxels = even.shape[1]
    return [
        even[start : start + count] if j == 1 else odd[start : start + count, j * width : j * width + voxels]
        for j in range(3)
    ]


def own_planes(width, p, q, weights, inner, partial, even, odd, ready=None):
    planes = q.shape[0]
    fill(even, odd, 0, q[...], width)
    if ready is not None:
        ready.wait()
    taps = [part for i in range(3) for part in planes_at(even, odd, i, planes - 2, width)]
    inner[...] = (p[1:-1].astype(jnp.float32) + convolve(taps, weights, width)).astype(inner.dtype)
    own = lambda plane: planes_at(even, odd, plane, 1, width)
    pair = lambda one, other: [jnp.concatenate(both, axis=0) for both in zip(own(one), own(other))]
    sources = (pair(planes - 2, planes - 1), pair(0, planes - 1), pair(0, 1))
    partial[...] = edges(sources, ((2, 3), (1, 2), (0, 1)), weights, width)


def inner_kernel(width, p, q, weights, inner, partial, even, odd):
    own_planes(width, p, q, weights, inner, partial, even, odd)


def loading_kernel(width, p, q, weights_hbm, inner, partial, weights, even, odd, sem):
    copy = pltpu.make_async_copy(weights_hbm, weights, sem)
    copy.start()
    own_planes(width, p, q, weights, inner, partial, even, odd, copy)


def edge_kernel(width, flags, p, inner, partial, near, far, weights, low, mid, high, even, odd):
    planes = p.shape[0]
    above = flags[2] > 0
    near, far = near[...].astype(jnp.float32), far[...].astype(jnp.float32)
    below, beyond = jnp.where(above, far, near), jnp.where(above, near, far)
    fill(even, odd, 0, below[:2], width)
    fill(even, odd, 2, beyond[:2], width)
    sources = [planes_at(even, odd, start, 2, width) for start in range(3)]
    total = partial[...] + edges(sources, ((0, 1), (0, 3), (2, 3)), weights, width)
    low[...] = jnp.where(flags[0] > 0, below[2:] + total[:1], 0.0).astype(low.dtype)
    mid[pl.ds(0, 1)] = (p[:1].astype(jnp.float32) + total[1:2]).astype(mid.dtype)
    mid[pl.ds(1, planes - 2)] = inner[...]
    mid[pl.ds(planes - 1, 1)] = (p[-1:].astype(jnp.float32) + total[2:3]).astype(mid.dtype)
    high[...] = jnp.where(flags[1] > 0, beyond[2:] + total[3:], 0.0).astype(high.dtype)


def second_sum(width, first_low, first_mid, first_high, q, weights, even, odd):
    planes = q.shape[0]
    fill(even, odd, 0, first_low[...], width)
    fill(even, odd, 1, first_mid[...], width)
    fill(even, odd, 1 + planes, first_high[...], width)
    taps = [part for i in range(3) for part in planes_at(even, odd, i, planes, width)]
    return q[...].astype(jnp.float32) + convolve(taps, weights, width)


def second_kernel(width, first_low, first_mid, first_high, q, weights, out, even, odd):
    out[...] = second_sum(width, first_low, first_mid, first_high, q, weights, even, odd).astype(out.dtype)


def last_kernel(width, first_low, first_mid, first_high, q, weights, out, even, odd, second, first_sem, low_sem, high_sem):
    first_copy = pltpu.make_async_copy(first_mid, out.at[0], first_sem)
    first_copy.start()
    planes = q.shape[0]
    fill(even, odd, 0, first_low[...], width)
    fill(even, odd, 1, first_mid[...], width)
    fill(even, odd, 1 + planes, first_high[...], width)
    half = planes // 2
    copies = [first_copy]
    for start, count, sem in ((0, half, low_sem), (half, planes - half, high_sem)):
        taps = [part for i in range(3) for part in planes_at(even, odd, start + i, count, width)]
        part = pl.ds(start, count)
        second[part] = (q[part].astype(jnp.float32) + convolve(taps, weights, width)).astype(second.dtype)
        copy = pltpu.make_async_copy(second.at[part], out.at[1, part], sem)
        copy.start()
        copies.append(copy)
    for copy in copies:
        copy.wait()


def call(kernel, outputs, scratch, arguments, width):
    specs = [pl.BlockSpec(memory_space=pltpu.VMEM) for _ in arguments]
    if kernel is edge_kernel:
        specs[0] = pl.BlockSpec(memory_space=pltpu.SMEM)
    if kernel is loading_kernel:
        specs[-1] = pl.BlockSpec(memory_space=pltpu.HBM)
    return pl.pallas_call(
        functools.partial(kernel, width),
        out_shape=[jax.ShapeDtypeStruct(shape, dtype) for shape, dtype in outputs],
        in_specs=specs,
        out_specs=[pl.BlockSpec(memory_space=pltpu.HBM if kernel is last_kernel else pltpu.VMEM) for _ in outputs],
        scratch_shapes=[pltpu.VMEM(shape, jnp.bfloat16) if shape else pltpu.SemaphoreType.DMA for shape in scratch],
        compiler_params=pltpu.CompilerParams(vmem_limit_bytes=VMEM_LIMIT),
        cost_estimate=pl.CostEstimate(flops=1, bytes_accessed=1, transcendentals=0),
    )(*arguments)


def stored(planes, voxels, chans, width):
    return (planes, voxels, chans), (planes, voxels + 2 * width, chans)


def inner_half(p, q, weights, width, load):
    planes, voxels, chans = q.shape
    outputs = [((planes - 2, voxels, chans), jnp.bfloat16), ((4, voxels, chans), jnp.float32)]
    scratch = stored(planes, voxels, chans, width)
    if load:
        weights = pltpu.with_memory_space_constraint(weights, pltpu.HBM)
        outputs.append((weights.shape, jnp.bfloat16))
        return call(loading_kernel, outputs, [*scratch, ()], (p, q, weights), width)
    return *call(inner_kernel, outputs, scratch, (p, q, weights), width), weights


def first_half(flags, p, kept, halos, weights, width):
    planes, voxels, chans = p.shape
    return call(
        edge_kernel,
        [((n, voxels, chans), jnp.bfloat16) for n in (1, planes, 1)],
        stored(4, voxels, chans, width),
        (flags, p, *kept, *halos, weights),
        width,
    )


def second_half(first, q, weights, width, last):
    shape = q.shape
    scratch = stored(shape[0] + 2, *shape[1:], width)
    output = shape
    if last:
        scratch, output = [*scratch, shape, (), (), ()], (2, *shape)
    (out,) = call(last_kernel if last else second_kernel, [(output, jnp.bfloat16)], scratch, (*first, q, weights), width)
    return out


def swap(turn, starts, *blocks):
    count = lax.axis_size("depth")
    parts = [lax.dynamic_slice_in_dim(block, starts[n][turn], n, axis=0) for block, n in blocks]
    pairs = [pair for i in range(turn, count - 1, 2) for pair in ((i, i + 1), (i + 1, i))]
    return lax.ppermute(jnp.concatenate(parts, axis=0), "depth", pairs)


def local(resident, previous, incoming, first_weights, second_weights):
    section = lax.axis_index("section")
    sections = lax.axis_size("section")
    half = sections // 2
    depth = lax.axis_index("depth")
    ticks = incoming.shape[0] + 1
    _, _, planes, rows, width, chans = resident.shape
    voxels = rows * width
    across = [(j, sections - 1 - j) for j in range(1, half - 1)]

    above = depth % 2 == 0
    places = {
        "flags": jnp.stack([depth > 0, depth < lax.axis_size("depth") - 1, above]).astype(jnp.int32),
        "starts": {
            n: (jnp.where(above, planes - n, 0), jnp.where(above, 0, planes - n)) for n in (1, 2)
        },
        "first": section == 0,
        "second": section == 1,
        "last": section == sections - 1,
        "decoder": section >= half,
        "direct": (section > half) & (section < sections - 1) if across else (),
    }
    places, resident, previous, incoming, first_weights, second_weights = lax.optimization_barrier(
        (places, resident, previous, incoming, first_weights, second_weights)
    )
    flags, starts = places["flags"], places["starts"]

    flat = lambda a: a.reshape(a.shape[0], 2, planes, voxels, chans)
    resident, previous, incoming = flat(resident)[0], flat(previous)[0], flat(incoming)
    w_one = first_weights.reshape(27 * chans, chans)
    w_two = second_weights.reshape(27 * chans, chans)

    def send(block, pairs):
        return lax.ppermute(block, "section", pairs) if pairs else block

    def join(held, skip):
        total = (held.astype(jnp.float32) + skip.astype(jnp.float32)).astype(jnp.bfloat16)
        return jnp.where(places["decoder"], total, held)

    newer, older, relayed, direct = {}, {}, {}, {}

    def arrived(slot, stream):
        fresh = incoming[min(slot, ticks - 1) - 1, stream]
        if slot == 1:
            return jnp.where(places["first"], fresh, join(resident[stream], mirrored[stream]))
        held = jnp.where(places["second"], older[stream], newer[stream])
        skip = jnp.where(places["last"], relayed[stream], newer[stream])
        if across:
            skip = jnp.where(places["direct"], direct[stream], skip)
        return jnp.where(places["first"], fresh, join(held, skip))

    p, q = resident
    near, far = (swap(turn, starts, (q, 2), (p, 1)) for turn in range(2))
    near, previous = lax.optimization_barrier((near, previous))
    mirrored = send(previous, [(j, sections - 1 - j) for j in range(half)])
    for slot in range(ticks + 1):
        if slot == 1:
            p, q, near, far = following
        elif slot > 1:
            p = arrived(slot, 0)
            p, newer[1] = lax.optimization_barrier((p, newer[1]))
            q = arrived(slot, 1)
            near, far = (swap(turn, starts, (q, 2), (p, 1)) for turn in range(2))
        *kept, w_one = inner_half(p, q, w_one, width, slot == 0)
        first = first_half(flags, p, kept, (near, far), w_one, width)
        onward = [(j, j + 1) for j in range(1, sections - 1)] if slot > 0 else []
        if slot < ticks - 1:
            onward = [(0, 1)] + onward
        received, relays = {}, {}
        if slot < ticks:
            received[0] = send(first[1], onward)
        second = second_half(first, q, w_two, width, slot == ticks)
        if slot < ticks:
            received[1] = send(second, onward)
        if slot == 0:
            mirrored, _ = lax.optimization_barrier((mirrored, second))
            following = arrived(1, 0), arrived(1, 1)
            following += tuple(swap(turn, starts, (following[1], 2), (following[0], 1)) for turn in range(2))
        elif slot < ticks:
            relay_q, second = lax.optimization_barrier((newer[1], second))
            relays = {0: send(newer[0], [(1, sections - 1)]), 1: send(relay_q, [(1, sections - 1)])}
            if across:
                direct = {0: send(first[1], across), 1: send(second, across)}
        older, newer, relayed = newer, received, relays
    result = second
    return result.reshape(1, 2, planes, rows, width, chans)


def solution(mesh):
    in_specs = (
        P("section", None, "depth", None, None, None),
        P("section", None, "depth", None, None, None),
        P(None, None, "depth", None, None, None),
        P("section", None, None, None, None, None),
        P("section", None, None, None, None, None),
    )
    out_specs = P("section", None, "depth", None, None, None)
    return jax.shard_map(local, mesh=mesh, in_specs=in_specs, out_specs=out_specs, check_vma=False)
```
